32 devices in a mesh: rows: 8 (over z, y), ch: 4 (over x, core).
Axes of the slice: x: 2, y: 2, z: 4, core: 2. Of those that a mesh axis runs over, the one named last changes fastest.
Arguments:
- pixels: bfloat16 [2, 16, 128, 768], P(None, 'rows', None, 'ch'), may hold values from -6 to 6
- row_starts: int32 [2, 16], replicated, may hold values from 0 to 1, as said below
- col_starts: int32 [2, 128], replicated, may hold values from 0 to 1
- log_step: float32 [2, 2, 768], P(None, None, 'ch'), may hold values from -6.9 to -2.3
- log_decay: float32 [2, 2, 768, 64], P(None, None, 'ch'), may hold values from -1 to 1
- frequency: float32 [2, 2, 768, 64], P(None, None, 'ch'), may hold values from 0 to 100
- coef_real: float32 [2, 2, 768, 64], P(None, None, 'ch'), may hold values from -12 to 12
- coef_imag: float32 [2, 2, 768, 64], P(None, None, 'ch'), may hold values from -12 to 12
- skip_gain: float32 [2, 768], P(None, 'ch'), may hold values from -4 to 4
- norm_gain: float32 [2, 768], P(None, 'ch'), may hold values from 0.5 to 1.5
- norm_shift: float32 [2, 768], P(None, 'ch'), may hold values from -3 to 3
- weight_in: bfloat16 [2, 768, 3072], P(None, None, 'ch'), may hold values from -0.21875 to 0.21875
- bias_in: float32 [2, 3072], P(None, 'ch'), may hold values from -3 to 3
- weight_out: bfloat16 [2, 3072, 768], P(None, 'ch'), may hold values from -0.109375 to 0.109375
- bias_out: float32 [2, 768], P(None, 'ch'), may hold values from -3 to 3
- layer_scale: float32 [2, 768], P(None, 'ch'), may hold values from 0.5 to 1.5
- cotangent: bfloat16 [2, 16, 128, 768], P(None, 'rows', None, 'ch'), may hold values from -6 to 6
Outputs:
- activations: bfloat16 [2, 16, 128, 768], P(None, 'rows', None, 'ch')
- pixels_grad: bfloat16 [2, 16, 128, 768], P(None, 'rows', None, 'ch')
- log_step_grad: float32 [2, 2, 768], P(None, None, 'ch')
- log_decay_grad: float32 [2, 2, 768, 64], P(None, None, 'ch')
- frequency_grad: float32 [2, 2, 768, 64], P(None, None, 'ch')
- coef_real_grad: float32 [2, 2, 768, 64], P(None, None, 'ch')
- coef_imag_grad: float32 [2, 2, 768, 64], P(None, None, 'ch')
- skip_gain_grad: float32 [2, 768], P(None, 'ch')
- norm_gain_grad: float32 [2, 768], P(None, 'ch')
- norm_shift_grad: float32 [2, 768], P(None, 'ch')
- weight_in_grad: float32 [2, 768, 3072], P(None, None, 'ch')
- bias_in_grad: float32 [2, 3072], P(None, 'ch')
- weight_out_grad: float32 [2, 3072, 768], P(None, 'ch')
- bias_out_grad: float32 [2, 768], P(None, 'ch')
- layer_scale_grad: float32 [2, 768], P(None, 'ch')
The draws below stay inside these ranges and needn't reach their ends.
Inputs may be any that keep to these rules, and one draw needn't show every extreme that they name: `row_starts`: entry 0 of every canvas is 1; in one canvas, drawn from the seed, no other entry is 1; every other canvas has at least one more 1.
All inputs are finite; a program needn't handle non-finite values.
Results may differ from the reference program's by a relative error of at most 0.02.
Values may be sent and summed in bfloat16 or wider, within the bound.
No kernel may reach another device: no remote copies, remote signals or barrier semaphores. Data moves between devices by JAX's collectives and lax.ppermute only.
A program may use at most 256 MiB of HBM per device.

```python
import jax
import jax.numpy as jnp
from jax import lax

C = 768
FF = 3072
NSTATE = 64
CANVASES = 2
W = 128
H = 16


def draw_row_starts(key, part):
    key = jax.random.fold_in(key, 11)
    first_key, second_key, third_key = jax.random.split(key, 3)
    places = jnp.arange(H)[None, :]
    ticks = jax.random.randint(first_key, (CANVASES, H), 0, 8)
    forced = jax.random.randint(third_key, (CANVASES, 1), 1, H)
    chosen = jax.random.randint(second_key, (), 0, CANVASES)
    canvas_ids = jnp.arange(CANVASES)[:, None]
    extra = jnp.logical_or(ticks == 0, places == forced).astype(jnp.int32)
    inner = jnp.where(canvas_ids == chosen, 0, extra)
    return jnp.where(places == 0, 1, inner).astype(jnp.int32)


def draw_col_starts(key, part):
    key = jax.random.fold_in(key, 12)
    places = jnp.arange(W)[None, :]
    ticks = jax.random.randint(key, (CANVASES, W), 0, 32)
    return jnp.where(places == 0, 1, (ticks == 0).astype(jnp.int32)).astype(jnp.int32)


def levels(own_key, shape, pieces, low, largest):
    gain, own = 1.0, jax.random.fold_in(own_key, 6)
    for dim, parts in pieces:
        draws = jnp.exp(jax.random.uniform(jax.random.fold_in(own, dim), (parts,), jnp.float32, low / len(pieces), largest / len(pieces)))
        gain = gain * jnp.repeat(draws, shape[dim] // parts).reshape([-1 if axis == dim else 1 for axis in range(len(shape))])
    return gain


def noise(own_key, dims, deviation, most, pieces=(), kind=jnp.bfloat16):
    entries = deviation * jax.random.normal(own_key, dims, jnp.float32)
    if pieces:
        entries = entries * levels(own_key, dims, pieces, -0.22, 0.18)
    return jnp.clip(entries, -most, most).astype(kind)


def setup_inputs(seed: int = 0) -> dict:
    streams_of = jax.random.split(jax.random.key(seed), 18)
    return {
        "pixels": noise(streams_of[0], (CANVASES, H, W, C), 1.0, 6.0, ((1, 8), (3, 4))),
        "row_starts": draw_row_starts(jax.random.fold_in(streams_of[17], 71), 0),
        "col_starts": draw_col_starts(jax.random.fold_in(streams_of[17], 71), 0),
        "log_step": jnp.clip(-6.9 + 4.6000001430511475 * jax.random.uniform(streams_of[3], (2, 2, C), jnp.float32) ** levels(streams_of[3], (2, 2, C), ((2, 4),), -0.2, 0.2), -6.9, -2.3),
        "log_decay": jnp.clip(jax.random.uniform(streams_of[4], (2, 2, C, NSTATE), jnp.float32, -1.0, 1.0) * levels(streams_of[4], (2, 2, C, NSTATE), ((2, 4),), -0.4, 0.0), -1.0, 1.0),
        "frequency": jnp.clip(100.0 * jax.random.uniform(streams_of[5], (2, 2, C, NSTATE), jnp.float32) ** levels(streams_of[5], (2, 2, C, NSTATE), ((2, 4),), -0.2, 0.2), 0.0, 100.0),
        "coef_real": noise(streams_of[6], (2, 2, C, NSTATE), 2.0, 12.0, ((2, 4),), jnp.float32),
        "coef_imag": noise(streams_of[7], (2, 2, C, NSTATE), 2.0, 12.0, ((2, 4),), jnp.float32),
        "skip_gain": noise(streams_of[8], (2, C), 1.0, 4.0, ((1, 4),), jnp.float32),
        "norm_gain": jnp.clip(1.0 + 0.1 * jax.random.normal(streams_of[9], (2, C), jnp.float32), 0.5, 1.5),
        "norm_shift": noise(streams_of[10], (2, C), 0.5, 3.0, ((1, 4),), jnp.float32),
        "weight_in": noise(streams_of[11], (2, C, FF), C ** -0.5, 0.21875, ((2, 4),)),
        "bias_in": noise(streams_of[12], (2, FF), 0.5, 3.0, ((1, 4),), jnp.float32),
        "weight_out": noise(streams_of[13], (2, FF, C), FF ** -0.5, 0.109375, ((1, 4),)),
        "bias_out": noise(streams_of[14], (2, C), 0.5, 3.0, ((1, 4),), jnp.float32),
        "layer_scale": jnp.clip(0.5 + 1.0 * jax.random.uniform(streams_of[15], (2, C), jnp.float32) ** levels(streams_of[15], (2, C), ((1, 4),), -0.2, 0.2), 0.5, 1.5),
        "cotangent": noise(streams_of[16], (CANVASES, H, W, C), 1.0, 6.0, ((1, 8), (3, 4))),
    }


epsilon = 1e-06
highest = lax.Precision.HIGHEST

@jax.custom_vjp
def low(v):
    return lax.optimization_barrier(v.astype(jnp.bfloat16)).astype(jnp.float32)

@jax.custom_vjp
def low_back(v):
    return v

def low_keep(v):
    return (low(v), None)

def low_pass(kept, grad):
    return (grad,)

def back_keep(v):
    return (v, None)

def back_low(kept, grad):
    return (low(grad),)
low.defvjp(low_keep, low_pass)
low_back.defvjp(back_keep, back_low)

def s4_kernel(log_step, log_decay, frequency, coef_real, coef_imag, length):
    step_size = jnp.exp(log_step)[:, None, None]
    places = jnp.arange(length).astype(jnp.float32)[None, None, :]
    fading = jnp.exp(-step_size * jnp.exp(log_decay)[:, :, None] * places)
    turning = step_size * frequency[:, :, None] * places
    waving = coef_real[:, :, None] * jnp.cos(turning) - coef_imag[:, :, None] * jnp.sin(turning)
    return step_size[:, :, 0] * lax.optimization_barrier(jnp.sum(fading * waving, axis=1))

def toeplitz(kernel):
    channels, length = kernel.shape
    widened = jnp.concatenate([kernel[:, :1], jnp.zeros((channels, length), kernel.dtype), kernel[:, 1:][:, ::-1]], axis=1)
    repeated = jnp.tile(widened, (1, length))[:, :length * (2 * length - 1)]
    return repeated.reshape(channels, length, 2 * length - 1)[:, :, :length]

def crop_mask(starts):
    labels = jnp.cumsum(starts, axis=1)
    return (labels[:, :, None] == labels[:, None, :]).astype(jnp.float32)

def along_width(inputs, kernel, crop_masks):
    matrix = toeplitz(kernel)

    def canvas_conv(element):
        picture, mask_one = element
        return jnp.einsum('cij,rjc->ric', matrix * mask_one[None], picture, precision=highest)
    return lax.map(jax.checkpoint(canvas_conv), (inputs, crop_masks))

def along_height(inputs, kernel, crop_masks):
    matrix = toeplitz(kernel)

    def canvas_conv(element):
        picture, mask_one = element
        return jnp.einsum('cij,jwc->iwc', matrix * mask_one[None], picture, precision=highest)
    return lax.map(jax.checkpoint(canvas_conv), (inputs, crop_masks))

def block(stream, params, row_masks, col_masks):
    log_step, log_decay, frequency, coef_real, coef_imag, skip_gain, norm_gain, norm_shift, weight_in, bias_in, weight_out, bias_out, layer_scale = params
    canvas_height, canvas_width, channels = (stream.shape[1], stream.shape[2], stream.shape[3])
    tall_kernel = low(s4_kernel(log_step[0], log_decay[0], frequency[0], coef_real[0], coef_imag[0], canvas_height))
    wide_kernel = low(s4_kernel(log_step[1], log_decay[1], frequency[1], coef_real[1], coef_imag[1], canvas_width))
    across = low(low_back(along_width(low(stream), wide_kernel, col_masks)))
    mixer_out = low(low_back(along_height(across, tall_kernel, row_masks)))
    mixed_rows = mixer_out + skip_gain * stream
    average = lax.optimization_barrier(jnp.mean(mixed_rows, axis=-1, keepdims=True))
    centred = mixed_rows - average
    spread = lax.optimization_barrier(jnp.mean(centred * centred, axis=-1, keepdims=True))
    normed = low(centred * lax.rsqrt(spread + epsilon) * norm_gain + norm_shift)
    rows_flat = normed.reshape(-1, channels)
    before = low_back(jnp.dot(rows_flat, weight_in, precision=highest) + bias_in)
    hidden = low(jax.nn.gelu(before))
    branch = low_back(jnp.dot(hidden, weight_out, precision=highest)) + bias_out
    return stream + layer_scale * branch.reshape(stream.shape)

def reference(pixels, row_starts, col_starts, log_step, log_decay, frequency, coef_real, coef_imag, skip_gain, norm_gain, norm_shift, weight_in, bias_in, weight_out, bias_out, layer_scale, cotangent):
    row_masks = crop_mask(row_starts)
    col_masks = crop_mask(col_starts)
    weights = (log_step, log_decay, frequency, coef_real, coef_imag, skip_gain, norm_gain, norm_shift, weight_in.astype(jnp.float32), bias_in, weight_out.astype(jnp.float32), bias_out, layer_scale)

    def forward(inputs, weight_set):
        stream = inputs
        for section_index in range(2):
            stream = block(stream, tuple((member[section_index] for member in weight_set)), row_masks, col_masks)
        return stream
    result, pullback = jax.vjp(forward, pixels.astype(jnp.float32), weights)
    input_grad, gradients = pullback(cotangent.astype(jnp.float32))
    return (result.astype(jnp.bfloat16), input_grad.astype(jnp.bfloat16), gradients[0], gradients[1], gradients[2], gradients[3], gradients[4], gradients[5], gradients[6], gradients[7], gradients[8], gradients[9], gradients[10], gradients[11], gradients[12])
```

```python
from functools import partial

import jax
import jax.numpy as jnp
from jax import lax
from jax.experimental import pallas as pl
from jax.experimental.pallas import tpu as pltpu
from jax.sharding import PartitionSpec as P


epsilon = 1e-06
bf16 = jnp.bfloat16
f32 = jnp.float32
vmem_bytes = 56 * 1024 * 1024
ahead = 8
band = 16
lane = 128


def dot(a, b, ca, cb):
    return lax.dot_general(a, b, (((ca,), (cb,)), ((), ())), preferred_element_type=f32)


def vmem_spec():
    return pl.BlockSpec(memory_space=pltpu.VMEM)


def smem_spec():
    return pl.BlockSpec(memory_space=pltpu.SMEM)


def struct(shape, dtype):
    return jax.ShapeDtypeStruct(shape, dtype)


def params(flops=0, moved=0):
    return dict(
        compiler_params=pltpu.CompilerParams(vmem_limit_bytes=vmem_bytes),
        cost_estimate=pl.CostEstimate(flops=flops, bytes_accessed=moved, transcendentals=0),
    )


def transposed(value):
    rows, cols = value.shape
    return jnp.transpose(value)


def state_powers(step, decay, frequency):
    size = jnp.exp(-step * decay)
    turn = step * frequency
    z = (size * jnp.cos(turn), size * jnp.sin(turn))

    def times(p, q):
        return (p[0] * q[0] - p[1] * q[1], p[0] * q[1] + p[1] * q[0])

    z2 = times(z, z)
    z3 = times(z2, z)
    z4 = times(z2, z2)
    return [None, z, z2, z3, z4, times(z4, z), times(z4, z2), times(z4, z3)], times(z4, z4), times


def s4_body(lengths, step_ref, decay_ref, freq_ref, real_ref, imag_ref, tall_ref, wide_ref,
            qr_ref, qi_ref, pr_ref, pi_ref, out_ref):
    channels = step_ref.shape[2]
    for direction, length in enumerate(lengths):
        step = jnp.exp(step_ref[0, direction:direction + 1, :])
        decay = jnp.exp(decay_ref[0, direction])
        powers, z8, times = state_powers(step, decay, freq_ref[0, direction])
        powers[0] = (jnp.ones_like(decay), jnp.zeros_like(decay))
        for a in range(ahead):
            qr_ref[a] = powers[a][0]
            qi_ref[a] = powers[a][1]
        pr_ref[0] = real_ref[0, direction]
        pi_ref[0] = imag_ref[0, direction]
        turns = length // ahead
        qr_ref[ahead] = z8[0]
        qi_ref[ahead] = z8[1]

        def block(b, carry):
            pr, pi = pr_ref[0], pi_ref[0]
            rows = []
            for a in range(ahead):
                rows.append(jnp.sum(pr * qr_ref[a] - pi * qi_ref[a], axis=0, keepdims=True))
            out_ref[pl.ds(pl.multiple_of(b * ahead, ahead), ahead), 0:channels] = (
                step * jnp.concatenate(rows, axis=0)
            ).astype(bf16).astype(f32)
            zr, zi = qr_ref[ahead], qi_ref[ahead]
            pr_ref[0] = pr * zr - pi * zi
            pi_ref[0] = pr * zi + pi * zr
            return carry

        lax.fori_loop(0, turns, block, 0)
        flipped = jnp.transpose(out_ref[...])[0:channels, :]
        if direction == 0:
            tall_ref[...] = flipped
        else:
            copies = wide_ref.shape[1] // channels
            wide_ref[...] = jnp.transpose(jnp.concatenate([flipped] * copies, axis=0))


def s4_kernels(section, lengths, log_step, log_decay, frequency, coef_real, coef_imag, copies):
    states, channels = log_decay.shape[2], log_decay.shape[3]
    whole = pl.BlockSpec((1, 2, states, channels), lambda i: (section, 0, 0, 0))
    wide_lanes = -(-channels // lane) * lane
    return pl.pallas_call(
        partial(s4_body, lengths),
        grid=(1,),
        in_specs=[pl.BlockSpec((1, 2, channels), lambda i: (section, 0, 0)), whole, whole, whole, whole],
        out_specs=[
            pl.BlockSpec((channels, lane), lambda i: (0, 0)),
            pl.BlockSpec((lane, copies * channels), lambda i: (0, 0)),
        ],
        out_shape=[struct((channels, lane), f32), struct((lane, copies * channels), f32)],
        scratch_shapes=[
            pltpu.VMEM((ahead + 1, states, channels), f32),
            pltpu.VMEM((ahead + 1, states, channels), f32),
            pltpu.VMEM((1, states, channels), f32),
            pltpu.VMEM((1, states, channels), f32),
            pltpu.VMEM((lane, wide_lanes), f32),
        ],
        name="s4_kernels",
        **params(10_000_000, 1_000_000),
    )(log_step, log_decay, frequency, coef_real, coef_imag)


def pull_body(lengths, tall_ref, wide_ref, step_ref, decay_ref, freq_ref, real_ref, imag_ref,
              dstep_ref, ddecay_ref, dfreq_ref, dreal_ref, dimag_ref, turn_ref, grad_ref, q_ref, s_ref):
    channels = step_ref.shape[2]
    states = decay_ref.shape[2]
    for direction, length in enumerate(lengths):
        step = jnp.exp(step_ref[0, direction:direction + 1, :])
        decay = jnp.exp(decay_ref[0, direction])
        freq = freq_ref[0, direction]
        powers, z8, times = state_powers(step, decay, freq)
        for a in range(1, ahead):
            q_ref[2 * a] = powers[a][0]
            q_ref[2 * a + 1] = powers[a][1]
        q_ref[0] = z8[0]
        q_ref[1] = z8[1]
        turn_ref[0:channels, :] = (tall_ref if direction == 0 else wide_ref)[0]
        flat = jnp.transpose(turn_ref[...])
        for place in range(length):
            grad_ref[place] = jnp.broadcast_to(flat[place:place + 1, 0:channels], (8, channels))
        turns = length // ahead

        def group(n, carry):
            off = pl.multiple_of(n * 8, 8)
            part = pl.ds(off, 8)
            q = [(q_ref[2 * a, part, :], q_ref[2 * a + 1, part, :]) for a in range(ahead)]
            zr, zi = q[0]

            def block(index, sums):
                s0r, s0i, s1r, s1i = sums
                b = turns - 1 - index
                g = grad_ref[b * ahead]
                t0r, t0i = g, jnp.zeros_like(g)
                t1r, t1i = jnp.zeros_like(g), jnp.zeros_like(g)
                for a in range(1, ahead):
                    g = grad_ref[b * ahead + a]
                    x, y = g * q[a][0], g * q[a][1]
                    t0r, t0i = t0r + x, t0i + y
                    t1r, t1i = t1r + a * x, t1i + a * y
                base = (b * ahead).astype(f32)
                v1r, v1i = t1r + base * t0r, t1i + base * t0i
                return (
                    s0r * zr - s0i * zi + t0r,
                    s0r * zi + s0i * zr + t0i,
                    s1r * zr - s1i * zi + v1r,
                    s1r * zi + s1i * zr + v1i,
                )

            zero = jnp.zeros((8, channels), f32)
            sums = lax.fori_loop(0, turns, block, (zero, zero, zero, zero))
            for k in range(4):
                s_ref[k, part, :] = sums[k]
            return carry

        lax.fori_loop(0, states // 8, group, 0)
        real, imag = real_ref[0, direction], imag_ref[0, direction]
        s0r, s0i, s1r, s1i = s_ref[0], s_ref[1], s_ref[2], s_ref[3]
        dreal = step * s0r
        dimag = -step * s0i
        ddecay = -step * step * decay * (real * s1r - imag * s1i)
        dfreq = -step * step * (real * s1i + imag * s1r)
        dreal_ref[0, direction] = dreal
        dimag_ref[0, direction] = dimag
        ddecay_ref[0, direction] = ddecay
        dfreq_ref[0, direction] = dfreq
        dstep_ref[0, direction:direction + 1, :] = jnp.sum(
            real * dreal + imag * dimag + ddecay + freq * dfreq, axis=0, keepdims=True
        )


def s4_pullback(lengths, tall_grads, wide_grads, log_step, log_decay, frequency, coef_real, coef_imag):
    states, channels = log_decay.shape[2], log_decay.shape[3]
    whole = pl.BlockSpec((1, 2, states, channels), lambda i: (i, 0, 0, 0))
    row = pl.BlockSpec((1, 2, channels), lambda i: (i, 0, 0))
    grad = pl.BlockSpec((1, channels, lane), lambda i: (i, 0, 0))
    wide_lanes = -(-channels // lane) * lane
    return pl.pallas_call(
        partial(pull_body, lengths),
        grid=(2,),
        in_specs=[grad, grad, row, whole, whole, whole, whole],
        out_specs=[row, whole, whole, whole, whole],
        out_shape=[struct(log_step.shape, f32)] + [struct(log_decay.shape, f32)] * 4,
        scratch_shapes=[
            pltpu.VMEM((wide_lanes, lane), f32),
            pltpu.VMEM((lane, 8, channels), f32),
            pltpu.VMEM((2 * ahead, states, channels), f32),
            pltpu.VMEM((4, states, channels), f32),
        ],
        name="s4_pullback",
        **params(100_000_000, 2_000_000),
    )(tall_grads, wide_grads, log_step, log_decay, frequency, coef_real, coef_imag)


def spread_kernel(wide_ref, spread_ref):
    for place in range(wide_ref.shape[0]):
        spread_ref[place] = jnp.broadcast_to(wide_ref[place:place + 1, :], (8, wide_ref.shape[1]))


def shift_copies(value, shifted_ref, sign):
    for s in range(ahead):
        shifted_ref[s] = value if s == 0 else pltpu.roll(value, (sign * s) % value.shape[0], 0)


def width_conv(canvas, sign, shifted_ref, spread_ref, age_ref, reach_ref, out_ref):
    width = out_ref.shape[0]
    groups = width // 8
    tiles = out_ref.shape[1] // lane
    per = band // 8
    for index in range(width // band):
        ages = [age_ref[canvas, pl.ds((index * per + k) * 8, 8), :] for k in range(per)]

        def body(q, sums):
            sums = list(sums)
            places = [
                pl.multiple_of(jnp.clip(index * per + k - sign * q, 0, groups - 1) * 8, 8) for k in range(per)
            ]
            for s in range(ahead):
                lag = q * ahead + s
                for k in range(per):
                    seen = ages[k] >= lag
                    for t in range(tiles):
                        cut = slice(t * lane, (t + 1) * lane)
                        x = shifted_ref[s, pl.ds(places[k], 8), cut]
                        sums[k * tiles + t] += spread_ref[lag, :, cut] * jnp.where(seen, x, 0.0)
            return tuple(sums)

        zero = jnp.zeros((8, lane), f32)
        sums = lax.fori_loop(0, reach_ref[canvas, index], body, (zero,) * (per * tiles))
        for k in range(per):
            for t in range(tiles):
                out_ref[pl.ds((index * per + k) * 8, 8), t * lane:(t + 1) * lane] = sums[k * tiles + t]


def width_products(canvas, shifted_ref, grad_ref, age_ref, reach_ref, total_ref):
    width = grad_ref.shape[0]
    groups = width // 8
    tiles = grad_ref.shape[1] // lane
    per = band // 8
    for index in range(width // band):
        ages = [age_ref[canvas, pl.ds((index * per + k) * 8, 8), :] for k in range(per)]
        grads = [
            [grad_ref[pl.ds((index * per + k) * 8, 8), t * lane:(t + 1) * lane] for t in range(tiles)]
            for k in range(per)
        ]

        def body(q, carry):
            places = [
                pl.multiple_of(jnp.clip(index * per + k - q, 0, groups - 1) * 8, 8) for k in range(per)
            ]
            for s in range(ahead):
                lag = q * ahead + s
                seen = [ages[k] >= lag for k in range(per)]
                for t in range(tiles):
                    cut = slice(t * lane, (t + 1) * lane)
                    total = total_ref[lag, :, cut]
                    for k in range(per):
                        x = shifted_ref[s, pl.ds(places[k], 8), cut]
                        total += grads[k][t] * jnp.where(seen[k], x, 0.0)
                    total_ref[lag, :, cut] = total
            return carry

        lax.fori_loop(0, reach_ref[canvas, index], body, 0)


def stacked_rows(ref, canvas):
    picture = ref[canvas].astype(f32)
    return jnp.transpose(picture.reshape(-1, picture.shape[2]))


def unstacked(value, rows):
    flat = jnp.transpose(value)
    return flat.reshape(rows, flat.shape[0] // rows, flat.shape[1])


def width_scratch(rows, channels):
    lanes = rows * channels
    return [
        pltpu.VMEM((ahead, lane, lanes), f32),
        pltpu.VMEM((lane, 8, lanes), f32),
        pltpu.VMEM((lane, lanes), f32),
    ]


def wide_forward_body(picture_ref, wide_ref, age_ref, reach_ref, out_ref, shifted_ref, spread_ref, sum_ref):
    rows = picture_ref.shape[1]
    spread_kernel(wide_ref, spread_ref)
    for canvas in range(picture_ref.shape[0]):
        shift_copies(stacked_rows(picture_ref, canvas), shifted_ref, 1)
        width_conv(canvas, 1, shifted_ref, spread_ref, age_ref, reach_ref, sum_ref)
        out_ref[canvas] = unstacked(sum_ref[...], rows).astype(bf16)


def wide_forward(picture, wide, age, reach):
    return pl.pallas_call(
        wide_forward_body,
        in_specs=[vmem_spec(), vmem_spec(), vmem_spec(), smem_spec()],
        out_specs=vmem_spec(),
        out_shape=struct(picture.shape, bf16),
        scratch_shapes=width_scratch(picture.shape[1], picture.shape[2]),
        name="wide_forward",
        **params(30_000_000, 2_000_000),
    )(picture, wide, age, reach)


def wide_mixed_body(tall_ref, stream_ref, wide_ref, age_ref, reach_ref, pack_ref, out_ref,
                    shifted_ref, spread_ref, sum_ref):
    rows = tall_ref.shape[1]
    skip = pack_ref[:, 0:1]
    spread_kernel(wide_ref, spread_ref)
    for canvas in range(tall_ref.shape[0]):
        shift_copies(stacked_rows(tall_ref, canvas), shifted_ref, 1)
        width_conv(canvas, 1, shifted_ref, spread_ref, age_ref, reach_ref, sum_ref)
        mixer = unstacked(sum_ref[...], rows)
        for row in range(rows):
            at = (canvas * rows + row) * lane
            out_ref[:, at:at + lane] = (
                mixer[row] + skip * stream_ref[canvas, row].astype(f32)
            ).astype(bf16)


def wide_mixed(tall, stream, wide, age, reach, pack):
    pixels = tall.shape[0] * tall.shape[1] * lane
    return pl.pallas_call(
        wide_mixed_body,
        in_specs=[vmem_spec()] * 4 + [smem_spec(), vmem_spec()],
        out_specs=vmem_spec(),
        out_shape=struct((tall.shape[2], pixels), bf16),
        scratch_shapes=width_scratch(tall.shape[1], tall.shape[2]),
        name="wide_mixed",
        **params(30_000_000, 2_000_000),
    )(tall, stream, wide, age, reach, pack)


def norm_backward(grads, mixed_ref, stats_ref, pack_ref, channels_all):
    channels = mixed_ref.shape[0]
    keep, near, far = grads
    total = keep[...].astype(f32) + near[...].astype(f32) + far[...].astype(f32)
    normed_grad = total[0:channels]
    scaled_mean = total[channels:channels + 1] / channels_all
    paired_mean = total[channels + 1:channels + 2] / channels_all
    average, inverse = stats_ref[0:1, :], stats_ref[1:2, :]
    centred = (mixed_ref[...].astype(f32) - average) * inverse
    gain = pack_ref[:, 1:2]
    mixed_grad = inverse * (normed_grad * gain - scaled_mean - centred * paired_mean)
    return (
        mixed_grad,
        jnp.sum(normed_grad * centred, axis=1, keepdims=True),
        jnp.sum(normed_grad, axis=1, keepdims=True),
    )


def put_columns(ref, columns):
    places = lax.broadcasted_iota(jnp.int32, ref.shape, 1)
    value = jnp.zeros(ref.shape, f32)
    for index, column in enumerate(columns):
        value = jnp.where(places == index, column, value)
    ref[...] = value


def wide_norm_back_body(channels_all, keep_ref, near_ref, far_ref, mixed_ref, stats_ref, pack_ref, stream_ref,
                        cotangent_ref, wide_ref, fore_ref, reach_ref, conv_ref, rest_ref, grad_ref, sums_ref,
                        shifted_ref, spread_ref, sum_ref):
    canvases, rows = conv_ref.shape[0], conv_ref.shape[1]
    mixed_grad, gain_grad, shift_grad = norm_backward(
        (keep_ref, near_ref, far_ref), mixed_ref, stats_ref, pack_ref, channels_all
    )
    skip = pack_ref[:, 0:1]
    skip_grad = jnp.zeros_like(gain_grad)
    spread_kernel(wide_ref, spread_ref)
    for canvas in range(canvases):
        for row in range(rows):
            at = (canvas * rows + row) * lane
            part = mixed_grad[:, at:at + lane]
            grad_ref[canvas, row] = part.astype(bf16)
            skip_grad += jnp.sum(part * stream_ref[canvas, row].astype(f32), axis=1, keepdims=True)
            rest_ref[canvas, row] = (cotangent_ref[canvas, row].astype(f32) + skip * part).astype(bf16)
        shift_copies(stacked_rows(grad_ref, canvas), shifted_ref, -1)
        width_conv(canvas, -1, shifted_ref, spread_ref, fore_ref, reach_ref, sum_ref)
        conv_ref[canvas] = unstacked(sum_ref[...], rows).astype(bf16)
    put_columns(sums_ref, [skip_grad, gain_grad, shift_grad])


def wide_norm_back(channels_all, grads, mixed, stats, pack, stream, cotangent, wide, fore, reach):
    return pl.pallas_call(
        partial(wide_norm_back_body, channels_all),
        in_specs=[vmem_spec()] * 10 + [smem_spec()],
        out_specs=[vmem_spec()] * 4,
        out_shape=[struct(stream.shape, bf16)] * 3 + [struct((stream.shape[2], lane), f32)],
        scratch_shapes=width_scratch(stream.shape[1], stream.shape[2]),
        name="wide_norm_back",
        **params(30_000_000, 2_000_000),
    )(*grads, mixed, stats, pack, stream, cotangent, wide, fore, reach)


def wide_back_body(grad_ref, rest_ref, wide_ref, fore_ref, reach_ref, out_ref, shifted_ref, spread_ref, sum_ref):
    rows = grad_ref.shape[1]
    spread_kernel(wide_ref, spread_ref)
    for canvas in range(grad_ref.shape[0]):
        shift_copies(stacked_rows(grad_ref, canvas), shifted_ref, -1)
        width_conv(canvas, -1, shifted_ref, spread_ref, fore_ref, reach_ref, sum_ref)
        out_ref[canvas] = (unstacked(sum_ref[...], rows) + rest_ref[canvas].astype(f32)).astype(bf16)


def wide_back(grad, rest, wide, fore, reach):
    return pl.pallas_call(
        wide_back_body,
        in_specs=[vmem_spec()] * 4 + [smem_spec()],
        out_specs=vmem_spec(),
        out_shape=struct(grad.shape, bf16),
        scratch_shapes=width_scratch(grad.shape[1], grad.shape[2]),
        name="wide_back",
        **params(30_000_000, 2_000_000),
    )(grad, rest, wide, fore, reach)


def wide_kernel_grad_body(grad_ref, input_ref, age_ref, reach_ref, out_ref, shifted_ref, total_ref, flat_ref, sum_ref):
    channels = grad_ref.shape[2]
    rows = grad_ref.shape[1]
    total_ref[...] = jnp.zeros(total_ref.shape, f32)
    for canvas in range(grad_ref.shape[0]):
        shift_copies(stacked_rows(input_ref, canvas), shifted_ref, 1)
        flat_ref[...] = stacked_rows(grad_ref, canvas)
        width_products(canvas, shifted_ref, flat_ref, age_ref, reach_ref, total_ref)

    def reduce(index, carry):
        at = pl.multiple_of(index * 8, 8)
        sum_ref[pl.ds(at, 8), :] = jnp.sum(total_ref[pl.ds(at, 8)], axis=1)
        return carry

    lax.fori_loop(0, total_ref.shape[0] // 8, reduce, 0)
    flat = jnp.transpose(sum_ref[...])
    out_ref[...] = sum(flat[row * channels:(row + 1) * channels] for row in range(rows))


def wide_kernel_grad(grad, inputs, age, reach):
    lanes = grad.shape[1] * grad.shape[2]
    return pl.pallas_call(
        wide_kernel_grad_body,
        in_specs=[vmem_spec()] * 3 + [smem_spec()],
        out_specs=vmem_spec(),
        out_shape=struct((grad.shape[2], lane), f32),
        scratch_shapes=width_scratch(grad.shape[1], grad.shape[2]) + [pltpu.VMEM((lane, lanes), f32)],
        name="wide_kernel_grad",
        **params(30_000_000, 2_000_000),
    )(grad, inputs, age, reach)


def height_loop(count, body, carry):
    if count <= 16:
        for lag in range(count):
            carry = body(lag, carry)
        return carry
    return lax.fori_loop(0, count, body, carry)


def tap(tall_ref, lag):
    if isinstance(lag, int):
        return tall_ref[:, lag:lag + 1]
    places = lax.broadcasted_iota(jnp.int32, tall_ref.shape, 1)
    return jnp.sum(jnp.where(places == lag, tall_ref[...], 0.0), axis=1, keepdims=True)


def height_conv(value, tall_ref, age, sign, height):
    columns = value.shape[1] // height

    def body(lag, total):
        moved = pltpu.roll(value, (sign * lag * columns) % value.shape[1], 1) if not isinstance(lag, int) or lag else value
        return total + tap(tall_ref, lag) * jnp.where(age >= lag, moved, 0.0)

    return height_loop(height, body, jnp.zeros_like(value))


def height_products(grad, value, age, height, start):
    columns = value.shape[1] // height
    places = lax.broadcasted_iota(jnp.int32, start.shape, 1)

    def body(lag, total):
        moved = pltpu.roll(value, (lag * columns) % value.shape[1], 1) if not isinstance(lag, int) or lag else value
        summed = jnp.sum(grad * jnp.where(age >= lag, moved, 0.0), axis=1, keepdims=True)
        return total + jnp.where(places == lag, summed, 0.0)

    return height_loop(height, body, start)


def canvas_cut(ref, canvas, canvases):
    each = ref.shape[1] // canvases
    return slice(canvas * each, (canvas + 1) * each)


def tall_mixed_body(height, across_ref, stream_ref, tall_ref, age_ref, pack_ref, out_ref):
    canvases = age_ref.shape[0]
    skip = pack_ref[:, 0:1]
    for canvas in range(canvases):
        cut = canvas_cut(across_ref, canvas, canvases)
        mixer = height_conv(across_ref[:, cut].astype(f32), tall_ref, age_ref[canvas], 1, height)
        out_ref[:, cut] = (mixer + skip * stream_ref[:, cut].astype(f32)).astype(bf16)


def tall_mixed(height, across, stream, tall, age, pack):
    return pl.pallas_call(
        partial(tall_mixed_body, height),
        in_specs=[vmem_spec()] * 5,
        out_specs=vmem_spec(),
        out_shape=struct(across.shape, bf16),
        name="tall_mixed",
        **params(10_000_000, 1_000_000),
    )(across, stream, tall, age, pack)


def tall_next_body(height, keep_ref, near_ref, far_ref, stream_ref, pack_ref, tall_ref, age_ref,
                   next_ref, branch_ref, out_ref):
    canvases = age_ref.shape[0]
    bias, scale = pack_ref[:, 3:4], pack_ref[:, 4:5]
    for canvas in range(canvases):
        cut = canvas_cut(stream_ref, canvas, canvases)
        branch = keep_ref[:, cut].astype(f32) + near_ref[:, cut].astype(f32) + far_ref[:, cut].astype(f32) + bias
        branch_ref[:, cut] = branch
        low = (stream_ref[:, cut].astype(f32) + scale * branch).astype(bf16)
        next_ref[:, cut] = low
        out_ref[:, cut] = height_conv(low.astype(f32), tall_ref, age_ref[canvas], 1, height).astype(bf16)


def tall_next(height, branches, stream, pack, tall, age):
    return pl.pallas_call(
        partial(tall_next_body, height),
        in_specs=[vmem_spec()] * 7,
        out_specs=[vmem_spec()] * 3,
        out_shape=[struct(stream.shape, bf16), struct(stream.shape, f32), struct(stream.shape, bf16)],
        name="tall_next",
        **params(10_000_000, 1_000_000),
    )(*branches, stream, pack, tall, age)


def tall_back_body(height, conv_ref, rest_ref, tall_ref, fore_ref, pack_ref, branch_ref,
                   grad_ref, low_ref, sums_ref):
    canvases = fore_ref.shape[0]
    scale = pack_ref[:, 4:5]
    scale_grad = jnp.zeros((conv_ref.shape[0], 1), f32)
    bias_grad = jnp.zeros((conv_ref.shape[0], 1), f32)
    for canvas in range(canvases):
        cut = canvas_cut(conv_ref, canvas, canvases)
        grad = rest_ref[:, cut].astype(f32) + height_conv(
            conv_ref[:, cut].astype(f32), tall_ref, fore_ref[canvas], -1, height
        )
        grad_ref[:, cut] = grad
        scaled = grad * scale
        low_ref[:, cut] = scaled.astype(bf16)
        scale_grad += jnp.sum(grad * branch_ref[:, cut], axis=1, keepdims=True)
        bias_grad += jnp.sum(scaled, axis=1, keepdims=True)
    put_columns(sums_ref, [scale_grad, bias_grad])


def tall_back(height, conv, rest, tall, fore, pack, branch):
    return pl.pallas_call(
        partial(tall_back_body, height),
        in_specs=[vmem_spec()] * 6,
        out_specs=[vmem_spec()] * 3,
        out_shape=[struct(conv.shape, f32), struct(conv.shape, bf16), struct((conv.shape[0], lane), f32)],
        name="tall_back",
        **params(10_000_000, 1_000_000),
    )(conv, rest, tall, fore, pack, branch)


def tall_norm_back_body(height, channels_all, keep_ref, near_ref, far_ref, mixed_ref, stats_ref, pack_ref, stream_ref,
                        grad_ref, tall_ref, fore_ref, conv_ref, rest_ref, low_ref, sums_ref):
    canvases = fore_ref.shape[0]
    mixed_grad, gain_grad, shift_grad = norm_backward(
        (keep_ref, near_ref, far_ref), mixed_ref, stats_ref, pack_ref, channels_all
    )
    skip = pack_ref[:, 0:1]
    low_ref[...] = mixed_grad.astype(bf16)
    rest_ref[...] = (grad_ref[...] + skip * mixed_grad).astype(bf16)
    skip_grad = jnp.sum(mixed_grad * stream_ref[...].astype(f32), axis=1, keepdims=True)
    for canvas in range(canvases):
        cut = canvas_cut(conv_ref, canvas, canvases)
        conv_ref[:, cut] = height_conv(
            low_ref[:, cut].astype(f32), tall_ref, fore_ref[canvas], -1, height
        ).astype(bf16)
    put_columns(sums_ref, [skip_grad, gain_grad, shift_grad])


def tall_norm_back(height, channels_all, grads, mixed, stats, pack, stream, grad, tall, fore):
    return pl.pallas_call(
        partial(tall_norm_back_body, height, channels_all),
        in_specs=[vmem_spec()] * 10,
        out_specs=[vmem_spec()] * 4,
        out_shape=[struct(mixed.shape, bf16)] * 3 + [struct((mixed.shape[0], lane), f32)],
        name="tall_norm_back",
        **params(10_000_000, 1_000_000),
    )(*grads, mixed, stats, pack, stream, grad, tall, fore)


def tall_kernel_grad_body(height, grad_ref, input_ref, age_ref, out_ref):
    canvases = age_ref.shape[0]
    total = jnp.zeros(out_ref.shape, f32)
    for canvas in range(canvases):
        cut = canvas_cut(grad_ref, canvas, canvases)
        total = height_products(
            grad_ref[:, cut].astype(f32), input_ref[:, cut].astype(f32), age_ref[canvas], height, total
        )
    out_ref[...] = total


def tall_kernel_grad(height, grad, inputs, age):
    return pl.pallas_call(
        partial(tall_kernel_grad_body, height),
        in_specs=[vmem_spec()] * 3,
        out_specs=vmem_spec(),
        out_shape=struct((grad.shape[0], lane), f32),
        name="tall_kernel_grad",
        **params(10_000_000, 1_000_000),
    )(grad, inputs, age)


root = 0.7978845608028654
cubic = 0.044715


def gather_into(me_ref, parts, whole_ref):
    me = me_ref[0]
    for flip, part in enumerate(parts):
        whole_ref[me ^ flip] = part[...]


def scatter_out(me_ref, whole_ref, outs):
    me = me_ref[0]
    for flip, out in zip((3, 1, 2, 0), outs, strict=True):
        out[...] = whole_ref[me ^ flip]


def mlp_forward(me_ref, parts, full_ref, shape_ref, weight_in_ref, bias_ref, normed_ref, hidden_ref, slope_ref, stats_ref):
    gather_into(me_ref, parts, full_ref)
    mixed = full_ref[...].astype(f32).reshape(-1, full_ref.shape[2])
    average = jnp.mean(mixed, axis=0, keepdims=True)
    moved = mixed - average
    inverse = lax.rsqrt(jnp.mean(moved * moved, axis=0, keepdims=True) + epsilon)
    centred = moved * inverse
    stats_ref[0:1, :] = average
    stats_ref[1:2, :] = inverse
    normed = (centred * shape_ref[:, 0:1] + shape_ref[:, 1:2]).astype(bf16)
    normed_ref[...] = normed
    before = dot(weight_in_ref[0], normed, 0, 0) + bias_ref[...]
    square = before * before
    bend = jnp.tanh(root * before * (1.0 + cubic * square))
    half = 0.5 * (1.0 + bend)
    hidden_ref[...] = (before * half).astype(bf16)
    slope_ref[...] = (half + 0.5 * before * (1.0 - bend * bend) * root * (1.0 + 3.0 * cubic * square)).astype(slope_ref.dtype)
    return centred


def mlp_first_body(me_ref, own, near, far, cross, shape_ref, weight_in_ref, bias_ref, weight_out_ref,
                   send_far, send_own, keep_far, keep_own, normed_ref, hidden_ref, slope_ref, stats_ref, full_ref, sum_ref):
    mlp_forward(me_ref, (own, near, far, cross), full_ref, shape_ref, weight_in_ref, bias_ref,
                normed_ref, hidden_ref, slope_ref, stats_ref)
    partial_out = dot(weight_out_ref[0], hidden_ref[...], 0, 0)
    sum_ref[...] = partial_out.astype(bf16).reshape(sum_ref.shape)
    scatter_out(me_ref, sum_ref, (send_far, send_own, keep_far, keep_own))


def mlp_backward(me_ref, parts, full_ref, weight_out_ref, weight_in_ref, normed_ref, hidden_ref, slope, shape_ref, centred,
                 sum_ref, outs, in_grad_ref, out_grad_ref, bias_grad_ref, in_total, out_total):
    step, last = pl.program_id(0), pl.num_programs(0) - 1
    gather_into(me_ref, parts, full_ref)
    grad = full_ref[...].reshape(-1, full_ref.shape[2])
    before_grad = (dot(weight_out_ref[0], grad, 1, 0) * slope).astype(bf16)
    normed_part = dot(weight_in_ref[0], before_grad, 1, 0)
    channels = sum_ref.shape[1] - 16
    scaled = normed_part * shape_ref[:, 0:1]
    scaled_sum = jnp.sum(scaled, axis=0, keepdims=True)
    paired_sum = jnp.sum(scaled * centred, axis=0, keepdims=True)
    places = lax.broadcasted_iota(jnp.int32, (16, grad.shape[1]), 0)
    tail = jnp.where(places == 0, scaled_sum, jnp.where(places == 1, paired_sum, 0.0)).astype(bf16)
    for index in range(sum_ref.shape[0]):
        sum_ref[index, 0:channels, :] = normed_part[index * channels:(index + 1) * channels].astype(bf16)
        sum_ref[index, channels:, :] = tail
    scatter_out(me_ref, sum_ref, outs)
    bias = jnp.sum(before_grad.astype(f32), axis=1, keepdims=True)
    in_part = dot(normed_ref[...], before_grad, 1, 1)
    out_part = dot(hidden_ref[...], grad, 1, 1)

    @pl.when(step == 0)
    def _():
        bias_grad_ref[...] = jnp.broadcast_to(bias, bias_grad_ref.shape)
        in_total[...] = in_part
        out_total[...] = out_part

    @pl.when(step > 0)
    def _():
        bias_grad_ref[...] += jnp.broadcast_to(bias, bias_grad_ref.shape)
        in_total[...] += in_part
        out_total[...] += out_part

    @pl.when(step == last)
    def _():
        in_grad_ref[...] = in_total[...].astype(bf16)
        out_grad_ref[...] = out_total[...].astype(bf16)


def mlp_both_body(me_ref, own, near, far, cross, grad_own, grad_near, grad_far, grad_cross, shape_ref, weight_in_ref,
                  bias_ref, weight_out_ref,
                  out_sf, out_so, out_kf, out_ko, back_sf, back_so, back_kf, back_ko, stats_ref,
                  in_grad_ref, out_grad_ref, bias_grad_ref,
                  full_ref, sum_ref, back_ref, normed_ref, hidden_ref, slope_ref, in_total, out_total):
    centred = mlp_forward(me_ref, (own, near, far, cross), full_ref, shape_ref, weight_in_ref, bias_ref,
                          normed_ref, hidden_ref, slope_ref, stats_ref)
    sum_ref[...] = dot(weight_out_ref[0], hidden_ref[...], 0, 0).astype(bf16).reshape(sum_ref.shape)
    scatter_out(me_ref, sum_ref, (out_sf, out_so, out_kf, out_ko))
    mlp_backward(me_ref, (grad_own, grad_near, grad_far, grad_cross), full_ref, weight_out_ref, weight_in_ref,
                 normed_ref, hidden_ref, slope_ref[...], shape_ref, centred, back_ref,
                 (back_sf, back_so, back_kf, back_ko), in_grad_ref, out_grad_ref, bias_grad_ref, in_total, out_total)


def mlp_back_body(me_ref, own, near, far, cross, grad_own, grad_near, grad_far, grad_cross, shape_ref, weight_in_ref,
                  weight_out_ref, normed_ref, hidden_ref, slope_ref, stats_ref,
                  back_sf, back_so, back_kf, back_ko, in_grad_ref, out_grad_ref, bias_grad_ref,
                  full_ref, back_ref, in_total, out_total):
    gather_into(me_ref, (own, near, far, cross), full_ref)
    centred = (full_ref[...].astype(f32).reshape(-1, full_ref.shape[2]) - stats_ref[0:1, :]) * stats_ref[1:2, :]
    mlp_backward(me_ref, (grad_own, grad_near, grad_far, grad_cross), full_ref, weight_out_ref, weight_in_ref,
                 normed_ref, hidden_ref, slope_ref[...], shape_ref, centred, back_ref,
                 (back_sf, back_so, back_kf, back_ko), in_grad_ref, out_grad_ref, bias_grad_ref, in_total, out_total)


tile = 256


def pixel_block(rows):
    return pl.BlockSpec((rows, tile), lambda i: (0, i))


def fixed_block(shape):
    return pl.BlockSpec(shape, lambda i: (0,) * len(shape))


def section_block(section, shape):
    return pl.BlockSpec((1,) + shape, lambda i: (section, 0, 0))


def mlp_first(section, me, parts, shaping, weight_in, bias, weight_out):
    own = parts[0]
    channels, pixels = own.shape
    wide, units = weight_in.shape[1], weight_in.shape[2]
    piece = pixel_block(channels)
    return pl.pallas_call(
        mlp_first_body,
        grid=(pixels // tile,),
        in_specs=[smem_spec()] + [piece] * 4 + [
            fixed_block(shaping.shape), section_block(section, (wide, units)), fixed_block(bias.shape),
            section_block(section, (units, wide)),
        ],
        out_specs=[piece] * 4 + [pixel_block(wide), pixel_block(units), pixel_block(units), pixel_block(8)],
        out_shape=[struct(own.shape, bf16)] * 4 + [
            struct((wide, pixels), bf16), struct((units, pixels), bf16), struct((units, pixels), f32), struct((8, pixels), f32),
        ],
        scratch_shapes=[pltpu.VMEM((4, channels, tile), bf16), pltpu.VMEM((4, channels, tile), bf16)],
        name="mlp_first",
        **params(1_300_000_000, 6_000_000),
    )(me, *parts, shaping, weight_in, bias, weight_out)


def mlp_both(section, me, parts, grads, shaping, weight_in, bias, weight_out):
    own = parts[0]
    channels, pixels = own.shape
    wide, units = weight_in.shape[1], weight_in.shape[2]
    piece, back = pixel_block(channels), pixel_block(channels + 16)
    return pl.pallas_call(
        mlp_both_body,
        grid=(pixels // tile,),
        in_specs=[smem_spec()] + [piece] * 8 + [
            fixed_block(shaping.shape), section_block(section, (wide, units)), fixed_block(bias.shape),
            section_block(section, (units, wide)),
        ],
        out_specs=[piece] * 4 + [back] * 4 + [
            pixel_block(8), fixed_block((wide, units)), fixed_block((units, wide)), fixed_block((units, lane)),
        ],
        out_shape=[struct(own.shape, bf16)] * 4 + [struct((channels + 16, pixels), bf16)] * 4 + [
            struct((8, pixels), f32), struct((wide, units), bf16), struct((units, wide), bf16), struct((units, lane), f32),
        ],
        scratch_shapes=[
            pltpu.VMEM((4, channels, tile), bf16), pltpu.VMEM((4, channels, tile), bf16),
            pltpu.VMEM((4, channels + 16, tile), bf16), pltpu.VMEM((wide, tile), bf16),
            pltpu.VMEM((units, tile), bf16), pltpu.VMEM((units, tile), f32),
            pltpu.VMEM((wide, units), f32), pltpu.VMEM((units, wide), f32),
        ],
        name="mlp_both",
        **params(3_600_000_000, 9_000_000),
    )(me, *parts, *grads, shaping, weight_in, bias, weight_out)


def mlp_back(section, me, parts, grads, shaping, weight_in, weight_out, normed, hidden, slope, stats):
    own = parts[0]
    channels, pixels = own.shape
    wide, units = weight_in.shape[1], weight_in.shape[2]
    piece, back = pixel_block(channels), pixel_block(channels + 16)
    return pl.pallas_call(
        mlp_back_body,
        grid=(pixels // tile,),
        in_specs=[smem_spec()] + [piece] * 8 + [
            fixed_block(shaping.shape), section_block(section, (wide, units)), section_block(section, (units, wide)),
            pixel_block(wide), pixel_block(units), pixel_block(units), pixel_block(8),
        ],
        out_specs=[back] * 4 + [fixed_block((wide, units)), fixed_block((units, wide)), fixed_block((units, lane))],
        out_shape=[struct((channels + 16, pixels), bf16)] * 4 + [
            struct((wide, units), bf16), struct((units, wide), bf16), struct((units, lane), f32),
        ],
        scratch_shapes=[
            pltpu.VMEM((4, channels, tile), bf16), pltpu.VMEM((4, channels + 16, tile), bf16),
            pltpu.VMEM((wide, units), f32), pltpu.VMEM((units, wide), f32),
        ],
        name="mlp_back",
        **params(2_400_000_000, 9_000_000),
    )(me, *parts, *grads, shaping, weight_in, weight_out, normed, hidden, slope, stats)


core_pairs = [(i, i ^ 1) for i in range(4)]
chip_pairs = [(i, i ^ 2) for i in range(4)]


def gather_channels(own):
    far = lax.ppermute(own, "ch", chip_pairs)
    near = lax.ppermute(own, "ch", core_pairs)
    cross = lax.ppermute(far, "ch", core_pairs)
    return (own, near, far, cross)


def scatter_channels(send_far, send_own, keep_far, keep_own):
    near_far = lax.ppermute(send_far, "ch", core_pairs)
    near_own = lax.ppermute(send_own, "ch", core_pairs)
    onward = (keep_far.astype(f32) + near_far.astype(f32)).astype(bf16)
    far = lax.ppermute(onward, "ch", chip_pairs)
    return (keep_own, near_own, far)


def rows_to_cols(parts, count):
    pieces = []
    for part in parts:
        canvases, rows, channels, width = part.shape
        cut = part.reshape(canvases, rows, channels, count, width // count)
        pieces.append(cut.transpose(3, 2, 0, 1, 4).reshape(count, channels, -1))
    moved = lax.all_to_all(jnp.stack(pieces, axis=1), "rows", split_axis=0, concat_axis=0, tiled=True)
    moved = moved.reshape(count, len(parts), channels, canvases, rows, width // count)
    return [moved[:, k].transpose(1, 2, 0, 3, 4).reshape(channels, -1) for k in range(len(parts))]


def cols_to_rows(parts, count, canvases, rows, width):
    channels = parts[0].shape[0]
    pieces = []
    for part in parts:
        cut = part.reshape(channels, canvases, count, rows, width // count)
        pieces.append(cut.transpose(2, 0, 1, 3, 4).reshape(count, channels, -1))
    moved = lax.all_to_all(jnp.stack(pieces, axis=1), "rows", split_axis=0, concat_axis=0, tiled=True)
    moved = moved.reshape(count, len(parts), channels, canvases, rows, width // count)
    return [moved[:, k].transpose(2, 3, 1, 0, 4).reshape(canvases, rows, channels, width) for k in range(len(parts))]


def crop_reach(starts):
    count = starts.shape[1]
    places = jnp.arange(count, dtype=jnp.int32)[None, :]
    first = lax.cummax(jnp.where(starts > 0, places, 0), axis=1)
    following = lax.cummin(jnp.where(starts > 0, places, count), axis=1, reverse=True)
    following = jnp.concatenate([following[:, 1:], jnp.full((starts.shape[0], 1), count, jnp.int32)], axis=1)
    return places - first, following - 1 - places


def band_turns(age):
    return jnp.max(age.reshape(age.shape[0], -1, band), axis=2) // ahead + 1


def on_device(
    count,
    pixels,
    row_starts,
    col_starts,
    log_step,
    log_decay,
    frequency,
    coef_real,
    coef_imag,
    skip_gain,
    norm_gain,
    norm_shift,
    weight_in,
    bias_in,
    weight_out,
    bias_out,
    layer_scale,
    cotangent,
):
    canvases, rows, width, channels = pixels.shape
    height = row_starts.shape[1]
    channels_all = weight_in.shape[1]
    lengths = (height, width)
    me = lax.axis_index("ch").astype(jnp.int32).reshape(1)

    stream = jnp.swapaxes(pixels, 2, 3)
    upstream = jnp.swapaxes(cotangent, 2, 3)
    states = [jnp.swapaxes(value, 2, 3) for value in (log_decay, frequency, coef_real, coef_imag)]

    age, fore = crop_reach(col_starts)
    age_reach, fore_reach = band_turns(age), band_turns(fore)
    age = jnp.broadcast_to(age[:, :, None], (canvases, width, lane))
    fore = jnp.broadcast_to(fore[:, :, None], (canvases, width, lane))
    row_age, row_fore = crop_reach(row_starts)
    row_age = jnp.repeat(row_age, width // count, axis=1)[:, None, :]
    row_fore = jnp.repeat(row_fore, width // count, axis=1)[:, None, :]

    packs = [
        jnp.stack([skip_gain[k], norm_gain[k], norm_shift[k], bias_out[k], layer_scale[k]], axis=1) for k in range(2)
    ]
    shaping_all = lax.all_gather(jnp.stack([norm_gain, norm_shift], axis=2), "ch", axis=1, tiled=True)
    bias_columns = [bias_in[k][:, None] for k in range(2)]

    top_scaled = upstream.astype(f32) * packs[1][:, 4:5]
    top_low = top_scaled.astype(bf16).transpose(2, 0, 1, 3).reshape(channels, -1)
    top_parts = gather_channels(top_low)
    top_bias_grad = jnp.sum(top_scaled, axis=(0, 1, 3))

    tall, wide = zip(
        *[s4_kernels(k, lengths, log_step, *states, rows) for k in range(2)], strict=True
    )

    across = wide_forward(stream, wide[0], age, age_reach)
    across_cols, stream_cols = rows_to_cols([across, stream], count)
    mixed_low = tall_mixed(height, across_cols, stream_cols, tall[0], row_age, packs[0])
    low_parts = gather_channels(mixed_low)
    first = mlp_first(0, me, low_parts, shaping_all[0], weight_in, bias_columns[0], weight_out)
    normed_low, hidden_low, slope_low, stats_low = first[4:]
    branches = scatter_channels(*first[:4])

    next_cols, branch_cols, tall_cols = tall_next(height, branches, stream_cols, packs[0], tall[1], row_age)
    tall_rows, next_rows = cols_to_rows([tall_cols, next_cols], count, canvases, rows, width)
    mixed_top = wide_mixed(tall_rows, next_rows, wide[1], age, age_reach, packs[1])
    top_mixed_parts = gather_channels(mixed_top)
    both = mlp_both(1, me, top_mixed_parts, top_parts, shaping_all[1], weight_in, bias_columns[1], weight_out)
    stats_top, top_in_grad, top_out_grad, top_bias_in = both[8:]
    top_grads = scatter_channels(*both[4:8])
    top_weights = lax.psum((top_in_grad, top_out_grad), "rows")

    conv_rows, rest_rows, grad_rows, top_sums = wide_norm_back(
        channels_all, top_grads, mixed_top, stats_top, packs[1], next_rows, upstream, wide[1], fore, fore_reach
    )
    conv_cols, rest_cols = rows_to_cols([conv_rows, rest_rows], count)
    grad_cols, grad_low, low_branch_sums = tall_back(height, conv_cols, rest_cols, tall[1], row_fore, packs[0], branch_cols)

    grad_parts = gather_channels(grad_low)
    back = mlp_back(
        0, me, low_parts, grad_parts, shaping_all[0], weight_in, weight_out, normed_low, hidden_low, slope_low, stats_low
    )
    low_in_grad, low_out_grad, low_bias_in = back[4:]
    low_grads = scatter_channels(*back[:4])
    low_conv_cols, low_rest_cols, low_grad_cols, low_sums = tall_norm_back(
        height, channels_all, low_grads, mixed_low, stats_low, packs[0], stream_cols, grad_cols, tall[0], row_fore
    )
    low_weights = lax.psum((low_in_grad, low_out_grad), "rows")
    low_conv_rows, low_rest_rows = cols_to_rows([low_conv_cols, low_rest_cols], count, canvases, rows, width)
    pixels_grad = wide_back(low_conv_rows, low_rest_rows, wide[0], fore, fore_reach)

    top_branches = scatter_channels(*both[:4])
    branch_top = sum(part.astype(f32) for part in top_branches) + packs[1][:, 3:4]
    branch_top = branch_top.reshape(channels, canvases, rows, width).transpose(1, 2, 0, 3)
    activations = (next_rows.astype(f32) + packs[1][:, 4:5] * branch_top).astype(bf16)
    top_scale_grad = jnp.sum(upstream.astype(f32) * branch_top, axis=(0, 1, 3))

    top_tall = tall_kernel_grad(height, conv_cols, next_cols, row_age)
    top_wide = wide_kernel_grad(grad_rows, tall_rows, age, age_reach)
    low_tall = tall_kernel_grad(height, low_grad_cols, across_cols, row_age)
    low_wide = wide_kernel_grad(low_conv_rows, stream, age, age_reach)
    tall_grads = jnp.stack([low_tall, top_tall])
    wide_grads = jnp.stack([low_wide, top_wide])
    columns = jnp.stack(
        [
            jnp.concatenate([low_sums[:, 0:3], low_branch_sums[:, 1:2], low_branch_sums[:, 0:1]], axis=1),
            jnp.concatenate([top_sums[:, 0:3], top_bias_grad[:, None], top_scale_grad[:, None]], axis=1),
        ]
    )
    bias_grads = jnp.stack([low_bias_in[:, 0], top_bias_in[:, 0]])
    tall_grads, wide_grads, columns, bias_grads = lax.psum((tall_grads, wide_grads, columns, bias_grads), "rows")
    step_grad, decay_grad, freq_grad, real_grad, imag_grad = s4_pullback(
        lengths, tall_grads, wide_grads, log_step, *states
    )
    return (
        jnp.swapaxes(activations, 2, 3),
        jnp.swapaxes(pixels_grad, 2, 3),
        step_grad,
        jnp.swapaxes(decay_grad, 2, 3),
        jnp.swapaxes(freq_grad, 2, 3),
        jnp.swapaxes(real_grad, 2, 3),
        jnp.swapaxes(imag_grad, 2, 3),
        columns[:, :, 0],
        columns[:, :, 1],
        columns[:, :, 2],
        jnp.stack([low_weights[0], top_weights[0]]).astype(f32),
        bias_grads,
        jnp.stack([low_weights[1], top_weights[1]]).astype(f32),
        columns[:, :, 3],
        columns[:, :, 4],
    )


def solution(mesh):
    picture = P(None, "rows", None, "ch")
    state = P(None, None, "ch", None)
    step = P(None, None, "ch")
    vector = P(None, "ch")
    into = P(None, None, "ch")
    out = P(None, "ch", None)
    in_specs = (
        picture, P(), P(), step, state, state, state, state, vector, vector, vector, into, vector, out, vector, vector, picture,
    )
    out_specs = (
        picture, picture, step, state, state, state, state, vector, vector, vector, into, vector, out, vector, vector,
    )
    return jax.shard_map(
        partial(on_device, mesh.shape["rows"]), mesh=mesh, in_specs=in_specs, out_specs=out_specs, check_vma=False
    )
```

```python
from functools import partial

import jax
import jax.numpy as jnp
from jax import lax
from jax.experimental import pallas as pl
from jax.experimental.pallas import tpu as pltpu
from jax.sharding import PartitionSpec as P


epsilon = 1e-06
bf16 = jnp.bfloat16
f32 = jnp.float32
vmem_bytes = 56 * 1024 * 1024
ahead = 8
band = 16
lane = 128


def dot(a, b, ca, cb):
    return lax.dot_general(a, b, (((ca,), (cb,)), ((), ())), preferred_element_type=f32)


def vmem_spec():
    return pl.BlockSpec(memory_space=pltpu.VMEM)


def smem_spec():
    return pl.BlockSpec(memory_space=pltpu.SMEM)


def any_spec():
    return pl.BlockSpec(memory_space=pl.ANY)


def struct(shape, dtype):
    return jax.ShapeDtypeStruct(shape, dtype)


def params(flops=0, moved=0):
    return dict(
        compiler_params=pltpu.CompilerParams(vmem_limit_bytes=vmem_bytes),
        cost_estimate=pl.CostEstimate(flops=flops, bytes_accessed=moved, transcendentals=0),
    )


def launch(body, name, ins, outs, scratch=(), scalars=(), after=()):
    given = len(scalars) + len(ins)

    def run(*refs):
        body(*refs[:given], *refs[given + len(after):])

    return pl.pallas_call(
        run,
        in_specs=[smem_spec()] * len(scalars) + [vmem_spec()] * len(ins) + [any_spec()] * len(after),
        out_specs=[vmem_spec()] * len(outs),
        out_shape=list(outs),
        scratch_shapes=list(scratch),
        name=name,
        **params(10_000_000, 1_000_000),
    )(*scalars, *ins, *after)


def swap(parts, number, chunk):
    width = 16 << chunk
    lanes = lax.broadcasted_iota(jnp.int32, parts[0].shape, 1)
    low = (lanes // width) % 2 == 0
    parts = list(parts)
    for i in range(8):
        j = i | (1 << number)
        if i != j:
            a, b = parts[i], parts[j]
            parts[i] = jnp.where(low, a, pltpu.roll(b, width, 1))
            parts[j] = jnp.where(low, pltpu.roll(a, lane - width, 1), b)
    return parts


half_rows = 96
strip = 32


def pieces_from_rows(get, out_ref, kind):
    for at in range(0, half_rows, strip):
        parts = [get((i >> 1) & 1, i & 1, slice((i >> 2) * half_rows + at, (i >> 2) * half_rows + at + strip)) for i in range(8)]
        for bit in range(3):
            parts = swap(parts, bit, bit)
        for target in range(8):
            out_ref[target, kind, at:at + strip, :] = parts[target].astype(bf16)


def rows_from_pieces(in_ref, kind, put):
    for at in range(0, half_rows, strip):
        parts = [in_ref[source, kind, at:at + strip, :].astype(f32) for source in range(8)]
        for bit in range(3):
            parts = swap(parts, bit, bit)
        for i in range(8):
            put((i >> 1) & 1, i & 1, slice((i >> 2) * half_rows + at, (i >> 2) * half_rows + at + strip), parts[i])


def pieces_from_cols(get, out_ref, kind):
    for at in range(0, half_rows, strip):
        parts = []
        for i in range(8):
            upper, half, canvas = i >> 2, (i >> 1) & 1, i & 1
            first = (canvas * 2 + upper) * lane
            parts.append(get(slice(half * half_rows + at, half * half_rows + at + strip), slice(first, first + lane)))
        parts = swap(swap(parts, 1, 2), 0, 1)
        for target in range(8):
            out_ref[target, kind, at:at + strip, :] = parts[target].astype(bf16)


def cols_from_pieces(in_ref, kind, out_ref):
    for at in range(0, half_rows, strip):
        parts = [in_ref[source, kind, at:at + strip, :].astype(f32) for source in range(8)]
        parts = swap(swap(parts, 1, 2), 0, 1)
        for i in range(8):
            upper, half, canvas = i >> 2, (i >> 1) & 1, i & 1
            first = (canvas * 2 + upper) * lane
            out_ref[half * half_rows + at:half * half_rows + at + strip, first:first + lane] = parts[i].astype(out_ref.dtype)


def piece_shape(kinds):
    return struct((8, kinds, half_rows, lane), bf16)


def state_powers(step, decay, frequency):
    size = jnp.exp(-step * decay)
    turn = step * frequency
    z = (size * jnp.cos(turn), size * jnp.sin(turn))

    def times(p, q):
        return (p[0] * q[0] - p[1] * q[1], p[0] * q[1] + p[1] * q[0])

    z2 = times(z, z)
    z3 = times(z2, z)
    z4 = times(z2, z2)
    return [None, z, z2, z3, z4, times(z4, z), times(z4, z2), times(z4, z3)], times(z4, z4), times


def pack_lanes(value):
    half = value.shape[0] // 2
    return jnp.concatenate([value[:half], value[half:]], axis=1)


def unpack_lanes(value):
    half = value.shape[1] // 2
    return jnp.concatenate([value[:, :half], value[:, half:]], axis=0)


def s4_section(direction, length, section, step_ref, decay_ref, freq_ref, real_ref, imag_ref, q_ref, flat_ref):
    channels = step_ref.shape[2]
    step = jnp.exp(step_ref[section, direction:direction + 1, :])
    step = jnp.concatenate([step, step], axis=1)
    decay = jnp.exp(pack_lanes(decay_ref[section, direction]))
    powers, z8, times = state_powers(step, decay, pack_lanes(freq_ref[section, direction]))
    for a in range(1, ahead):
        q_ref[2 * a] = powers[a][0]
        q_ref[2 * a + 1] = powers[a][1]
    q_ref[0] = z8[0]
    q_ref[1] = z8[1]

    def block(b, carry):
        pr, pi = carry
        rows = [jnp.sum(pr, axis=0, keepdims=True)]
        for a in range(1, ahead):
            rows.append(jnp.sum(pr * q_ref[2 * a] - pi * q_ref[2 * a + 1], axis=0, keepdims=True))
        flat_ref[pl.ds(pl.multiple_of(b * ahead, ahead), ahead), :] = step * jnp.concatenate(rows, axis=0)
        zr, zi = q_ref[0], q_ref[1]
        return (pr * zr - pi * zi, pr * zi + pi * zr)

    start = (pack_lanes(real_ref[section, direction]), pack_lanes(imag_ref[section, direction]))
    lax.fori_loop(0, length // ahead, block, start)
    flat = jnp.transpose(flat_ref[...])
    return (flat[:channels] + flat[channels:]).astype(bf16).astype(f32)


def s4_scratch(states, channels):
    return [pltpu.VMEM((2 * ahead, states // 2, 2 * channels), f32), pltpu.VMEM((lane, 2 * channels), f32)]


def s4_wide_body(length, section, copies, step_ref, decay_ref, freq_ref, real_ref, imag_ref, out_ref, q_ref, flat_ref):
    kernel = s4_section(1, length, section, step_ref, decay_ref, freq_ref, real_ref, imag_ref, q_ref, flat_ref)
    out_ref[...] = jnp.transpose(jnp.concatenate([kernel] * copies, axis=0))


def s4_wide(section, length, copies, log_step, *states):
    channels = states[0].shape[3]
    return launch(
        partial(s4_wide_body, length, section, copies), "s4_wide", [log_step, *states],
        [struct((lane, copies * channels), f32)], s4_scratch(states[0].shape[2], channels),
    )[0]


def s4_rest_body(lengths, copies, step_ref, decay_ref, freq_ref, real_ref, imag_ref, upstream_ref, pack_ref,
                 tall_low, tall_top, wide_top, scaled_ref, sums_ref, q_ref, flat_ref):
    refs = (step_ref, decay_ref, freq_ref, real_ref, imag_ref, q_ref, flat_ref)
    tall_low[...] = s4_section(0, lengths[0], 0, *refs)
    tall_top[...] = s4_section(0, lengths[0], 1, *refs)
    wide_top[...] = jnp.transpose(jnp.concatenate([s4_section(1, lengths[1], 1, *refs)] * copies, axis=0))
    scale = pack_ref[:, 4:5]
    total = jnp.zeros(scale.shape, f32)
    rows = upstream_ref.shape[1]
    for canvas in range(upstream_ref.shape[0]):
        for row in range(rows):
            scaled = upstream_ref[canvas, row].astype(f32) * scale
            at = (canvas * rows + row) * lane
            scaled_ref[:, at:at + lane] = scaled.astype(bf16)
            total += jnp.sum(scaled, axis=1, keepdims=True)
    put_columns(sums_ref, [total])


def s4_rest(lengths, copies, log_step, states, upstream, pack, after):
    channels = states[0].shape[3]
    pixels = upstream.shape[0] * upstream.shape[1] * lane
    column = struct((channels, lane), f32)
    return launch(
        partial(s4_rest_body, lengths, copies), "s4_rest", [log_step, *states, upstream, pack],
        [column, column, struct((lane, copies * channels), f32), struct((channels, pixels), bf16), column],
        s4_scratch(states[0].shape[2], channels), after=after,
    )


def pull_body(section, lengths, count, *refs):
    grads_ref, step_ref, decay_ref, freq_ref, real_ref, imag_ref = refs[:6]
    dstep_ref, ddecay_ref, dfreq_ref, dreal_ref, dimag_ref, vectors_ref, turn_ref, spread_ref, q_ref, s_ref = refs[6 + count:]
    channels = step_ref.shape[2]
    states = decay_ref.shape[2]
    tiles = 2 * channels // lane
    for direction, length in enumerate(lengths):
        step = jnp.exp(step_ref[0, direction:direction + 1, :])
        decay = jnp.exp(decay_ref[0, direction])
        freq = freq_ref[0, direction]
        wide_step = jnp.concatenate([step, step], axis=1)
        powers, z8, times = state_powers(wide_step, pack_lanes(decay), pack_lanes(freq))
        for a in range(ahead):
            for part in range(2):
                value = (z8 if a == 0 else powers[a])[part]
                for t in range(tiles):
                    q_ref[2 * a + part, t] = value[:, t * lane:(t + 1) * lane]
        first = (1 - direction) * lane
        turn_ref[0:channels, :] = grads_ref[:, first:first + lane]
        turn_ref[channels:2 * channels, :] = grads_ref[:, first:first + lane]
        flat = jnp.transpose(turn_ref[...])
        if direction == 0:
            vectors_ref[...] = flat[length:length + 16, 0:channels] if length + 16 <= lane else jnp.zeros((16, channels), f32)
        for place in range(length):
            for t in range(tiles):
                spread_ref[t, place] = jnp.broadcast_to(flat[place:place + 1, t * lane:(t + 1) * lane], (8, lane))
        turns = length // ahead
        groups = states // 16

        def group(index, carry):
            t = index // groups
            part = pl.ds(pl.multiple_of(lax.rem(index, groups) * 8, 8), 8)
            q = [(q_ref[2 * a, t, part, :], q_ref[2 * a + 1, t, part, :]) for a in range(ahead)]
            zr, zi = q[0]

            def block(turn, sums):
                s0r, s0i, s1r, s1i = sums
                b = turns - 1 - turn
                t0r = t0i = t1r = t1i = None
                for a in range(ahead - 1, 0, -1):
                    g = spread_ref[t, b * ahead + a]
                    x, y = g * q[a][0], g * q[a][1]
                    t0r, t0i = (x, y) if t0r is None else (t0r + x, t0i + y)
                    t1r, t1i = (t0r, t0i) if t1r is None else (t1r + t0r, t1i + t0i)
                t0r = t0r + spread_ref[t, b * ahead]
                base = (b * ahead).astype(f32)
                v1r, v1i = t1r + base * t0r, t1i + base * t0i
                return (
                    s0r * zr - s0i * zi + t0r,
                    s0r * zi + s0i * zr + t0i,
                    s1r * zr - s1i * zi + v1r,
                    s1r * zi + s1i * zr + v1i,
                )

            zero = jnp.zeros((8, lane), f32)
            sums = lax.fori_loop(0, turns, block, (zero, zero, zero, zero))
            for k in range(4):
                s_ref[k, t, part, :] = sums[k]
            return carry

        lax.fori_loop(0, tiles * groups, group, 0)
        s0r, s0i, s1r, s1i = [
            unpack_lanes(jnp.concatenate([s_ref[k, t] for t in range(tiles)], axis=1)) for k in range(4)
        ]
        real, imag = real_ref[0, direction], imag_ref[0, direction]
        dreal = step * s0r
        dimag = -step * s0i
        ddecay = -step * step * decay * (real * s1r - imag * s1i)
        dfreq = -step * step * (real * s1i + imag * s1r)
        dreal_ref[0, direction] = dreal
        dimag_ref[0, direction] = dimag
        ddecay_ref[0, direction] = ddecay
        dfreq_ref[0, direction] = dfreq
        dstep_ref[0, direction:direction + 1, :] = jnp.sum(
            real * dreal + imag * dimag + ddecay + freq * dfreq, axis=0, keepdims=True
        )


def s4_pullback(section, lengths, grads, log_step, log_decay, frequency, coef_real, coef_imag, earlier, after=()):
    states, channels = log_decay.shape[2], log_decay.shape[3]
    whole = pl.BlockSpec((1, 2, states, channels), lambda i: (section, 0, 0, 0))
    row = pl.BlockSpec((1, 2, channels), lambda i: (section, 0, 0))
    tiles = 2 * channels // lane
    held = [*earlier, *after]
    return pl.pallas_call(
        partial(pull_body, section, lengths, len(held)),
        grid=(1,),
        in_specs=[pl.BlockSpec((channels, 2 * lane), lambda i: (0, 0)), row, whole, whole, whole, whole] + [any_spec()] * len(held),
        out_specs=[row, whole, whole, whole, whole, pl.BlockSpec((16, channels), lambda i: (0, 0))],
        out_shape=[struct(log_step.shape, f32)] + [struct(log_decay.shape, f32)] * 4 + [struct((16, channels), f32)],
        scratch_shapes=[
            pltpu.VMEM((2 * channels, lane), f32),
            pltpu.VMEM((tiles, lane, 8, lane), f32),
            pltpu.VMEM((2 * ahead, tiles, states // 2, lane), f32),
            pltpu.VMEM((4, tiles, states // 2, lane), f32),
        ],
        input_output_aliases={6 + k: k for k in range(len(earlier))},
        name="s4_pullback",
        **params(50_000_000, 1_000_000),
    )(grads, log_step, log_decay, frequency, coef_real, coef_imag, *held)


pad = 8


def lane_tiles(value):
    return [value[:, at:at + lane] for at in range(0, value.shape[1], lane)]


def load_tiles(value, ref, first):
    for index, part in enumerate(lane_tiles(value)):
        ref[index, first:first + part.shape[0], :] = part


def width_conv(canvas, sign, signal_ref, kernel_ref, age_ref, reach_ref, out_ref):
    tiles, width = out_ref.shape[0], out_ref.shape[1]
    per = band // 8
    for index in range(width // band):
        ages = [age_ref[canvas, pl.ds((index * per + k) * 8, 8), :] for k in range(per)]

        def body(q, sums):
            sums = list(sums)
            places = [
                pl.multiple_of(jnp.clip(index * per + k - sign * q, 0, width // 8 - 1) * 8, 8) for k in range(per)
            ]
            for s in range(ahead):
                lag = q * ahead + s
                seen = [ages[k] >= lag for k in range(per)]
                for t in range(tiles):
                    value = jnp.broadcast_to(kernel_ref[t, pl.ds(lag, 1), :], (8, lane))
                    for k in range(per):
                        x = signal_ref[t, pl.ds(places[k] + (pad - sign * s), 8), :]
                        sums[k * tiles + t] += value * jnp.where(seen[k], x, 0.0)
            return tuple(sums)

        zero = jnp.zeros((8, lane), f32)
        sums = lax.fori_loop(0, reach_ref[canvas, index], body, (zero,) * (per * tiles))
        for k in range(per):
            for t in range(tiles):
                out_ref[t, pl.ds((index * per + k) * 8, 8), :] = sums[k * tiles + t]


def width_products(canvas, signal_ref, grad_ref, age_ref, reach_ref, total_ref):
    tiles, width = grad_ref.shape[0], grad_ref.shape[1]
    per = band // 8
    for index in range(width // band):
        ages = [age_ref[canvas, pl.ds((index * per + k) * 8, 8), :] for k in range(per)]
        grads = [[grad_ref[t, pl.ds((index * per + k) * 8, 8), :] for t in range(tiles)] for k in range(per)]

        def body(q, carry):
            places = [
                pl.multiple_of(jnp.clip(index * per + k - q, 0, width // 8 - 1) * 8, 8) for k in range(per)
            ]
            for s in range(ahead):
                lag = q * ahead + s
                seen = [ages[k] >= lag for k in range(per)]
                for t in range(tiles):
                    total = total_ref[t, lag]
                    for k in range(per):
                        x = signal_ref[t, pl.ds(places[k] + (pad - s), 8), :]
                        total += grads[k][t] * jnp.where(seen[k], x, 0.0)
                    total_ref[t, lag] = total
            return carry

        lax.fori_loop(0, reach_ref[canvas, index], body, 0)


def stacked_rows(ref, canvas):
    picture = ref[canvas].astype(f32)
    return jnp.transpose(picture.reshape(-1, picture.shape[2]))


def unstacked(ref, rows):
    flat = jnp.concatenate([jnp.transpose(ref[t]) for t in range(ref.shape[0])], axis=0)
    return flat.reshape(rows, flat.shape[0] // rows, flat.shape[1])


def width_scratch(rows, channels):
    tiles = rows * channels // lane
    return [
        pltpu.VMEM((tiles, lane + 2 * pad, lane), f32),
        pltpu.VMEM((tiles, lane, lane), f32),
        pltpu.VMEM((tiles, lane, lane), f32),
    ]


def convolve_canvas(canvas, sign, picture_ref, age_ref, reach_ref, signal_ref, kernel_ref, sum_ref):
    load_tiles(stacked_rows(picture_ref, canvas), signal_ref, pad)
    width_conv(canvas, sign, signal_ref, kernel_ref, age_ref, reach_ref, sum_ref)
    return unstacked(sum_ref, picture_ref.shape[1])


def wide_forward_body(packed, reach_ref, picture_ref, wide_ref, age_ref, out_ref, signal_ref, kernel_ref, sum_ref, *held):
    load_tiles(wide_ref[...], kernel_ref, 0)
    across_ref = held[0] if packed else out_ref
    for canvas in range(picture_ref.shape[0]):
        across_ref[canvas] = convolve_canvas(
            canvas, 1, picture_ref, age_ref, reach_ref, signal_ref, kernel_ref, sum_ref
        ).astype(across_ref.dtype)
    if packed:
        pieces_from_rows(lambda b, r, c: across_ref[b, r, c, :], out_ref, 0)
        pieces_from_rows(lambda b, r, c: picture_ref[b, r, c, :].astype(f32), out_ref, 1)


def wide_forward(packed, picture, wide, age, reach):
    out = piece_shape(2) if packed else struct(picture.shape, bf16)
    scratch = width_scratch(picture.shape[1], picture.shape[2])
    return launch(
        partial(wide_forward_body, packed), "wide_forward", [picture, wide, age], [out],
        scratch + [pltpu.VMEM(picture.shape, f32)] * packed, scalars=[reach],
    )[0]


def split_refs(packed, refs, held):
    return (refs[0], refs[1:]) if packed else (refs[:held], refs[held:])


def wide_mixed_body(packed, reach_ref, *refs):
    if packed:
        pieces, wide_ref, age_ref, pack_ref, out_ref, tall_ref, stream_ref, signal_ref, kernel_ref, sum_ref = refs
        for kind, ref in enumerate((tall_ref, stream_ref)):
            def put(b, r, c, value, ref=ref):
                ref[b, r, c, :] = value.astype(bf16)
            rows_from_pieces(pieces, kind, put)
    else:
        tall_ref, stream_ref, wide_ref, age_ref, pack_ref, out_ref, signal_ref, kernel_ref, sum_ref = refs
    rows = tall_ref.shape[1]
    skip = pack_ref[:, 0:1]
    load_tiles(wide_ref[...], kernel_ref, 0)
    for canvas in range(tall_ref.shape[0]):
        mixer = convolve_canvas(canvas, 1, tall_ref, age_ref, reach_ref, signal_ref, kernel_ref, sum_ref)
        for row in range(rows):
            at = (canvas * rows + row) * lane
            out_ref[:, at:at + lane] = (
                mixer[row] + skip * stream_ref[canvas, row].astype(f32)
            ).astype(bf16)


def wide_mixed(packed, moved, picture, wide, age, reach, pack):
    canvases, rows, channels, width = picture
    outs = [struct((channels, canvases * rows * lane), bf16)] + [struct(picture, bf16)] * (2 * packed)
    got = launch(
        partial(wide_mixed_body, packed), "wide_mixed", [*moved, wide, age, pack], outs,
        width_scratch(rows, channels), scalars=[reach],
    )
    return tuple(got) if packed else (got[0], *moved)


def norm_backward(grads, mixed_ref, stats_ref, pack_ref, channels_all):
    channels = mixed_ref.shape[0]
    keep, near, far = grads
    total = keep[...].astype(f32) + near[...].astype(f32) + far[...].astype(f32)
    normed_grad = total[0:channels]
    scaled_mean = total[channels:channels + 1] / channels_all
    paired_mean = total[channels + 1:channels + 2] / channels_all
    average, inverse = stats_ref[0:1, :], stats_ref[1:2, :]
    centred = (mixed_ref[...].astype(f32) - average) * inverse
    gain = pack_ref[:, 1:2]
    mixed_grad = inverse * (normed_grad * gain - scaled_mean - centred * paired_mean)
    return (
        mixed_grad,
        jnp.sum(normed_grad * centred, axis=1, keepdims=True),
        jnp.sum(normed_grad, axis=1, keepdims=True),
    )


def put_columns(ref, columns):
    places = lax.broadcasted_iota(jnp.int32, ref.shape, 1)
    value = jnp.zeros(ref.shape, f32)
    for index, column in enumerate(columns):
        value = jnp.where(places == index, column, value)
    ref[...] = value


def wide_norm_back_body(packed, channels_all, reach_ref, keep_ref, near_ref, far_ref, mixed_ref, stats_ref, pack_ref,
                        stream_ref, cotangent_ref, wide_ref, fore_ref, *refs):
    if packed:
        out_ref, grad_ref, sums_ref, signal_ref, kernel_ref, sum_ref, conv_ref, rest_ref = refs
    else:
        conv_ref, rest_ref, grad_ref, sums_ref, signal_ref, kernel_ref, sum_ref = refs
    canvases, rows = conv_ref.shape[0], conv_ref.shape[1]
    mixed_grad, gain_grad, shift_grad = norm_backward(
        (keep_ref, near_ref, far_ref), mixed_ref, stats_ref, pack_ref, channels_all
    )
    skip = pack_ref[:, 0:1]
    skip_grad = jnp.zeros_like(gain_grad)
    load_tiles(wide_ref[...], kernel_ref, 0)
    for canvas in range(canvases):
        for row in range(rows):
            at = (canvas * rows + row) * lane
            part = mixed_grad[:, at:at + lane]
            grad_ref[canvas, row] = part.astype(bf16)
            skip_grad += jnp.sum(part * stream_ref[canvas, row].astype(f32), axis=1, keepdims=True)
            rest_ref[canvas, row] = (cotangent_ref[canvas, row].astype(f32) + skip * part).astype(rest_ref.dtype)
        conv_ref[canvas] = convolve_canvas(
            canvas, -1, grad_ref, fore_ref, reach_ref, signal_ref, kernel_ref, sum_ref
        ).astype(conv_ref.dtype)
    put_columns(sums_ref, [skip_grad, gain_grad, shift_grad])
    if packed:
        pieces_from_rows(lambda b, r, c: conv_ref[b, r, c, :], out_ref, 0)
        pieces_from_rows(lambda b, r, c: rest_ref[b, r, c, :], out_ref, 1)


def wide_norm_back(packed, channels_all, grads, mixed, stats, pack, stream, cotangent, wide, fore, reach, after):
    plain = struct(stream.shape, bf16)
    sums = struct((stream.shape[2], lane), f32)
    got = launch(
        partial(wide_norm_back_body, packed, channels_all), "wide_norm_back",
        [*grads, mixed, stats, pack, stream, cotangent, wide, fore],
        [piece_shape(2), plain, sums] if packed else [plain, plain, plain, sums],
        width_scratch(stream.shape[1], stream.shape[2]) + [pltpu.VMEM(stream.shape, f32)] * (2 * packed),
        scalars=[reach], after=after,
    )
    return got[:-2], got[-2], got[-1]


def wide_back_body(packed, reach_ref, *refs):
    if packed:
        pieces, wide_ref, fore_ref, out_ref, grad_ref, signal_ref, kernel_ref, sum_ref, rest_ref = refs

        def put_grad(b, r, c, value):
            grad_ref[b, r, c, :] = value.astype(bf16)

        def put_rest(b, r, c, value):
            rest_ref[b, r, c, :] = value

        rows_from_pieces(pieces, 0, put_grad)
        rows_from_pieces(pieces, 1, put_rest)
    else:
        grad_ref, rest_ref, wide_ref, fore_ref, out_ref, signal_ref, kernel_ref, sum_ref = refs
    load_tiles(wide_ref[...], kernel_ref, 0)
    for canvas in range(grad_ref.shape[0]):
        value = convolve_canvas(canvas, -1, grad_ref, fore_ref, reach_ref, signal_ref, kernel_ref, sum_ref)
        out_ref[canvas] = (value + rest_ref[canvas].astype(f32)).astype(bf16)


def wide_back(packed, moved, picture, wide, fore, reach, after):
    plain = struct(picture, bf16)
    got = launch(
        partial(wide_back_body, packed), "wide_back", [*moved, wide, fore], [plain] * (1 + packed),
        width_scratch(picture[1], picture[2]) + [pltpu.VMEM(picture, f32)] * packed, scalars=[reach], after=after,
    )
    return (got[0], got[1] if packed else moved[0])


def wide_kernel_grad_body(reach_ref, grad_ref, input_ref, age_ref, out_ref, signal_ref, flat_ref, sum_ref, total_ref):
    channels = grad_ref.shape[2]
    rows = grad_ref.shape[1]
    total_ref[...] = jnp.zeros(total_ref.shape, f32)
    for canvas in range(grad_ref.shape[0]):
        load_tiles(stacked_rows(input_ref, canvas), signal_ref, pad)
        load_tiles(stacked_rows(grad_ref, canvas), flat_ref, 0)
        width_products(canvas, signal_ref, flat_ref, age_ref, reach_ref, total_ref)

    def reduce(index, carry):
        at = pl.multiple_of(index * 8, 8)
        for t in range(sum_ref.shape[0]):
            sum_ref[t, pl.ds(at, 8), :] = jnp.sum(total_ref[t, pl.ds(at, 8)], axis=1)
        return carry

    lax.fori_loop(0, lane // 8, reduce, 0)
    picture = unstacked(sum_ref, rows)
    out_ref[...] = sum(picture[row] for row in range(rows))


def wide_kernel_grad(grad, inputs, age, reach, after=()):
    channels = grad.shape[2]
    return launch(
        wide_kernel_grad_body, "wide_kernel_grad", [grad, inputs, age], [struct((channels, lane), f32)],
        width_scratch(grad.shape[1], channels) + [pltpu.VMEM((grad.shape[1] * channels // lane, lane, 8, lane), f32)],
        scalars=[reach], after=after,
    )[0]


def height_loop(count, body, carry):
    if count <= 16:
        for lag in range(count):
            carry = body(lag, carry)
        return carry
    return lax.fori_loop(0, count, body, carry)


def tap(kernel, lag):
    if isinstance(lag, int):
        return kernel[:, lag:lag + 1]
    places = lax.broadcasted_iota(jnp.int32, kernel.shape, 1)
    return jnp.sum(jnp.where(places == lag, kernel, 0.0), axis=1, keepdims=True)


def moved_by(value, shift):
    size = value.shape[1]
    if not isinstance(shift, int):
        return pltpu.roll(value, lax.rem(shift + size, size), 1)
    shift %= size
    return pltpu.roll(value, shift, 1) if shift else value


def height_conv(get, put, channels, kernel_ref, age_ref, sign, height):
    for at in range(0, channels, strip):
        rows = slice(at, at + strip)
        kernel = kernel_ref[rows, :]
        for canvas in range(age_ref.shape[0]):
            value, age = get(rows, canvas), age_ref[canvas]
            columns = value.shape[1] // height

            def body(lag, total):
                return total + tap(kernel, lag) * jnp.where(age >= lag, moved_by(value, sign * lag * columns), 0.0)

            put(rows, canvas, height_loop(height, body, jnp.zeros_like(value)))


def height_products(grads, values, ages, height):
    columns = values[0].shape[1] // height
    channels = values[0].shape[0]
    places = lax.broadcasted_iota(jnp.int32, (channels, lane), 1)

    def body(lag, total):
        part = None
        for grad, value, age in zip(grads, values, ages, strict=True):
            product = grad * jnp.where(age >= lag, moved_by(value, lag * columns), 0.0)
            for piece in lane_tiles(product):
                part = piece if part is None else part + piece
        return total + jnp.where(places == lag, jnp.sum(part, axis=1, keepdims=True), 0.0)

    return height_loop(height, body, jnp.zeros((channels, lane), f32))


def canvas_cut(ref, canvas, canvases):
    each = ref.shape[1] // canvases
    return slice(canvas * each, (canvas + 1) * each)


def tall_mixed_body(packed, height, *refs):
    if packed:
        pieces, kernel_ref, age_ref, pack_ref, out_ref, across_ref, stream_ref = refs
        cols_from_pieces(pieces, 0, across_ref)
        cols_from_pieces(pieces, 1, stream_ref)
    else:
        across_ref, stream_ref, kernel_ref, age_ref, pack_ref, out_ref = refs
    canvases = age_ref.shape[0]

    def get(rows, canvas):
        return across_ref[rows, canvas_cut(across_ref, canvas, canvases)].astype(f32)

    def put(rows, canvas, mixer):
        cut = canvas_cut(across_ref, canvas, canvases)
        out_ref[rows, cut] = (mixer + pack_ref[rows, 0:1] * stream_ref[rows, cut].astype(f32)).astype(bf16)

    height_conv(get, put, out_ref.shape[0], kernel_ref, age_ref, 1, height)


def tall_mixed(packed, height, moved, cols, kernel, age, pack):
    got = launch(
        partial(tall_mixed_body, packed, height), "tall_mixed", [*moved, kernel, age, pack],
        [struct(cols, bf16)] * (1 + 2 * packed),
    )
    return tuple(got) if packed else (got[0], *moved)


def tall_next_body(packed, height, keep_ref, near_ref, far_ref, stream_ref, pack_ref, kernel_ref, age_ref,
                   next_ref, branch_ref, out_ref, *held):
    canvases = age_ref.shape[0]
    conv_ref = held[0] if packed else out_ref

    def get(rows, canvas):
        cut = canvas_cut(stream_ref, canvas, canvases)
        branch = (
            keep_ref[rows, cut].astype(f32) + near_ref[rows, cut].astype(f32) + far_ref[rows, cut].astype(f32)
            + pack_ref[rows, 3:4]
        )
        branch_ref[rows, cut] = branch
        low = (stream_ref[rows, cut].astype(f32) + pack_ref[rows, 4:5] * branch).astype(bf16)
        next_ref[rows, cut] = low
        return low.astype(f32)

    def put(rows, canvas, value):
        conv_ref[rows, canvas_cut(stream_ref, canvas, canvases)] = value.astype(conv_ref.dtype)

    height_conv(get, put, stream_ref.shape[0], kernel_ref, age_ref, 1, height)
    if packed:
        pieces_from_cols(lambda rows, cut: conv_ref[rows, cut], out_ref, 0)
        pieces_from_cols(lambda rows, cut: next_ref[rows, cut].astype(f32), out_ref, 1)


def tall_next(packed, height, branches, stream, pack, kernel, age):
    got = launch(
        partial(tall_next_body, packed, height), "tall_next", [*branches, stream, pack, kernel, age],
        [struct(stream.shape, bf16), struct(stream.shape, f32), piece_shape(2) if packed else struct(stream.shape, bf16)],
        [pltpu.VMEM(stream.shape, f32)] * packed,
    )
    return got[0], got[1], [got[2]] if packed else [got[2], got[0]]


def tall_back_body(packed, height, *refs):
    if packed:
        pieces, kernel_ref, fore_ref, pack_ref, branch_ref, grad_ref, low_ref, sums_ref, conv_ref, rest_ref = refs
        cols_from_pieces(pieces, 0, conv_ref)
        cols_from_pieces(pieces, 1, rest_ref)
    else:
        conv_ref, rest_ref, kernel_ref, fore_ref, pack_ref, branch_ref, grad_ref, low_ref, sums_ref = refs
    canvases = fore_ref.shape[0]

    def get(rows, canvas):
        return conv_ref[rows, canvas_cut(conv_ref, canvas, canvases)].astype(f32)

    def put(rows, canvas, value):
        cut = canvas_cut(conv_ref, canvas, canvases)
        grad = rest_ref[rows, cut].astype(f32) + value
        grad_ref[rows, cut] = grad
        low_ref[rows, cut] = (grad * pack_ref[rows, 4:5]).astype(bf16)

    height_conv(get, put, conv_ref.shape[0], kernel_ref, fore_ref, -1, height)
    sums_ref[...] = jnp.zeros(sums_ref.shape, f32)


def tall_back(packed, height, moved, cols, kernel, fore, pack, branch, after):
    got = launch(
        partial(tall_back_body, packed, height), "tall_back", [*moved, kernel, fore, pack, branch],
        [struct(cols, f32), struct(cols, bf16), struct((cols[0], lane), f32)] + [struct(cols, bf16)] * packed,
        [pltpu.VMEM(cols, f32)] * packed, after=after,
    )
    return got[0], got[1], got[3] if packed else moved[0]


def branch_sums_body(grad_ref, branch_ref, pack_ref, bias_ref, scale_ref):
    grad = grad_ref[...]
    put_columns(bias_ref, [jnp.sum(grad * pack_ref[:, 4:5], axis=1, keepdims=True)])
    put_columns(scale_ref, [jnp.sum(grad * branch_ref[...], axis=1, keepdims=True)])


def branch_sums(grad, branch, pack, after):
    return launch(branch_sums_body, "branch_sums", [grad, branch, pack], [struct((grad.shape[0], lane), f32)] * 2, after=after)


def tall_norm_back_body(packed, height, channels_all, keep_ref, near_ref, far_ref, mixed_ref, stats_ref, pack_ref, stream_ref,
                        grad_ref, kernel_ref, fore_ref, *refs):
    if packed:
        out_ref, low_ref, sums_ref, conv_ref, rest_ref = refs
    else:
        conv_ref, rest_ref, low_ref, sums_ref = refs
    canvases = fore_ref.shape[0]
    mixed_grad, gain_grad, shift_grad = norm_backward(
        (keep_ref, near_ref, far_ref), mixed_ref, stats_ref, pack_ref, channels_all
    )
    low_ref[...] = mixed_grad.astype(bf16)
    rest_ref[...] = (grad_ref[...] + pack_ref[:, 0:1] * mixed_grad).astype(rest_ref.dtype)
    skip_grad = jnp.sum(mixed_grad * stream_ref[...].astype(f32), axis=1, keepdims=True)

    def get(rows, canvas):
        return low_ref[rows, canvas_cut(low_ref, canvas, canvases)].astype(f32)

    def put(rows, canvas, value):
        conv_ref[rows, canvas_cut(low_ref, canvas, canvases)] = value.astype(conv_ref.dtype)

    height_conv(get, put, low_ref.shape[0], kernel_ref, fore_ref, -1, height)
    put_columns(sums_ref, [skip_grad, gain_grad, shift_grad])
    if packed:
        pieces_from_cols(lambda rows, cut: conv_ref[rows, cut], out_ref, 0)
        pieces_from_cols(lambda rows, cut: rest_ref[rows, cut], out_ref, 1)


def tall_norm_back(packed, height, channels_all, grads, mixed, stats, pack, stream, grad, kernel, fore, after):
    plain, sums = struct(mixed.shape, bf16), struct((mixed.shape[0], lane), f32)
    got = launch(
        partial(tall_norm_back_body, packed, height, channels_all), "tall_norm_back",
        [*grads, mixed, stats, pack, stream, grad, kernel, fore],
        [piece_shape(2), plain, sums] if packed else [plain, plain, plain, sums],
        [pltpu.VMEM(mixed.shape, f32)] * (2 * packed), after=after,
    )
    return got[:-2], got[-2], got[-1]


def tall_kernel_grad_body(height, grad_ref, input_ref, age_ref, out_ref):
    canvases = age_ref.shape[0]
    for at in range(0, out_ref.shape[0], strip):
        rows = slice(at, at + strip)
        cuts = [canvas_cut(grad_ref, canvas, canvases) for canvas in range(canvases)]
        out_ref[rows, :] = height_products(
            [grad_ref[rows, cut].astype(f32) for cut in cuts], [input_ref[rows, cut].astype(f32) for cut in cuts],
            [age_ref[canvas] for canvas in range(canvases)], height,
        )


def tall_kernel_grad(height, grad, inputs, age, after=()):
    return launch(
        partial(tall_kernel_grad_body, height), "tall_kernel_grad", [grad, inputs, age],
        [struct((grad.shape[0], lane), f32)], after=after,
    )[0]


root = 0.7978845608028654
cubic = 0.044715


def gather_into(me_ref, parts, whole_ref):
    me = me_ref[0]
    for flip, part in enumerate(parts):
        whole_ref[me ^ flip] = part[...]


def scatter_out(me_ref, whole_ref, outs):
    me = me_ref[0]
    for flip, out in zip((3, 1, 2, 0), outs, strict=True):
        out[...] = whole_ref[me ^ flip]


def gather_shape(me_ref, parts, section, shape_ref):
    gather_into(me_ref, parts, shape_ref)
    every = shape_ref[...].reshape(-1, shape_ref.shape[2])
    return every[:, 2 * section:2 * section + 1], every[:, 2 * section + 1:2 * section + 2]


def mlp_forward(me_ref, parts, full_ref, shape, weight_in_ref, bias_ref, normed_ref, hidden_ref, slope_ref, stats_ref):
    gather_into(me_ref, parts, full_ref)
    mixed = full_ref[...].astype(f32).reshape(-1, full_ref.shape[2])
    average = jnp.mean(mixed, axis=0, keepdims=True)
    moved = mixed - average
    inverse = lax.rsqrt(jnp.mean(moved * moved, axis=0, keepdims=True) + epsilon)
    centred = moved * inverse
    stats_ref[0:1, :] = average
    stats_ref[1:2, :] = inverse
    normed = (centred * shape[0] + shape[1]).astype(bf16)
    normed_ref[...] = normed
    before = dot(weight_in_ref[0], normed, 0, 0) + bias_ref[...]
    square = before * before
    bend = jnp.tanh(root * before * (1.0 + cubic * square))
    half = 0.5 * (1.0 + bend)
    hidden_ref[...] = (before * half).astype(bf16)
    slope_ref[...] = (half + 0.5 * before * (1.0 - bend * bend) * root * (1.0 + 3.0 * cubic * square)).astype(slope_ref.dtype)
    return centred


def mlp_first_body(section, me_ref, own, near, far, cross, shape_own, shape_near, shape_far, shape_cross, weight_in_ref,
                   bias_ref, weight_out_ref,
                   send_far, send_own, keep_far, keep_own, normed_ref, hidden_ref, slope_ref, stats_ref, full_ref, sum_ref,
                   shape_ref):
    shape = gather_shape(me_ref, (shape_own, shape_near, shape_far, shape_cross), section, shape_ref)
    mlp_forward(me_ref, (own, near, far, cross), full_ref, shape, weight_in_ref, bias_ref,
                normed_ref, hidden_ref, slope_ref, stats_ref)
    partial_out = dot(weight_out_ref[0], hidden_ref[...], 0, 0)
    sum_ref[...] = partial_out.astype(bf16).reshape(sum_ref.shape)
    scatter_out(me_ref, sum_ref, (send_far, send_own, keep_far, keep_own))


def mlp_backward(me_ref, parts, full_ref, weight_out_ref, weight_in_ref, slope, gain, centred, sum_ref, outs, before_grad_ref):
    gather_into(me_ref, parts, full_ref)
    grad = full_ref[...].reshape(-1, full_ref.shape[2])
    before_grad = (dot(weight_out_ref[0], grad, 1, 0) * slope).astype(bf16)
    before_grad_ref[...] = before_grad
    normed_part = dot(weight_in_ref[0], before_grad, 1, 0)
    channels = sum_ref.shape[1] - 16
    scaled = normed_part * gain
    scaled_sum = jnp.sum(scaled, axis=0, keepdims=True)
    paired_sum = jnp.sum(scaled * centred, axis=0, keepdims=True)
    places = lax.broadcasted_iota(jnp.int32, (16, grad.shape[1]), 0)
    tail = jnp.where(places == 0, scaled_sum, jnp.where(places == 1, paired_sum, 0.0)).astype(bf16)
    for index in range(sum_ref.shape[0]):
        sum_ref[index, 0:channels, :] = normed_part[index * channels:(index + 1) * channels].astype(bf16)
        sum_ref[index, channels:, :] = tail
    scatter_out(me_ref, sum_ref, outs)


def mlp_top_body(section, me_ref, own, near, far, cross, grad_own, grad_near, grad_far, grad_cross,
                 shape_own, shape_near, shape_far, shape_cross, weight_in_ref, bias_ref, weight_out_ref,
                 back_sf, back_so, back_kf, back_ko, stats_ref, normed_ref, hidden_ref, before_grad_ref,
                 full_ref, back_ref, slope_ref, shape_ref):
    shape = gather_shape(me_ref, (shape_own, shape_near, shape_far, shape_cross), section, shape_ref)
    centred = mlp_forward(me_ref, (own, near, far, cross), full_ref, shape, weight_in_ref, bias_ref,
                          normed_ref, hidden_ref, slope_ref, stats_ref)
    mlp_backward(me_ref, (grad_own, grad_near, grad_far, grad_cross), full_ref, weight_out_ref, weight_in_ref,
                 slope_ref[...], shape[0], centred, back_ref, (back_sf, back_so, back_kf, back_ko), before_grad_ref)


def mlp_back_body(section, me_ref, own, near, far, cross, grad_own, grad_near, grad_far, grad_cross,
                  shape_own, shape_near, shape_far, shape_cross, weight_in_ref, weight_out_ref, slope_ref, stats_ref,
                  back_sf, back_so, back_kf, back_ko, before_grad_ref, full_ref, back_ref, shape_ref):
    shape = gather_shape(me_ref, (shape_own, shape_near, shape_far, shape_cross), section, shape_ref)
    gather_into(me_ref, (own, near, far, cross), full_ref)
    centred = (full_ref[...].astype(f32).reshape(-1, full_ref.shape[2]) - stats_ref[0:1, :]) * stats_ref[1:2, :]
    mlp_backward(me_ref, (grad_own, grad_near, grad_far, grad_cross), full_ref, weight_out_ref, weight_in_ref,
                 slope_ref[...].astype(f32), shape[0], centred, back_ref, (back_sf, back_so, back_kf, back_ko), before_grad_ref)


tile = 256


def pixel_block(rows):
    return pl.BlockSpec((rows, tile), lambda i: (0, i))


def fixed_block(shape):
    return pl.BlockSpec(shape, lambda i: (0,) * len(shape))


def section_block(section, shape):
    return pl.BlockSpec((1,) + shape, lambda i: (section, 0, 0))


def mlp_first(section, me, parts, shaping, weight_in, bias, weight_out):
    own = parts[0]
    channels, pixels = own.shape
    wide, units = weight_in.shape[1], weight_in.shape[2]
    piece = pixel_block(channels)
    return pl.pallas_call(
        partial(mlp_first_body, section),
        grid=(pixels // tile,),
        in_specs=[smem_spec()] + [piece] * 4 + [
            *[fixed_block(shaping[0].shape)] * 4, section_block(section, (wide, units)), fixed_block(bias.shape),
            section_block(section, (units, wide)),
        ],
        out_specs=[piece] * 4 + [pixel_block(wide), pixel_block(units), pixel_block(units), pixel_block(8)],
        out_shape=[struct(own.shape, bf16)] * 4 + [
            struct((wide, pixels), bf16), struct((units, pixels), bf16), struct((units, pixels), bf16), struct((8, pixels), f32),
        ],
        scratch_shapes=[
            pltpu.VMEM((4, channels, tile), bf16), pltpu.VMEM((4, channels, tile), bf16), pltpu.VMEM((4,) + shaping[0].shape, f32),
        ],
        name="mlp_first",
        **params(10_000_000, 1_000_000),
    )(me, *parts, *shaping, weight_in, bias, weight_out)


def mlp_top(section, me, parts, grads, shaping, weight_in, bias, weight_out):
    own = parts[0]
    channels, pixels = own.shape
    wide, units = weight_in.shape[1], weight_in.shape[2]
    piece, back = pixel_block(channels), pixel_block(channels + 16)
    return pl.pallas_call(
        partial(mlp_top_body, section),
        grid=(pixels // tile,),
        in_specs=[smem_spec()] + [piece] * 8 + [
            *[fixed_block(shaping[0].shape)] * 4, section_block(section, (wide, units)), fixed_block(bias.shape),
            section_block(section, (units, wide)),
        ],
        out_specs=[back] * 4 + [pixel_block(8), pixel_block(wide), pixel_block(units), pixel_block(units)],
        out_shape=[struct((channels + 16, pixels), bf16)] * 4 + [
            struct((8, pixels), f32), struct((wide, pixels), bf16), struct((units, pixels), bf16), struct((units, pixels), bf16),
        ],
        scratch_shapes=[
            pltpu.VMEM((4, channels, tile), bf16), pltpu.VMEM((4, channels + 16, tile), bf16),
            pltpu.VMEM((units, tile), f32), pltpu.VMEM((4,) + shaping[0].shape, f32),
        ],
        name="mlp_top",
        **params(10_000_000, 1_000_000),
    )(me, *parts, *grads, *shaping, weight_in, bias, weight_out)


def mlp_back(section, me, parts, grads, shaping, weight_in, weight_out, slope, stats):
    own = parts[0]
    channels, pixels = own.shape
    wide, units = weight_in.shape[1], weight_in.shape[2]
    piece, back = pixel_block(channels), pixel_block(channels + 16)
    return pl.pallas_call(
        partial(mlp_back_body, section),
        grid=(pixels // tile,),
        in_specs=[smem_spec()] + [piece] * 8 + [
            *[fixed_block(shaping[0].shape)] * 4, section_block(section, (wide, units)), section_block(section, (units, wide)),
            pixel_block(units), pixel_block(8),
        ],
        out_specs=[back] * 4 + [pixel_block(units)],
        out_shape=[struct((channels + 16, pixels), bf16)] * 4 + [struct((units, pixels), bf16)],
        scratch_shapes=[
            pltpu.VMEM((4, channels, tile), bf16), pltpu.VMEM((4, channels + 16, tile), bf16),
            pltpu.VMEM((4,) + shaping[0].shape, f32),
        ],
        name="mlp_back",
        **params(10_000_000, 1_000_000),
    )(me, *parts, *grads, *shaping, weight_in, weight_out, slope, stats)


def mlp_out_body(me_ref, hidden_ref, weight_out_ref, send_far, send_own, keep_far, keep_own, sum_ref):
    sum_ref[...] = dot(weight_out_ref[0], hidden_ref[...], 0, 0).astype(bf16).reshape(sum_ref.shape)
    scatter_out(me_ref, sum_ref, (send_far, send_own, keep_far, keep_own))


def mlp_out(section, me, hidden, weight_out, after):
    units, wide = weight_out.shape[1:]
    pixels = hidden.shape[1]
    channels = wide // 4
    piece = pixel_block(channels)

    def body(me_ref, hidden_ref, weight_out_ref, *refs):
        mlp_out_body(me_ref, hidden_ref, weight_out_ref, *refs[len(after):])

    return pl.pallas_call(
        body,
        grid=(pixels // tile,),
        in_specs=[smem_spec(), pixel_block(units), section_block(section, (units, wide))] + [any_spec()] * len(after),
        out_specs=[piece] * 4,
        out_shape=[struct((channels, pixels), bf16)] * 4,
        scratch_shapes=[pltpu.VMEM((4, channels, tile), bf16)],
        name="mlp_out",
        **params(10_000_000, 1_000_000),
    )(me, hidden, weight_out, *after)


def put_halves(me_ref, total, outs):
    if len(outs) == 1:
        outs[0][...] = total[...].astype(bf16)
        return
    part = outs[0].shape[0]
    mine = lax.rem(me_ref[1], 2)

    @pl.when(mine == 0)
    def _():
        outs[0][...] = total[:part].astype(bf16)
        outs[1][...] = total[part:].astype(bf16)

    @pl.when(mine == 1)
    def _():
        outs[0][...] = total[part:].astype(bf16)
        outs[1][...] = total[:part].astype(bf16)


def out_grad_body(me_ref, hidden_ref, grad_own, grad_near, grad_far, grad_cross, *refs):
    *outs, full_ref, total_ref = refs
    gather_into(me_ref, (grad_own, grad_near, grad_far, grad_cross), full_ref)
    total_ref[...] = dot(hidden_ref[...], full_ref[...].reshape(-1, full_ref.shape[2]), 1, 1)
    put_halves(me_ref, total_ref, outs)


def halves_of(rows, columns, halves):
    return [struct((rows // 2, columns), bf16)] * 2 if halves else [struct((rows, columns), bf16)]


def out_grad(halves, me, hidden, grads, after=()):
    units = hidden.shape[0]
    wide = 4 * grads[0].shape[0]
    return launch(
        out_grad_body, "out_grad", [hidden, *grads], halves_of(units, wide, halves),
        [pltpu.VMEM((4,) + grads[0].shape, bf16), pltpu.VMEM((units, wide), f32)], scalars=[me], after=after,
    )


def in_grad_body(me_ref, normed_ref, before_grad_ref, *refs):
    *outs, bias_ref, total_ref = refs
    before_grad = before_grad_ref[...]
    total_ref[...] = dot(normed_ref[...], before_grad, 1, 1)
    put_halves(me_ref, total_ref, outs)
    bias_ref[...] = jnp.broadcast_to(jnp.sum(before_grad.astype(f32), axis=1, keepdims=True), bias_ref.shape)


def in_grad(halves, me, normed, before_grad, after=()):
    wide, units = normed.shape[0], before_grad.shape[0]
    return launch(
        in_grad_body, "in_grad", [normed, before_grad], halves_of(wide, units, halves) + [struct((units, lane), f32)],
        [pltpu.VMEM((wide, units), f32)], scalars=[me], after=after,
    )


def top_output_body(keep_ref, near_ref, far_ref, stream_ref, cotangent_ref, pack_ref, out_ref, sums_ref):
    bias, scale = pack_ref[:, 3:4], pack_ref[:, 4:5]
    total = jnp.zeros(scale.shape, f32)
    rows = stream_ref.shape[1]
    for canvas in range(stream_ref.shape[0]):
        for row in range(rows):
            at = (canvas * rows + row) * lane
            cut = slice(at, at + lane)
            branch = keep_ref[:, cut].astype(f32) + near_ref[:, cut].astype(f32) + far_ref[:, cut].astype(f32) + bias
            out_ref[canvas, row] = (stream_ref[canvas, row].astype(f32) + scale * branch).astype(bf16)
            total += jnp.sum(cotangent_ref[canvas, row].astype(f32) * branch, axis=1, keepdims=True)
    put_columns(sums_ref, [total])


def top_output(branches, stream, cotangent, pack, after):
    return launch(
        top_output_body, "top_output", [*branches, stream, cotangent, pack],
        [struct(stream.shape, bf16), struct((stream.shape[2], lane), f32)], after=after,
    )


core_pairs = [(i, i ^ 1) for i in range(4)]
chip_pairs = [(i, i ^ 2) for i in range(4)]


def gather_channels(own):
    far = lax.ppermute(own, "ch", chip_pairs)
    near = lax.ppermute(own, "ch", core_pairs)
    cross = lax.ppermute(far, "ch", core_pairs)
    return (own, near, far, cross)


def scatter_channels(send_far, send_own, keep_far, keep_own):
    near_far = lax.ppermute(send_far, "ch", core_pairs)
    near_own = lax.ppermute(send_own, "ch", core_pairs)
    onward = (keep_far.astype(f32) + near_far.astype(f32)).astype(bf16)
    far = lax.ppermute(onward, "ch", chip_pairs)
    return (keep_own, near_own, far)


def across_rows(value, flip):
    return lax.ppermute(value, "rows", [(i, i ^ flip) for i in range(8)])


def rows_sum(value):
    for flip in (1, 2, 4):
        value = value + across_rows(value, flip)
    return value


def collect_body(height, tall_ref, wide_ref, norm_ref, bias_ref, scale_ref, units_ref, out_ref):
    channels = tall_ref.shape[0]
    places = lax.broadcasted_iota(jnp.int32, tall_ref.shape, 1)
    held = jnp.where(places < height, tall_ref[...], 0.0)
    columns = [norm_ref[:, k:k + 1] for k in range(3)] + [bias_ref[:, 0:1], scale_ref[:, 0:1]]
    columns += [units_ref[at:at + channels, 0:1] for at in range(0, units_ref.shape[0], channels)]
    for index, column in enumerate(columns):
        held = jnp.where(places == height + index, column, held)
    out_ref[:, 0:lane] = wide_ref[...]
    out_ref[:, lane:] = held


def collect(height, *parts):
    return launch(partial(collect_body, height), "collect", parts, [struct((parts[0].shape[0], 2 * lane), f32)])[0]


def quarter_body(me_ref, keep_ref, near_ref, *outs):
    mine = me_ref[1] // 2
    part = outs[0].shape[0]
    for flip, out in enumerate(outs):
        cut = pl.ds(pl.multiple_of((mine ^ flip) * part, part), part)
        out[...] = (keep_ref[cut, :].astype(f32) + near_ref[cut, :].astype(f32)).astype(bf16)


def quarters(me, keep, near, after=()):
    shape = struct((keep.shape[0] // 4, keep.shape[1]), bf16)
    return launch(quarter_body, "quarters", [keep, near], [shape] * 4, scalars=[me], after=after)


def rows_sum_matrix(me, keep, near, after=()):
    own, *others = quarters(me, keep, near, after)
    total = own.astype(f32)
    for index, other in enumerate(others):
        total = total + across_rows(other, 2 * (index + 1)).astype(f32)
    total = total.astype(bf16)
    half = jnp.concatenate([total] + [across_rows(total, 2 * flip) for flip in (1, 2, 3)], axis=0)
    return half, across_rows(half, 1)


def assemble_body(me_ref, half_ref, other_ref, top_ref, out_ref):
    mine, group = lax.rem(me_ref[1], 2), me_ref[1] // 2
    size = half_ref.shape[0]
    part = size // 4
    for flip in range(4):
        for side, ref in ((mine, half_ref), (1 - mine, other_ref)):
            at = pl.multiple_of(side * size + (group ^ flip) * part, part)
            out_ref[0, pl.ds(at, part), :] = ref[flip * part:(flip + 1) * part, :].astype(f32)
    out_ref[1] = top_ref[...].astype(f32)


def assemble(me, half, other, top):
    return pl.pallas_call(
        assemble_body,
        in_specs=[smem_spec()] + [vmem_spec()] * 3,
        out_specs=vmem_spec(),
        out_shape=struct((2,) + top.shape, f32),
        name="assemble",
        **params(1_000_000, 7_000_000),
    )(me, half, other, top)


def exchange(pieces):
    return lax.all_to_all(pieces, "rows", split_axis=0, concat_axis=0, tiled=True)


def rows_to_cols(packed, moving, count, picture):
    if packed:
        return [exchange(moving[0])]
    canvases, rows, channels, width = picture
    pieces = []
    for part in moving:
        cut = part.reshape(canvases, rows, channels, count, width // count)
        pieces.append(cut.transpose(3, 2, 0, 1, 4).reshape(count, channels, -1))
    moved = exchange(jnp.stack(pieces, axis=1))
    moved = moved.reshape(count, len(moving), channels, canvases, rows, width // count)
    return [moved[:, k].transpose(1, 2, 0, 3, 4).reshape(channels, -1) for k in range(len(moving))]


def cols_to_rows(packed, moving, count, picture):
    if packed:
        return [exchange(moving[0])]
    canvases, rows, channels, width = picture
    pieces = []
    for part in moving:
        cut = part.reshape(channels, canvases, count, rows, width // count)
        pieces.append(cut.transpose(2, 0, 1, 3, 4).reshape(count, channels, -1))
    moved = exchange(jnp.stack(pieces, axis=1))
    moved = moved.reshape(count, len(moving), channels, canvases, rows, width // count)
    return [moved[:, k].transpose(2, 3, 1, 0, 4).reshape(picture) for k in range(len(moving))]


def crop_reach(starts):
    count = starts.shape[1]
    places = jnp.arange(count, dtype=jnp.int32)
    here, there = places[None, :, None], places[None, None, :]
    begins = starts[:, None, :] > 0
    first = jnp.max(jnp.where(begins & (there <= here), there, 0), axis=2)
    following = jnp.min(jnp.where(begins & (there > here), there, count), axis=2)
    return places[None, :] - first, following - 1 - places[None, :]


def band_turns(age):
    return jnp.max(age.reshape(age.shape[0], -1, band), axis=2) // ahead + 1


def on_device(
    count,
    pixels,
    row_starts,
    col_starts,
    log_step,
    log_decay,
    frequency,
    coef_real,
    coef_imag,
    skip_gain,
    norm_gain,
    norm_shift,
    weight_in,
    bias_in,
    weight_out,
    bias_out,
    layer_scale,
    cotangent,
):
    canvases, rows, width, channels = pixels.shape
    height = row_starts.shape[1]
    channels_all = weight_in.shape[1]
    lengths = (height, width)
    picture = (canvases, rows, channels, width)
    cols = (channels, canvases * height * (width // count))
    me = jnp.stack([lax.axis_index("ch"), lax.axis_index("rows")]).astype(jnp.int32)
    eight = count == 8
    packed = eight and picture == (2, 2, 2 * half_rows, lane)

    stream = jnp.swapaxes(pixels, 2, 3)
    upstream = jnp.swapaxes(cotangent, 2, 3)
    states = [jnp.swapaxes(value, 2, 3) for value in (log_decay, frequency, coef_real, coef_imag)]

    age, fore = crop_reach(col_starts)
    age_reach, fore_reach = band_turns(age), band_turns(fore)
    age = jnp.broadcast_to(age[:, :, None], (canvases, width, lane))
    fore = jnp.broadcast_to(fore[:, :, None], (canvases, width, lane))
    row_age, row_fore = crop_reach(row_starts)
    row_age = jnp.repeat(row_age, width // count, axis=1)[:, None, :]
    row_fore = jnp.repeat(row_fore, width // count, axis=1)[:, None, :]

    packs = [
        jnp.stack([skip_gain[k], norm_gain[k], norm_shift[k], bias_out[k], layer_scale[k]], axis=1) for k in range(2)
    ]
    shaping = gather_channels(jnp.stack([norm_gain[0], norm_shift[0], norm_gain[1], norm_shift[1]], axis=1))
    bias_columns = [bias_in[k][:, None] for k in range(2)]

    wide_low = s4_wide(0, width, rows, log_step, *states)
    across = wide_forward(packed, stream, wide_low, age, age_reach)
    tall_low, tall_top, wide_top, top_scaled, top_bias_sums = s4_rest(
        lengths, rows, log_step, states, upstream, packs[1], [across]
    )
    moved = rows_to_cols(packed, [across] if packed else [across, stream], count, picture)
    mixed_low, across_cols, stream_cols = tall_mixed(packed, height, moved, cols, tall_low, row_age, packs[0])
    low_parts = gather_channels(mixed_low)
    first = mlp_first(0, me, low_parts, shaping, weight_in, bias_columns[0], weight_out)
    normed_low, hidden_low, slope_low, stats_low = first[4:]
    branches = scatter_channels(*first[:4])
    top_parts = gather_channels(top_scaled)

    next_cols, branch_cols, moving = tall_next(packed, height, branches, stream_cols, packs[0], tall_top, row_age)
    moved = cols_to_rows(packed, moving, count, picture)
    mixed_top, tall_rows, next_rows = wide_mixed(packed, moved, picture, wide_top, age, age_reach, packs[1])
    top_mixed_parts = gather_channels(mixed_top)
    top = mlp_top(1, me, top_mixed_parts, top_parts, shaping, weight_in, bias_columns[1], weight_out)
    stats_top, normed_top, hidden_top, before_grad_top = top[4:]
    top_grads = scatter_channels(*top[:4])
    top_out = out_grad(False, me, hidden_top, top_parts)[0]
    top_in, top_units = in_grad(False, me, normed_top, before_grad_top)
    top_weights = lax.psum((top_in, top_out), "rows")

    moving, grad_rows, top_sums = wide_norm_back(
        packed, channels_all, top_grads, mixed_top, stats_top, packs[1], next_rows, upstream, wide_top, fore, fore_reach,
        [top_in, top_out],
    )
    top_partials = mlp_out(1, me, hidden_top, weight_out, moving[:1])
    moved = rows_to_cols(packed, moving, count, picture)
    grad_cols, grad_low, conv_cols = tall_back(packed, height, moved, cols, tall_top, row_fore, packs[0], branch_cols, top_partials[:1])

    grad_parts = gather_channels(grad_low)
    *back, before_grad_low = mlp_back(0, me, low_parts, grad_parts, shaping, weight_in, weight_out, slope_low, stats_low)
    low_grads = scatter_channels(*back)
    low_out = out_grad(eight, me, hidden_low, grad_parts, [before_grad_low])
    if eight:
        near_out = across_rows(low_out[1], 1)
        *low_in, low_units = in_grad(True, me, normed_low, before_grad_low, [near_out])
        near_in = across_rows(low_in[1], 1)
    else:
        *low_in, low_units = in_grad(False, me, normed_low, before_grad_low)
    moving, low_grad_cols, low_sums = tall_norm_back(
        packed, height, channels_all, low_grads, mixed_low, stats_low, packs[0], stream_cols, grad_cols, tall_low, row_fore,
        low_out[1:],
    )
    moved = cols_to_rows(packed, moving, count, picture)
    pixels_grad, low_conv_rows = wide_back(packed, moved, picture, wide_low, fore, fore_reach, top_weights[:1])
    if eight:
        in_grads = assemble(me, *rows_sum_matrix(me, low_in[0], near_in), top_weights[0])
        out_grads = assemble(me, *rows_sum_matrix(me, low_out[0], near_out), top_weights[1])
    else:
        low_weights = lax.psum((low_in[0], low_out[0]), "rows")
        in_grads = jnp.stack([low_weights[0], top_weights[0]]).astype(f32)
        out_grads = jnp.stack([low_weights[1], top_weights[1]]).astype(f32)

    top_branches = scatter_channels(*top_partials)
    activations, top_scale_sums = top_output(top_branches, next_rows, upstream, packs[1], moving[:1])
    low_branch = branch_sums(grad_cols, branch_cols, packs[0], moving[:1])
    top_tall = tall_kernel_grad(height, conv_cols, next_cols, row_age, moving[:1])
    top_wide = wide_kernel_grad(grad_rows, tall_rows, age, age_reach, moving[:1])
    low_tall = tall_kernel_grad(height, low_grad_cols, across_cols, row_age, moving[:1])
    low_wide = wide_kernel_grad(low_conv_rows, stream, age, age_reach)
    small = [
        [low_tall, low_wide, low_sums, *low_branch, low_units],
        [top_tall, top_wide, top_sums, top_bias_sums, top_scale_sums, top_units],
    ]
    if eight:
        sums = [rows_sum(collect(height, *parts)) for parts in small]
    else:
        small = lax.psum(small, "rows")
        sums = [jnp.concatenate([parts[1], parts[0]], axis=1) for parts in small]
    state_grads = []
    vectors = [None, None]
    for section in (1, 0):
        *state_grads, vectors[section] = s4_pullback(section, lengths, sums[section], log_step, *states, state_grads)
    if not eight:
        vectors = [
            jnp.concatenate([parts[2][:, :3].T, parts[3][:, :1].T, parts[4][:, :1].T, parts[5][:, 0].reshape(-1, channels)], axis=0)
            for parts in small
        ]
    step_grad, decay_grad, freq_grad, real_grad, imag_grad = state_grads
    vectors = jnp.stack([value[:5 + weight_in.shape[2] // channels] for value in vectors])
    return (
        jnp.swapaxes(activations, 2, 3),
        jnp.swapaxes(pixels_grad, 2, 3),
        step_grad,
        jnp.swapaxes(decay_grad, 2, 3),
        jnp.swapaxes(freq_grad, 2, 3),
        jnp.swapaxes(real_grad, 2, 3),
        jnp.swapaxes(imag_grad, 2, 3),
        vectors[:, 0],
        vectors[:, 1],
        vectors[:, 2],
        in_grads,
        vectors[:, 5:].reshape(2, -1),
        out_grads,
        vectors[:, 3],
        vectors[:, 4],
    )


def solution(mesh):
    picture = P(None, "rows", None, "ch")
    state = P(None, None, "ch", None)
    step = P(None, None, "ch")
    vector = P(None, "ch")
    into = P(None, None, "ch")
    out = P(None, "ch", None)
    in_specs = (
        picture, P(), P(), step, state, state, state, state, vector, vector, vector, into, vector, out, vector, vector, picture,
    )
    out_specs = (
        picture, picture, step, state, state, state, state, vector, vector, vector, into, vector, out, vector, vector,
    )
    return jax.shard_map(
        partial(on_device, mesh.shape["rows"]), mesh=mesh, in_specs=in_specs, out_specs=out_specs, check_vma=False
    )
```

```python
from functools import partial

import jax
import jax.numpy as jnp
from jax import lax
from jax.experimental import pallas as pl
from jax.experimental.pallas import tpu as pltpu
from jax.sharding import PartitionSpec as P


epsilon = 1e-06
bf16 = jnp.bfloat16
f32 = jnp.float32
vmem_bytes = 56 * 1024 * 1024
ahead = 8
band = 16
lane = 128


def dot(a, b, ca, cb):
    return lax.dot_general(a, b, (((ca,), (cb,)), ((), ())), preferred_element_type=f32)


def vmem_spec():
    return pl.BlockSpec(memory_space=pltpu.VMEM)


def smem_spec():
    return pl.BlockSpec(memory_space=pltpu.SMEM)


def any_spec():
    return pl.BlockSpec(memory_space=pl.ANY)


def struct(shape, dtype):
    return jax.ShapeDtypeStruct(shape, dtype)


def params():
    return dict(
        compiler_params=pltpu.CompilerParams(vmem_limit_bytes=vmem_bytes),
        cost_estimate=pl.CostEstimate(flops=1, bytes_accessed=1, transcendentals=0),
    )


def launch(body, name, ins, outs, scratch=(), scalars=(), after=(), through=()):
    given, kept = len(scalars) + len(ins), len(after) + len(through)

    def run(*refs):
        body(*refs[:given], *refs[given + kept:given + kept + len(outs)], *refs[given + kept + len(outs) + len(through):])

    return pl.pallas_call(
        run,
        in_specs=[smem_spec()] * len(scalars) + [vmem_spec()] * len(ins) + [any_spec()] * kept,
        out_specs=[vmem_spec()] * len(outs) + [any_spec()] * len(through),
        out_shape=list(outs) + [struct(value.shape, value.dtype) for value in through],
        scratch_shapes=list(scratch),
        input_output_aliases={given + len(after) + k: len(outs) + k for k in range(len(through))},
        name=name,
        **params(),
    )(*scalars, *ins, *after, *through)


def swap(parts, number, chunk):
    width = 16 << chunk
    lanes = lax.broadcasted_iota(jnp.int32, parts[0].shape, 1)
    low = (lanes // width) % 2 == 0
    parts = list(parts)
    for i in range(8):
        j = i | (1 << number)
        if i != j:
            a, b = parts[i], parts[j]
            parts[i] = jnp.where(low, a, pltpu.roll(b, width, 1))
            parts[j] = jnp.where(low, pltpu.roll(a, lane - width, 1), b)
    return parts


half_rows = 96
strip = 32


def pieces_from_rows(get, out_ref, kind):
    for at in range(0, half_rows, strip):
        parts = [get((i >> 1) & 1, i & 1, slice((i >> 2) * half_rows + at, (i >> 2) * half_rows + at + strip)) for i in range(8)]
        for bit in range(3):
            parts = swap(parts, bit, bit)
        for target in range(8):
            out_ref[target, kind, at:at + strip, :] = parts[target].astype(bf16)


def rows_from_pieces(in_ref, kind, put):
    for at in range(0, half_rows, strip):
        parts = [in_ref[source, kind, at:at + strip, :].astype(f32) for source in range(8)]
        for bit in range(3):
            parts = swap(parts, bit, bit)
        for i in range(8):
            put((i >> 1) & 1, i & 1, slice((i >> 2) * half_rows + at, (i >> 2) * half_rows + at + strip), parts[i])


def pieces_from_cols(get, out_ref, kind):
    for at in range(0, half_rows, strip):
        parts = []
        for i in range(8):
            upper, half, canvas = i >> 2, (i >> 1) & 1, i & 1
            first = (canvas * 2 + upper) * lane
            parts.append(get(slice(half * half_rows + at, half * half_rows + at + strip), slice(first, first + lane)))
        parts = swap(swap(parts, 1, 2), 0, 1)
        for target in range(8):
            out_ref[target, kind, at:at + strip, :] = parts[target].astype(bf16)


def cols_from_pieces(in_ref, kind, out_ref):
    for at in range(0, half_rows, strip):
        parts = [in_ref[source, kind, at:at + strip, :].astype(f32) for source in range(8)]
        parts = swap(swap(parts, 1, 2), 0, 1)
        for i in range(8):
            upper, half, canvas = i >> 2, (i >> 1) & 1, i & 1
            first = (canvas * 2 + upper) * lane
            out_ref[half * half_rows + at:half * half_rows + at + strip, first:first + lane] = parts[i].astype(out_ref.dtype)


def piece_shape(kinds):
    return struct((8, kinds, half_rows, lane), bf16)


def state_powers(step, decay, frequency):
    size = jnp.exp(-step * decay)
    turn = step * frequency
    z = (size * jnp.cos(turn), size * jnp.sin(turn))

    def times(p, q):
        return (p[0] * q[0] - p[1] * q[1], p[0] * q[1] + p[1] * q[0])

    z2 = times(z, z)
    z3 = times(z2, z)
    z4 = times(z2, z2)
    return [None, z, z2, z3, z4, times(z4, z), times(z4, z2), times(z4, z3)], times(z4, z4), times


def pack_lanes(value):
    half = value.shape[0] // 2
    return jnp.concatenate([value[:half], value[half:]], axis=1)


def unpack_lanes(value):
    half = value.shape[1] // 2
    return jnp.concatenate([value[:, :half], value[:, half:]], axis=0)


def s4_section(direction, length, section, step_ref, decay_ref, freq_ref, real_ref, imag_ref, q_ref, flat_ref):
    channels = step_ref.shape[2]
    step = jnp.exp(step_ref[section, direction:direction + 1, :])
    step = jnp.concatenate([step, step], axis=1)
    decay = jnp.exp(pack_lanes(decay_ref[section, direction]))
    powers, z8, times = state_powers(step, decay, pack_lanes(freq_ref[section, direction]))
    for a in range(1, ahead):
        q_ref[2 * a] = powers[a][0]
        q_ref[2 * a + 1] = powers[a][1]
    q_ref[0] = z8[0]
    q_ref[1] = z8[1]

    def block(b, carry):
        pr, pi = carry
        rows = [jnp.sum(pr, axis=0, keepdims=True)]
        for a in range(1, ahead):
            rows.append(jnp.sum(pr * q_ref[2 * a] - pi * q_ref[2 * a + 1], axis=0, keepdims=True))
        flat_ref[pl.ds(pl.multiple_of(b * ahead, ahead), ahead), :] = step * jnp.concatenate(rows, axis=0)
        zr, zi = q_ref[0], q_ref[1]
        return (pr * zr - pi * zi, pr * zi + pi * zr)

    start = (pack_lanes(real_ref[section, direction]), pack_lanes(imag_ref[section, direction]))
    lax.fori_loop(0, length // ahead, block, start)
    flat = jnp.transpose(flat_ref[...])
    return (flat[:channels] + flat[channels:]).astype(bf16).astype(f32)


def s4_scratch(states, channels):
    return [pltpu.VMEM((2 * ahead, states // 2, 2 * channels), f32), pltpu.VMEM((lane, 2 * channels), f32)]


def s4_wide_body(length, section, copies, step_ref, decay_ref, freq_ref, real_ref, imag_ref, out_ref, q_ref, flat_ref):
    kernel = s4_section(1, length, section, step_ref, decay_ref, freq_ref, real_ref, imag_ref, q_ref, flat_ref)
    out_ref[...] = jnp.transpose(jnp.concatenate([kernel] * copies, axis=0))


def s4_wide(section, length, copies, log_step, *states):
    channels = states[0].shape[3]
    return launch(
        partial(s4_wide_body, length, section, copies), "s4_wide", [log_step, *states],
        [struct((lane, copies * channels), f32)], s4_scratch(states[0].shape[2], channels),
    )[0]


def s4_rest_body(lengths, copies, step_ref, decay_ref, freq_ref, real_ref, imag_ref, upstream_ref, pack_ref,
                 tall_low, tall_top, wide_top, scaled_ref, sums_ref, q_ref, flat_ref):
    refs = (step_ref, decay_ref, freq_ref, real_ref, imag_ref, q_ref, flat_ref)
    tall_low[...] = s4_section(0, lengths[0], 0, *refs)
    tall_top[...] = s4_section(0, lengths[0], 1, *refs)
    wide_top[...] = jnp.transpose(jnp.concatenate([s4_section(1, lengths[1], 1, *refs)] * copies, axis=0))
    scale = pack_ref[:, 4:5]
    total = jnp.zeros(scale.shape, f32)
    rows = upstream_ref.shape[1]
    for canvas in range(upstream_ref.shape[0]):
        for row in range(rows):
            scaled = upstream_ref[canvas, row].astype(f32) * scale
            at = (canvas * rows + row) * lane
            scaled_ref[:, at:at + lane] = scaled.astype(bf16)
            total += jnp.sum(scaled, axis=1, keepdims=True)
    put_columns(sums_ref, [total])


def s4_rest(lengths, copies, log_step, states, upstream, pack, after):
    channels = states[0].shape[3]
    pixels = upstream.shape[0] * upstream.shape[1] * lane
    column = struct((channels, lane), f32)
    return launch(
        partial(s4_rest_body, lengths, copies), "s4_rest", [log_step, *states, upstream, pack],
        [column, column, struct((lane, copies * channels), f32), struct((channels, pixels), bf16), column],
        s4_scratch(states[0].shape[2], channels), after=after,
    )


def pull_section(direction, length, grads_ref, step_ref, decay_ref, freq_ref, real_ref, imag_ref,
                 dstep_ref, ddecay_ref, dfreq_ref, dreal_ref, dimag_ref, turn_ref, spread_ref, q_ref, s_ref):
    channels = step_ref.shape[2]
    states = decay_ref.shape[2]
    tiles = 2 * channels // lane
    step = jnp.exp(step_ref[0, direction:direction + 1, :])
    decay = jnp.exp(decay_ref[0, direction])
    freq = freq_ref[0, direction]
    wide_step = jnp.concatenate([step, step], axis=1)
    powers, z8, times = state_powers(wide_step, pack_lanes(decay), pack_lanes(freq))
    for a in range(ahead):
        for part in range(2):
            value = (z8 if a == 0 else powers[a])[part]
            for t in range(tiles):
                q_ref[2 * a + part, t] = value[:, t * lane:(t + 1) * lane]
    first = (1 - direction) * lane
    grads = grads_ref[0, :, first:first + lane].astype(f32)
    turn_ref[0:channels, :] = grads
    turn_ref[channels:2 * channels, :] = grads
    flat = jnp.transpose(turn_ref[...])
    for place in range(length):
        for t in range(tiles):
            spread_ref[t, place] = jnp.broadcast_to(flat[place:place + 1, t * lane:(t + 1) * lane], (8, lane))
    turns = length // ahead
    groups = states // 16

    def group(index, carry):
        t = index // groups
        part = pl.ds(pl.multiple_of(lax.rem(index, groups) * 8, 8), 8)
        q = [(q_ref[2 * a, t, part, :], q_ref[2 * a + 1, t, part, :]) for a in range(ahead)]
        zr, zi = q[0]

        def block(turn, sums):
            s0r, s0i, s1r, s1i = sums
            b = turns - 1 - turn
            t0r = t0i = t1r = t1i = None
            for a in range(ahead - 1, 0, -1):
                g = spread_ref[t, b * ahead + a]
                x, y = g * q[a][0], g * q[a][1]
                t0r, t0i = (x, y) if t0r is None else (t0r + x, t0i + y)
                t1r, t1i = (t0r, t0i) if t1r is None else (t1r + t0r, t1i + t0i)
            t0r = t0r + spread_ref[t, b * ahead]
            base = (b * ahead).astype(f32)
            v1r, v1i = t1r + base * t0r, t1i + base * t0i
            return (
                s0r * zr - s0i * zi + t0r,
                s0r * zi + s0i * zr + t0i,
                s1r * zr - s1i * zi + v1r,
                s1r * zi + s1i * zr + v1i,
            )

        zero = jnp.zeros((8, lane), f32)
        sums = lax.fori_loop(0, turns, block, (zero, zero, zero, zero))
        for k in range(4):
            s_ref[k, t, part, :] = sums[k]
        return carry

    lax.fori_loop(0, tiles * groups, group, 0)
    s0r, s0i, s1r, s1i = [
        unpack_lanes(jnp.concatenate([s_ref[k, t] for t in range(tiles)], axis=1)) for k in range(4)
    ]
    real, imag = real_ref[0, direction], imag_ref[0, direction]
    dreal = step * s0r
    dimag = -step * s0i
    ddecay = -step * step * decay * (real * s1r - imag * s1i)
    dfreq = -step * step * (real * s1i + imag * s1r)
    dreal_ref[0, direction] = dreal
    dimag_ref[0, direction] = dimag
    ddecay_ref[0, direction] = ddecay
    dfreq_ref[0, direction] = dfreq
    dstep_ref[0, direction:direction + 1, :] = jnp.sum(
        real * dreal + imag * dimag + ddecay + freq * dfreq, axis=0, keepdims=True
    )
    return flat


def pull_body(lengths, grads_ref, step_ref, decay_ref, freq_ref, real_ref, imag_ref, dstep_ref, ddecay_ref, dfreq_ref, dreal_ref,
              dimag_ref, skip_ref, gain_ref, shift_ref, units_ref, bias_ref, scale_ref, *scratch):
    channels = step_ref.shape[2]
    refs = (grads_ref, step_ref, decay_ref, freq_ref, real_ref, imag_ref, dstep_ref, ddecay_ref, dfreq_ref, dreal_ref, dimag_ref)
    pull_section(1, lengths[1], *refs, *scratch)
    rows = pull_section(0, lengths[0], *refs, *scratch)
    first = lengths[0]
    if first + 16 > lane:
        turn_ref = scratch[0]
        turn_ref[0:channels, :] = grads_ref[0, :, 2 * lane:].astype(f32)
        rows, first = jnp.transpose(turn_ref[...]), first - lane
    per = units_ref.shape[1] // channels
    section = pl.program_id(0)

    def row(index):
        return rows[first + index:first + index + 1, 0:channels]

    def put(at):
        for index, ref in enumerate((skip_ref, gain_ref, shift_ref, bias_ref)):
            ref[at:at + 1, :] = row(index)
        units_ref[at:at + 1, :] = jnp.concatenate([row(4 + index) for index in range(per)], axis=1)

    @pl.when(section == 0)
    def _():
        put(0)
        scale_ref[0:1, :] = row(4 + per)
        scale_ref[1:2, :] = row(5 + per)

    @pl.when(section == 1)
    def _():
        put(1)


def s4_pullback(lengths, units, grads, log_step, log_decay, frequency, coef_real, coef_imag, after):
    states, channels = log_decay.shape[2], log_decay.shape[3]
    whole = pl.BlockSpec((1, 2, states, channels), lambda i: (i, 0, 0, 0))
    row = pl.BlockSpec((1, 2, channels), lambda i: (i, 0, 0))
    tiles = 2 * channels // lane
    vectors = [(2, channels)] * 3 + [(2, units)] + [(2, channels)] * 2

    def body(*refs):
        pull_body(lengths, *refs[:6], *refs[6 + len(after):])

    return pl.pallas_call(
        body,
        grid=(2,),
        in_specs=[pl.BlockSpec((1,) + grads.shape[1:], lambda i: (i, 0, 0)), row, whole, whole, whole, whole]
        + [any_spec()] * len(after),
        out_specs=[row, whole, whole, whole, whole] + [pl.BlockSpec(shape, lambda i: (0, 0)) for shape in vectors],
        out_shape=[struct(log_step.shape, f32)] + [struct(log_decay.shape, f32)] * 4 + [struct(shape, f32) for shape in vectors],
        scratch_shapes=[
            pltpu.VMEM((2 * channels, lane), f32),
            pltpu.VMEM((tiles, lane, 8, lane), f32),
            pltpu.VMEM((2 * ahead, tiles, states // 2, lane), f32),
            pltpu.VMEM((4, tiles, states // 2, lane), f32),
        ],
        name="s4_pullback",
        **params(),
    )(grads, log_step, log_decay, frequency, coef_real, coef_imag, *after)


pad = 8


def lane_tiles(value):
    return [value[:, at:at + lane] for at in range(0, value.shape[1], lane)]


def load_tiles(value, ref, first):
    for index, part in enumerate(lane_tiles(value)):
        ref[index, first:first + part.shape[0], :] = part


def width_conv(canvas, sign, signal_ref, kernel_ref, age_ref, reach_ref, out_ref):
    tiles, width = out_ref.shape[0], out_ref.shape[1]
    per = band // 8
    for index in range(width // band):
        ages = [age_ref[canvas, pl.ds((index * per + k) * 8, 8), :] for k in range(per)]

        def body(q, sums):
            sums = list(sums)
            places = [
                pl.multiple_of(jnp.clip(index * per + k - sign * q, 0, width // 8 - 1) * 8, 8) for k in range(per)
            ]
            for s in range(ahead):
                lag = q * ahead + s
                seen = [ages[k] >= lag for k in range(per)]
                for t in range(tiles):
                    value = jnp.broadcast_to(kernel_ref[t, pl.ds(lag, 1), :], (8, lane))
                    for k in range(per):
                        x = signal_ref[t, pl.ds(places[k] + (pad - sign * s), 8), :]
                        sums[k * tiles + t] += value * jnp.where(seen[k], x, 0.0)
            return tuple(sums)

        zero = jnp.zeros((8, lane), f32)
        sums = lax.fori_loop(0, reach_ref[canvas, index], body, (zero,) * (per * tiles))
        for k in range(per):
            for t in range(tiles):
                out_ref[t, pl.ds((index * per + k) * 8, 8), :] = sums[k * tiles + t]


def width_products(canvas, signal_ref, grad_ref, age_ref, reach_ref, total_ref):
    tiles, width = grad_ref.shape[0], grad_ref.shape[1]
    per = band // 8
    for index in range(width // band):
        ages = [age_ref[canvas, pl.ds((index * per + k) * 8, 8), :] for k in range(per)]
        grads = [[grad_ref[t, pl.ds((index * per + k) * 8, 8), :] for t in range(tiles)] for k in range(per)]

        def body(q, carry):
            places = [
                pl.multiple_of(jnp.clip(index * per + k - q, 0, width // 8 - 1) * 8, 8) for k in range(per)
            ]
            for s in range(ahead):
                lag = q * ahead + s
                seen = [ages[k] >= lag for k in range(per)]
                for t in range(tiles):
                    total = total_ref[t, lag]
                    for k in range(per):
                        x = signal_ref[t, pl.ds(places[k] + (pad - s), 8), :]
                        total += grads[k][t] * jnp.where(seen[k], x, 0.0)
                    total_ref[t, lag] = total
            return carry

        lax.fori_loop(0, reach_ref[canvas, index], body, 0)


def stacked_rows(ref, canvas):
    picture = ref[canvas].astype(f32)
    return jnp.transpose(picture.reshape(-1, picture.shape[2]))


def unstacked(ref, rows):
    flat = jnp.concatenate([jnp.transpose(ref[t]) for t in range(ref.shape[0])], axis=0)
    return flat.reshape(rows, flat.shape[0] // rows, flat.shape[1])


def width_scratch(rows, channels):
    tiles = rows * channels // lane
    return [
        pltpu.VMEM((tiles, lane + 2 * pad, lane), f32),
        pltpu.VMEM((tiles, lane, lane), f32),
        pltpu.VMEM((tiles, lane, lane), f32),
    ]


def convolve_canvas(canvas, sign, picture_ref, age_ref, reach_ref, signal_ref, kernel_ref, sum_ref):
    load_tiles(stacked_rows(picture_ref, canvas), signal_ref, pad)
    width_conv(canvas, sign, signal_ref, kernel_ref, age_ref, reach_ref, sum_ref)
    return unstacked(sum_ref, picture_ref.shape[1])


def wide_forward_body(packed, reach_ref, picture_ref, wide_ref, age_ref, out_ref, signal_ref, kernel_ref, sum_ref, *held):
    load_tiles(wide_ref[...], kernel_ref, 0)
    across_ref = held[0] if packed else out_ref
    for canvas in range(picture_ref.shape[0]):
        across_ref[canvas] = convolve_canvas(
            canvas, 1, picture_ref, age_ref, reach_ref, signal_ref, kernel_ref, sum_ref
        ).astype(across_ref.dtype)
    if packed:
        pieces_from_rows(lambda b, r, c: across_ref[b, r, c, :], out_ref, 0)
        pieces_from_rows(lambda b, r, c: picture_ref[b, r, c, :].astype(f32), out_ref, 1)


def wide_forward(packed, picture, wide, age, reach):
    out = piece_shape(2) if packed else struct(picture.shape, bf16)
    scratch = width_scratch(picture.shape[1], picture.shape[2])
    return launch(
        partial(wide_forward_body, packed), "wide_forward", [picture, wide, age], [out],
        scratch + [pltpu.VMEM(picture.shape, f32)] * packed, scalars=[reach],
    )[0]


def split_refs(packed, refs, held):
    return (refs[0], refs[1:]) if packed else (refs[:held], refs[held:])


def wide_mixed_body(packed, reach_ref, *refs):
    if packed:
        pieces, wide_ref, age_ref, pack_ref, out_ref, tall_ref, stream_ref, signal_ref, kernel_ref, sum_ref = refs
        for kind, ref in enumerate((tall_ref, stream_ref)):
            def put(b, r, c, value, ref=ref):
                ref[b, r, c, :] = value.astype(bf16)
            rows_from_pieces(pieces, kind, put)
    else:
        tall_ref, stream_ref, wide_ref, age_ref, pack_ref, out_ref, signal_ref, kernel_ref, sum_ref = refs
    rows = tall_ref.shape[1]
    skip = pack_ref[:, 0:1]
    load_tiles(wide_ref[...], kernel_ref, 0)
    for canvas in range(tall_ref.shape[0]):
        mixer = convolve_canvas(canvas, 1, tall_ref, age_ref, reach_ref, signal_ref, kernel_ref, sum_ref)
        for row in range(rows):
            at = (canvas * rows + row) * lane
            out_ref[:, at:at + lane] = (
                mixer[row] + skip * stream_ref[canvas, row].astype(f32)
            ).astype(bf16)


def wide_mixed(packed, moved, picture, wide, age, reach, pack):
    canvases, rows, channels, width = picture
    outs = [struct((channels, canvases * rows * lane), bf16)] + [struct(picture, bf16)] * (2 * packed)
    got = launch(
        partial(wide_mixed_body, packed), "wide_mixed", [*moved, wide, age, pack], outs,
        width_scratch(rows, channels), scalars=[reach],
    )
    return tuple(got) if packed else (got[0], *moved)


def norm_backward(grads, mixed_ref, stats_ref, pack_ref, channels_all):
    channels = mixed_ref.shape[0]
    keep, near, far = grads
    total = keep[...].astype(f32) + near[...].astype(f32) + far[...].astype(f32)
    normed_grad = total[0:channels]
    scaled_mean = total[channels:channels + 1] / channels_all
    paired_mean = total[channels + 1:channels + 2] / channels_all
    average, inverse = stats_ref[0:1, :], stats_ref[1:2, :]
    centred = (mixed_ref[...].astype(f32) - average) * inverse
    gain = pack_ref[:, 1:2]
    mixed_grad = inverse * (normed_grad * gain - scaled_mean - centred * paired_mean)
    return (
        mixed_grad,
        jnp.sum(normed_grad * centred, axis=1, keepdims=True),
        jnp.sum(normed_grad, axis=1, keepdims=True),
    )


def put_columns(ref, columns):
    places = lax.broadcasted_iota(jnp.int32, ref.shape, 1)
    value = jnp.zeros(ref.shape, f32)
    for index, column in enumerate(columns):
        value = jnp.where(places == index, column, value)
    ref[...] = value


def wide_norm_back_body(packed, channels_all, reach_ref, keep_ref, near_ref, far_ref, mixed_ref, stats_ref, pack_ref,
                        stream_ref, cotangent_ref, wide_ref, fore_ref, *refs):
    if packed:
        out_ref, grad_ref, sums_ref, signal_ref, kernel_ref, sum_ref, conv_ref, rest_ref = refs
    else:
        conv_ref, rest_ref, grad_ref, sums_ref, signal_ref, kernel_ref, sum_ref = refs
    canvases, rows = conv_ref.shape[0], conv_ref.shape[1]
    mixed_grad, gain_grad, shift_grad = norm_backward(
        (keep_ref, near_ref, far_ref), mixed_ref, stats_ref, pack_ref, channels_all
    )
    skip = pack_ref[:, 0:1]
    skip_grad = jnp.zeros_like(gain_grad)
    load_tiles(wide_ref[...], kernel_ref, 0)
    for canvas in range(canvases):
        for row in range(rows):
            at = (canvas * rows + row) * lane
            part = mixed_grad[:, at:at + lane]
            grad_ref[canvas, row] = part.astype(bf16)
            skip_grad += jnp.sum(part * stream_ref[canvas, row].astype(f32), axis=1, keepdims=True)
            rest_ref[canvas, row] = (cotangent_ref[canvas, row].astype(f32) + skip * part).astype(rest_ref.dtype)
        conv_ref[canvas] = convolve_canvas(
            canvas, -1, grad_ref, fore_ref, reach_ref, signal_ref, kernel_ref, sum_ref
        ).astype(conv_ref.dtype)
    put_columns(sums_ref, [skip_grad, gain_grad, shift_grad])
    if packed:
        pieces_from_rows(lambda b, r, c: conv_ref[b, r, c, :], out_ref, 0)
        pieces_from_rows(lambda b, r, c: rest_ref[b, r, c, :], out_ref, 1)


def wide_norm_back(packed, channels_all, grads, mixed, stats, pack, stream, cotangent, wide, fore, reach, after):
    plain = struct(stream.shape, bf16)
    sums = struct((stream.shape[2], lane), f32)
    got = launch(
        partial(wide_norm_back_body, packed, channels_all), "wide_norm_back",
        [*grads, mixed, stats, pack, stream, cotangent, wide, fore],
        [piece_shape(2), plain, sums] if packed else [plain, plain, plain, sums],
        width_scratch(stream.shape[1], stream.shape[2]) + [pltpu.VMEM(stream.shape, f32)] * (2 * packed),
        scalars=[reach], after=after,
    )
    return got[:-2], got[-2], got[-1]


def kernel_products(grad_ref, input_ref, age_ref, reach_ref, signal_ref, flat_ref, sum_ref, total_ref):
    channels = grad_ref.shape[2]
    rows = grad_ref.shape[1]
    total_ref[...] = jnp.zeros(total_ref.shape, f32)
    for canvas in range(grad_ref.shape[0]):
        load_tiles(stacked_rows(input_ref, canvas), signal_ref, pad)
        load_tiles(stacked_rows(grad_ref, canvas), flat_ref, 0)
        width_products(canvas, signal_ref, flat_ref, age_ref, reach_ref, total_ref)

    def reduce(index, carry):
        at = pl.multiple_of(index * 8, 8)
        for t in range(sum_ref.shape[0]):
            sum_ref[t, pl.ds(at, 8), :] = jnp.sum(total_ref[t, pl.ds(at, 8)], axis=1)
        return carry

    lax.fori_loop(0, lane // 8, reduce, 0)
    picture = unstacked(sum_ref, rows)
    return sum(picture[row] for row in range(rows))


def products_scratch(rows, channels):
    return width_scratch(rows, channels) + [pltpu.VMEM((rows * channels // lane, lane, 8, lane), f32)]


def wide_top_grad_body(reach_ref, grad_ref, input_ref, age_ref, out_ref, *scratch):
    out_ref[...] = kernel_products(grad_ref, input_ref, age_ref, reach_ref, *scratch)


def wide_top_grad(grad, inputs, age, reach, after=()):
    channels = grad.shape[2]
    return launch(
        wide_top_grad_body, "wide_top_grad", [grad, inputs, age], [struct((channels, lane), f32)],
        products_scratch(grad.shape[1], channels), scalars=[reach], after=after,
    )[0]


def wide_last_body(packed, forth_reach, back_reach, *refs):
    if packed:
        pieces, input_ref, wide_ref, age_ref, fore_ref, held_ref, top_ref, out_ref, total_out, *refs = refs
        signal_ref, kernel_ref, sum_ref, total_ref, grad_ref, rest_ref = refs

        def put_grad(b, r, c, value):
            grad_ref[b, r, c, :] = value.astype(bf16)

        def put_rest(b, r, c, value):
            rest_ref[b, r, c, :] = value

        rows_from_pieces(pieces, 0, put_grad)
        rows_from_pieces(pieces, 1, put_rest)
    else:
        grad_ref, rest_ref, input_ref, wide_ref, age_ref, fore_ref, held_ref, top_ref, out_ref, total_out, *refs = refs
        signal_ref, kernel_ref, sum_ref, total_ref = refs
    total_out[0, :, 0:lane] = kernel_products(
        grad_ref, input_ref, age_ref, forth_reach, signal_ref, kernel_ref, sum_ref, total_ref
    ).astype(bf16)
    total_out[0, :, lane:] = held_ref[...].astype(bf16)
    total_out[1] = top_ref[...]
    load_tiles(wide_ref[...], kernel_ref, 0)
    for canvas in range(grad_ref.shape[0]):
        value = convolve_canvas(canvas, -1, grad_ref, fore_ref, back_reach, signal_ref, kernel_ref, sum_ref)
        out_ref[canvas] = (value + rest_ref[canvas].astype(f32)).astype(bf16)


def wide_last(packed, moved, picture, inputs, wide, age, fore, held, top, forth_reach, back_reach, after):
    plain = struct(picture, bf16)
    scratch = products_scratch(picture[1], picture[2])
    if packed:
        scratch += [pltpu.VMEM(picture, bf16), pltpu.VMEM(picture, f32)]
    return launch(
        partial(wide_last_body, packed), "wide_last", [*moved, inputs, wide, age, fore, held, top],
        [plain, struct((2,) + top.shape, bf16)], scratch, scalars=[forth_reach, back_reach], after=after,
    )


def height_loop(count, body, carry):
    if count <= 16:
        for lag in range(count):
            carry = body(lag, carry)
        return carry
    return lax.fori_loop(0, count, body, carry)


def tap(kernel, lag):
    if isinstance(lag, int):
        return kernel[:, lag:lag + 1]
    places = lax.broadcasted_iota(jnp.int32, kernel.shape, 1)
    return jnp.sum(jnp.where(places == lag, kernel, 0.0), axis=1, keepdims=True)


def moved_by(value, shift):
    size = value.shape[1]
    if not isinstance(shift, int):
        return pltpu.roll(value, lax.rem(shift + size, size), 1)
    shift %= size
    return pltpu.roll(value, shift, 1) if shift else value


def height_conv(get, put, channels, kernel_ref, age_ref, sign, height):
    for at in range(0, channels, strip):
        rows = slice(at, at + strip)
        kernel = kernel_ref[rows, :]
        for canvas in range(age_ref.shape[0]):
            value, age = get(rows, canvas), age_ref[canvas]
            columns = value.shape[1] // height

            def body(lag, total):
                return total + tap(kernel, lag) * jnp.where(age >= lag, moved_by(value, sign * lag * columns), 0.0)

            put(rows, canvas, height_loop(height, body, jnp.zeros_like(value)))


def height_products(grads, values, ages, height):
    columns = values[0].shape[1] // height
    channels = values[0].shape[0]
    places = lax.broadcasted_iota(jnp.int32, (channels, lane), 1)

    def body(lag, total):
        part = None
        for grad, value, age in zip(grads, values, ages, strict=True):
            product = grad * jnp.where(age >= lag, moved_by(value, lag * columns), 0.0)
            for piece in lane_tiles(product):
                part = piece if part is None else part + piece
        return total + jnp.where(places == lag, jnp.sum(part, axis=1, keepdims=True), 0.0)

    return height_loop(height, body, jnp.zeros((channels, lane), f32))


def canvas_cut(ref, canvas, canvases):
    each = ref.shape[1] // canvases
    return slice(canvas * each, (canvas + 1) * each)


def tall_mixed_body(packed, height, *refs):
    if packed:
        pieces, kernel_ref, age_ref, pack_ref, out_ref, across_ref, stream_ref = refs
        cols_from_pieces(pieces, 0, across_ref)
        cols_from_pieces(pieces, 1, stream_ref)
    else:
        across_ref, stream_ref, kernel_ref, age_ref, pack_ref, out_ref = refs
    canvases = age_ref.shape[0]

    def get(rows, canvas):
        return across_ref[rows, canvas_cut(across_ref, canvas, canvases)].astype(f32)

    def put(rows, canvas, mixer):
        cut = canvas_cut(across_ref, canvas, canvases)
        out_ref[rows, cut] = (mixer + pack_ref[rows, 0:1] * stream_ref[rows, cut].astype(f32)).astype(bf16)

    height_conv(get, put, out_ref.shape[0], kernel_ref, age_ref, 1, height)


def tall_mixed(packed, height, moved, cols, kernel, age, pack):
    got = launch(
        partial(tall_mixed_body, packed, height), "tall_mixed", [*moved, kernel, age, pack],
        [struct(cols, bf16)] * (1 + 2 * packed),
    )
    return tuple(got) if packed else (got[0], *moved)


def tall_next_body(packed, height, keep_ref, near_ref, far_ref, stream_ref, pack_ref, kernel_ref, age_ref,
                   next_ref, branch_ref, out_ref, *held):
    canvases = age_ref.shape[0]
    conv_ref = held[0] if packed else out_ref

    def get(rows, canvas):
        cut = canvas_cut(stream_ref, canvas, canvases)
        branch = (
            keep_ref[rows, cut].astype(f32) + near_ref[rows, cut].astype(f32) + far_ref[rows, cut].astype(f32)
            + pack_ref[rows, 3:4]
        )
        branch_ref[rows, cut] = branch
        low = (stream_ref[rows, cut].astype(f32) + pack_ref[rows, 4:5] * branch).astype(bf16)
        next_ref[rows, cut] = low
        return low.astype(f32)

    def put(rows, canvas, value):
        conv_ref[rows, canvas_cut(stream_ref, canvas, canvases)] = value.astype(conv_ref.dtype)

    height_conv(get, put, stream_ref.shape[0], kernel_ref, age_ref, 1, height)
    if packed:
        pieces_from_cols(lambda rows, cut: conv_ref[rows, cut], out_ref, 0)
        pieces_from_cols(lambda rows, cut: next_ref[rows, cut].astype(f32), out_ref, 1)


def tall_next(packed, height, branches, stream, pack, kernel, age):
    got = launch(
        partial(tall_next_body, packed, height), "tall_next", [*branches, stream, pack, kernel, age],
        [struct(stream.shape, bf16), struct(stream.shape, f32), piece_shape(2) if packed else struct(stream.shape, bf16)],
        [pltpu.VMEM(stream.shape, f32)] * packed,
    )
    return got[0], got[1], [got[2]] if packed else [got[2], got[0]]


def tall_back_body(packed, height, *refs):
    if packed:
        pieces, kernel_ref, fore_ref, pack_ref, branch_ref, grad_ref, low_ref, sums_ref, conv_ref, rest_ref = refs
        cols_from_pieces(pieces, 0, conv_ref)
        cols_from_pieces(pieces, 1, rest_ref)
    else:
        conv_ref, rest_ref, kernel_ref, fore_ref, pack_ref, branch_ref, grad_ref, low_ref, sums_ref = refs
    canvases = fore_ref.shape[0]

    def get(rows, canvas):
        return conv_ref[rows, canvas_cut(conv_ref, canvas, canvases)].astype(f32)

    def put(rows, canvas, value):
        cut = canvas_cut(conv_ref, canvas, canvases)
        grad = rest_ref[rows, cut].astype(f32) + value
        grad_ref[rows, cut] = grad
        low_ref[rows, cut] = (grad * pack_ref[rows, 4:5]).astype(bf16)

    height_conv(get, put, conv_ref.shape[0], kernel_ref, fore_ref, -1, height)
    sums_ref[...] = jnp.zeros(sums_ref.shape, f32)


def tall_back(packed, height, moved, cols, kernel, fore, pack, branch, after, through):
    got = launch(
        partial(tall_back_body, packed, height), "tall_back", [*moved, kernel, fore, pack, branch],
        [struct(cols, f32), struct(cols, bf16), struct((cols[0], lane), f32)] + [struct(cols, bf16)] * packed,
        [pltpu.VMEM(cols, f32)] * packed, after=after, through=through,
    )
    return got[0], got[1], got[3] if packed else moved[0], *got[3 + packed:]


def tall_norm_back_body(packed, height, channels_all, keep_ref, near_ref, far_ref, mixed_ref, stats_ref, pack_ref, stream_ref,
                        grad_ref, kernel_ref, fore_ref, *refs):
    if packed:
        out_ref, low_ref, sums_ref, conv_ref, rest_ref = refs
    else:
        conv_ref, rest_ref, low_ref, sums_ref = refs
    canvases = fore_ref.shape[0]
    mixed_grad, gain_grad, shift_grad = norm_backward(
        (keep_ref, near_ref, far_ref), mixed_ref, stats_ref, pack_ref, channels_all
    )
    low_ref[...] = mixed_grad.astype(bf16)
    rest_ref[...] = (grad_ref[...] + pack_ref[:, 0:1] * mixed_grad).astype(rest_ref.dtype)
    skip_grad = jnp.sum(mixed_grad * stream_ref[...].astype(f32), axis=1, keepdims=True)

    def get(rows, canvas):
        return low_ref[rows, canvas_cut(low_ref, canvas, canvases)].astype(f32)

    def put(rows, canvas, value):
        conv_ref[rows, canvas_cut(low_ref, canvas, canvases)] = value.astype(conv_ref.dtype)

    height_conv(get, put, low_ref.shape[0], kernel_ref, fore_ref, -1, height)
    put_columns(sums_ref, [skip_grad, gain_grad, shift_grad])
    if packed:
        pieces_from_cols(lambda rows, cut: conv_ref[rows, cut], out_ref, 0)
        pieces_from_cols(lambda rows, cut: rest_ref[rows, cut], out_ref, 1)


def tall_norm_back(packed, height, channels_all, grads, mixed, stats, pack, stream, grad, kernel, fore, after):
    plain, sums = struct(mixed.shape, bf16), struct((mixed.shape[0], lane), f32)
    got = launch(
        partial(tall_norm_back_body, packed, height, channels_all), "tall_norm_back",
        [*grads, mixed, stats, pack, stream, grad, kernel, fore],
        [piece_shape(2), plain, sums] if packed else [plain, plain, plain, sums],
        [pltpu.VMEM(mixed.shape, f32)] * (2 * packed), after=after,
    )
    return got[:-2], got[-2], got[-1]


def tall_products(height, grad_ref, input_ref, age_ref, put):
    canvases = age_ref.shape[0]
    for at in range(0, grad_ref.shape[0], strip):
        rows = slice(at, at + strip)
        cuts = [canvas_cut(grad_ref, canvas, canvases) for canvas in range(canvases)]
        put(rows, height_products(
            [grad_ref[rows, cut].astype(f32) for cut in cuts], [input_ref[rows, cut].astype(f32) for cut in cuts],
            [age_ref[canvas] for canvas in range(canvases)], height,
        ))


def held_lanes(height):
    return -(-(height + 16) // lane) * lane


def beside(held, height, columns):
    if held_lanes(height) > lane:
        held = jnp.concatenate([held, jnp.zeros_like(held)], axis=1)
    places = lax.broadcasted_iota(jnp.int32, held.shape, 1)
    held = jnp.where(places < height, held, 0.0)
    for index, column in enumerate(columns):
        held = jnp.where(places == height + index, column, held)
    return held


def unit_columns(units_ref, rows, channels):
    return [units_ref[at + rows.start:at + rows.stop, 0:1] for at in range(0, units_ref.shape[0], channels)]


def tall_top_grad_body(height, grad_ref, input_ref, age_ref, wide_ref, norm_ref, bias_ref, units_ref, out_ref):
    channels = grad_ref.shape[0]

    def put(rows, held):
        columns = [norm_ref[rows, k:k + 1] for k in range(3)] + [bias_ref[rows, 0:1]]
        out_ref[rows, lane:] = beside(held, height, columns + unit_columns(units_ref, rows, channels)).astype(bf16)

    tall_products(height, grad_ref, input_ref, age_ref, put)
    out_ref[:, 0:lane] = wide_ref[...].astype(bf16)


def tall_top_grad(height, grad, inputs, age, wide, norm, bias, units, after):
    return launch(
        partial(tall_top_grad_body, height), "tall_top_grad", [grad, inputs, age, wide, norm, bias, units],
        [struct((grad.shape[0], lane + held_lanes(height)), bf16)], after=after,
    )[0]


def tall_low_grad_body(height, grad_ref, input_ref, age_ref, norm_ref, grad_out_ref, branch_ref, pack_ref, scale_ref, units_ref,
                       out_ref):
    channels = grad_ref.shape[0]

    def put(rows, held):
        grad = grad_out_ref[rows, :]
        columns = [norm_ref[rows, k:k + 1] for k in range(3)]
        columns.append(jnp.sum(grad, axis=1, keepdims=True) * pack_ref[rows, 4:5])
        columns += unit_columns(units_ref, rows, channels)
        columns.append(jnp.sum(grad * branch_ref[rows, :], axis=1, keepdims=True))
        columns.append(scale_ref[rows, 0:1])
        out_ref[rows, :] = beside(held, height, columns)

    tall_products(height, grad_ref, input_ref, age_ref, put)


def tall_low_grad(height, grad, inputs, age, norm, grad_out, branch, pack, scale, units, after):
    return launch(
        partial(tall_low_grad_body, height), "tall_low_grad",
        [grad, inputs, age, norm, grad_out, branch, pack, scale, units],
        [struct((grad.shape[0], held_lanes(height)), f32)], after=after,
    )[0]


root = 0.7978845608028654
cubic = 0.044715


def gather_into(me_ref, parts, whole_ref):
    me = me_ref[0]
    for flip, part in enumerate(parts):
        whole_ref[me ^ flip] = part[...]


def scatter_out(me_ref, whole_ref, outs):
    me = me_ref[0]
    for flip, out in zip((3, 1, 2, 0), outs, strict=True):
        out[...] = whole_ref[me ^ flip]


def gather_shape(me_ref, parts, section, shape_ref):
    gather_into(me_ref, parts, shape_ref)
    every = shape_ref[...].reshape(-1, shape_ref.shape[2])
    return every[:, 2 * section:2 * section + 1], every[:, 2 * section + 1:2 * section + 2]


def mlp_forward(me_ref, parts, full_ref, shape, weight_in_ref, bias_ref, normed_ref, hidden_ref, slope_ref, stats_ref):
    gather_into(me_ref, parts, full_ref)
    mixed = full_ref[...].astype(f32).reshape(-1, full_ref.shape[2])
    average = jnp.mean(mixed, axis=0, keepdims=True)
    moved = mixed - average
    inverse = lax.rsqrt(jnp.mean(moved * moved, axis=0, keepdims=True) + epsilon)
    centred = moved * inverse
    stats_ref[0:1, :] = average
    stats_ref[1:2, :] = inverse
    normed = (centred * shape[0] + shape[1]).astype(bf16)
    normed_ref[...] = normed
    before = dot(weight_in_ref[0], normed, 0, 0) + bias_ref[...]
    square = before * before
    bend = jnp.tanh(root * before * (1.0 + cubic * square))
    half = 0.5 * (1.0 + bend)
    hidden_ref[...] = (before * half).astype(bf16)
    slope_ref[...] = (half + 0.5 * before * (1.0 - bend * bend) * root * (1.0 + 3.0 * cubic * square)).astype(slope_ref.dtype)
    return centred


def mlp_first_body(section, me_ref, own, near, far, cross, shape_own, shape_near, shape_far, shape_cross, weight_in_ref,
                   bias_ref, weight_out_ref,
                   send_far, send_own, keep_far, keep_own, normed_ref, hidden_ref, slope_ref, stats_ref, full_ref, sum_ref,
                   shape_ref):
    shape = gather_shape(me_ref, (shape_own, shape_near, shape_far, shape_cross), section, shape_ref)
    mlp_forward(me_ref, (own, near, far, cross), full_ref, shape, weight_in_ref, bias_ref,
                normed_ref, hidden_ref, slope_ref, stats_ref)
    partial_out = dot(weight_out_ref[0], hidden_ref[...], 0, 0)
    sum_ref[...] = partial_out.astype(bf16).reshape(sum_ref.shape)
    scatter_out(me_ref, sum_ref, (send_far, send_own, keep_far, keep_own))


def mlp_backward(me_ref, parts, full_ref, weight_out_ref, weight_in_ref, slope, gain, centred, sum_ref, outs, before_grad_ref):
    gather_into(me_ref, parts, full_ref)
    grad = full_ref[...].reshape(-1, full_ref.shape[2])
    before_grad = (dot(weight_out_ref[0], grad, 1, 0) * slope).astype(bf16)
    before_grad_ref[...] = before_grad
    normed_part = dot(weight_in_ref[0], before_grad, 1, 0)
    channels = sum_ref.shape[1] - 16
    scaled = normed_part * gain
    scaled_sum = jnp.sum(scaled, axis=0, keepdims=True)
    paired_sum = jnp.sum(scaled * centred, axis=0, keepdims=True)
    places = lax.broadcasted_iota(jnp.int32, (16, grad.shape[1]), 0)
    tail = jnp.where(places == 0, scaled_sum, jnp.where(places == 1, paired_sum, 0.0)).astype(bf16)
    for index in range(sum_ref.shape[0]):
        sum_ref[index, 0:channels, :] = normed_part[index * channels:(index + 1) * channels].astype(bf16)
        sum_ref[index, channels:, :] = tail
    scatter_out(me_ref, sum_ref, outs)


def mlp_top_body(section, me_ref, own, near, far, cross, grad_own, grad_near, grad_far, grad_cross,
                 shape_own, shape_near, shape_far, shape_cross, weight_in_ref, bias_ref, weight_out_ref,
                 back_sf, back_so, back_kf, back_ko, stats_ref, normed_ref, hidden_ref, before_grad_ref,
                 full_ref, back_ref, slope_ref, shape_ref):
    shape = gather_shape(me_ref, (shape_own, shape_near, shape_far, shape_cross), section, shape_ref)
    centred = mlp_forward(me_ref, (own, near, far, cross), full_ref, shape, weight_in_ref, bias_ref,
                          normed_ref, hidden_ref, slope_ref, stats_ref)
    mlp_backward(me_ref, (grad_own, grad_near, grad_far, grad_cross), full_ref, weight_out_ref, weight_in_ref,
                 slope_ref[...], shape[0], centred, back_ref, (back_sf, back_so, back_kf, back_ko), before_grad_ref)


def mlp_back_body(section, me_ref, own, near, far, cross, grad_own, grad_near, grad_far, grad_cross,
                  shape_own, shape_near, shape_far, shape_cross, weight_in_ref, weight_out_ref, slope_ref, stats_ref,
                  back_sf, back_so, back_kf, back_ko, before_grad_ref, full_ref, back_ref, shape_ref):
    shape = gather_shape(me_ref, (shape_own, shape_near, shape_far, shape_cross), section, shape_ref)
    gather_into(me_ref, (own, near, far, cross), full_ref)
    centred = (full_ref[...].astype(f32).reshape(-1, full_ref.shape[2]) - stats_ref[0:1, :]) * stats_ref[1:2, :]
    mlp_backward(me_ref, (grad_own, grad_near, grad_far, grad_cross), full_ref, weight_out_ref, weight_in_ref,
                 slope_ref[...].astype(f32), shape[0], centred, back_ref, (back_sf, back_so, back_kf, back_ko), before_grad_ref)


tile = 256


def pixel_block(rows):
    return pl.BlockSpec((rows, tile), lambda i: (0, i))


def fixed_block(shape):
    return pl.BlockSpec(shape, lambda i: (0,) * len(shape))


def section_block(section, shape):
    return pl.BlockSpec((1,) + shape, lambda i: (section, 0, 0))


def mlp_first(section, me, parts, shaping, weight_in, bias, weight_out):
    own = parts[0]
    channels, pixels = own.shape
    wide, units = weight_in.shape[1], weight_in.shape[2]
    piece = pixel_block(channels)
    return pl.pallas_call(
        partial(mlp_first_body, section),
        grid=(pixels // tile,),
        in_specs=[smem_spec()] + [piece] * 4 + [
            *[fixed_block(shaping[0].shape)] * 4, section_block(section, (wide, units)), fixed_block(bias.shape),
            section_block(section, (units, wide)),
        ],
        out_specs=[piece] * 4 + [pixel_block(wide), pixel_block(units), pixel_block(units), pixel_block(8)],
        out_shape=[struct(own.shape, bf16)] * 4 + [
            struct((wide, pixels), bf16), struct((units, pixels), bf16), struct((units, pixels), bf16), struct((8, pixels), f32),
        ],
        scratch_shapes=[
            pltpu.VMEM((4, channels, tile), bf16), pltpu.VMEM((4, channels, tile), bf16), pltpu.VMEM((4,) + shaping[0].shape, f32),
        ],
        name="mlp_first",
        **params(),
    )(me, *parts, *shaping, weight_in, bias, weight_out)


def mlp_top(section, me, parts, grads, shaping, weight_in, bias, weight_out):
    own = parts[0]
    channels, pixels = own.shape
    wide, units = weight_in.shape[1], weight_in.shape[2]
    piece, back = pixel_block(channels), pixel_block(channels + 16)
    return pl.pallas_call(
        partial(mlp_top_body, section),
        grid=(pixels // tile,),
        in_specs=[smem_spec()] + [piece] * 8 + [
            *[fixed_block(shaping[0].shape)] * 4, section_block(section, (wide, units)), fixed_block(bias.shape),
            section_block(section, (units, wide)),
        ],
        out_specs=[back] * 4 + [pixel_block(8), pixel_block(wide), pixel_block(units), pixel_block(units)],
        out_shape=[struct((channels + 16, pixels), bf16)] * 4 + [
            struct((8, pixels), f32), struct((wide, pixels), bf16), struct((units, pixels), bf16), struct((units, pixels), bf16),
        ],
        scratch_shapes=[
            pltpu.VMEM((4, channels, tile), bf16), pltpu.VMEM((4, channels + 16, tile), bf16),
            pltpu.VMEM((units, tile), f32), pltpu.VMEM((4,) + shaping[0].shape, f32),
        ],
        name="mlp_top",
        **params(),
    )(me, *parts, *grads, *shaping, weight_in, bias, weight_out)


def mlp_back(section, me, parts, grads, shaping, weight_in, weight_out, slope, stats, after):
    own = parts[0]
    channels, pixels = own.shape
    wide, units = weight_in.shape[1], weight_in.shape[2]
    piece, back = pixel_block(channels), pixel_block(channels + 16)
    given = 1 + 8 + 4 + 4

    def body(*refs):
        mlp_back_body(section, *refs[:given], *refs[given + len(after):])

    return pl.pallas_call(
        body,
        grid=(pixels // tile,),
        in_specs=[smem_spec()] + [piece] * 8 + [
            *[fixed_block(shaping[0].shape)] * 4, section_block(section, (wide, units)), section_block(section, (units, wide)),
            pixel_block(units), pixel_block(8), *[any_spec()] * len(after),
        ],
        out_specs=[back] * 4 + [pixel_block(units)],
        out_shape=[struct((channels + 16, pixels), bf16)] * 4 + [struct((units, pixels), bf16)],
        scratch_shapes=[
            pltpu.VMEM((4, channels, tile), bf16), pltpu.VMEM((4, channels + 16, tile), bf16),
            pltpu.VMEM((4,) + shaping[0].shape, f32),
        ],
        name="mlp_back",
        **params(),
    )(me, *parts, *grads, *shaping, weight_in, weight_out, slope, stats, *after)


def mlp_out_body(section, me_ref, hidden_ref, weight_out_ref, send_far, send_own, keep_far, keep_own, sum_ref):
    for at in range(0, hidden_ref.shape[1], tile):
        cut = slice(at, at + tile)
        value = dot(weight_out_ref[section], hidden_ref[:, cut], 0, 0).astype(bf16)
        sum_ref[:, :, cut] = value.reshape(sum_ref.shape[0], sum_ref.shape[1], tile)
    scatter_out(me_ref, sum_ref, (send_far, send_own, keep_far, keep_own))


def mlp_out(section, me, hidden, weight_out, after):
    wide, pixels = weight_out.shape[2], hidden.shape[1]
    piece = struct((wide // 4, pixels), bf16)
    return launch(
        partial(mlp_out_body, section), "mlp_out", [hidden, weight_out], [piece] * 4,
        [pltpu.VMEM((4, wide // 4, pixels), bf16)], scalars=[me], after=after,
    )


def put_halves(ref, at, outs):
    size = outs[0].shape[0]
    for side, out in zip((at, 1 - at), outs, strict=True):
        out[...] = ref[pl.ds(pl.multiple_of(side * size, size), size), :].astype(bf16)


def weights_body(me_ref, hidden_ref, grad_own, grad_near, grad_far, grad_cross, normed_ref, before_grad_ref,
                 keep, send, units_ref, full_ref, total_ref):
    units = hidden_ref.shape[0]
    gather_into(me_ref, (grad_own, grad_near, grad_far, grad_cross), full_ref)
    total_ref[0:units] = dot(hidden_ref[...], full_ref[...].reshape(-1, full_ref.shape[2]), 1, 1)
    before_grad = before_grad_ref[...]
    total_ref[units:] = dot(normed_ref[...], before_grad, 1, 1)
    units_ref[...] = jnp.broadcast_to(jnp.sum(before_grad.astype(f32), axis=1, keepdims=True), units_ref.shape)
    put_halves(total_ref, me_ref[2], (keep, send))


def weight_grads(me, hidden, grads, normed, before_grad, after=()):
    units, wide = hidden.shape[0], normed.shape[0]
    return launch(
        weights_body, "weight_grads", [hidden, *grads, normed, before_grad],
        [struct((units, wide), bf16)] * 2 + [struct((units, lane), f32)],
        [pltpu.VMEM((4,) + grads[0].shape, bf16), pltpu.VMEM((units + wide, wide), f32)], scalars=[me], after=after,
    )


def out_grad_body(me_ref, hidden_ref, grad_own, grad_near, grad_far, grad_cross, keep, send, full_ref, total_ref):
    gather_into(me_ref, (grad_own, grad_near, grad_far, grad_cross), full_ref)
    total_ref[...] = dot(hidden_ref[...], full_ref[...].reshape(-1, full_ref.shape[2]), 1, 1)
    put_halves(total_ref, me_ref[2], (keep, send))


def out_grad(me, hidden, grads, after=()):
    units, wide = hidden.shape[0], 4 * grads[0].shape[0]
    return launch(
        out_grad_body, "out_grad", [hidden, *grads], [struct((units // 2, wide), bf16)] * 2,
        [pltpu.VMEM((4,) + grads[0].shape, bf16), pltpu.VMEM((units, wide), f32)], scalars=[me], after=after,
    )


def in_grad_body(me_ref, normed_ref, before_grad_ref, keep, send, units_ref, total_ref):
    before_grad = before_grad_ref[...]
    total_ref[...] = dot(normed_ref[...], before_grad, 1, 1)
    put_halves(total_ref, me_ref[2], (keep, send))
    units_ref[...] = jnp.broadcast_to(jnp.sum(before_grad.astype(f32), axis=1, keepdims=True), units_ref.shape)


def in_grad(me, normed, before_grad, after=()):
    wide, units = normed.shape[0], before_grad.shape[0]
    return launch(
        in_grad_body, "in_grad", [normed, before_grad],
        [struct((wide // 2, units), bf16)] * 2 + [struct((units, lane), f32)],
        [pltpu.VMEM((wide, units), f32)], scalars=[me], after=after,
    )


def top_output_body(keep_ref, near_ref, far_ref, stream_ref, cotangent_ref, pack_ref, out_ref, sums_ref):
    bias, scale = pack_ref[:, 3:4], pack_ref[:, 4:5]
    total = jnp.zeros(scale.shape, f32)
    rows = stream_ref.shape[1]
    for canvas in range(stream_ref.shape[0]):
        for row in range(rows):
            at = (canvas * rows + row) * lane
            cut = slice(at, at + lane)
            branch = keep_ref[:, cut].astype(f32) + near_ref[:, cut].astype(f32) + far_ref[:, cut].astype(f32) + bias
            out_ref[canvas, row] = (stream_ref[canvas, row].astype(f32) + scale * branch).astype(bf16)
            total += jnp.sum(cotangent_ref[canvas, row].astype(f32) * branch, axis=1, keepdims=True)
    put_columns(sums_ref, [total])


def top_output(branches, stream, cotangent, pack, after):
    return launch(
        top_output_body, "top_output", [*branches, stream, cotangent, pack],
        [struct(stream.shape, bf16), struct((stream.shape[2], lane), f32)], after=after,
    )


core_pairs = [(i, i ^ 1) for i in range(4)]
chip_pairs = [(i, i ^ 2) for i in range(4)]


def gather_channels(own):
    far = lax.ppermute(own, "ch", chip_pairs)
    near = lax.ppermute(own, "ch", core_pairs)
    cross = lax.ppermute(far, "ch", core_pairs)
    return (own, near, far, cross)


def scatter_channels(send_far, send_own, keep_far, keep_own):
    near_far = lax.ppermute(send_far, "ch", core_pairs)
    near_own = lax.ppermute(send_own, "ch", core_pairs)
    onward = (keep_far.astype(f32) + near_far.astype(f32)).astype(bf16)
    far = lax.ppermute(onward, "ch", chip_pairs)
    return (keep_own, near_own, far), onward


def across_rows(value, flip):
    return lax.ppermute(value, "rows", [(i, i ^ flip) for i in range(8)])


def rows_sum(value):
    for flip in (1, 2, 4):
        value = (value.astype(f32) + across_rows(value, flip).astype(f32)).astype(bf16)
    return value


def total_of(refs):
    return sum(ref[...].astype(f32) for ref in refs)


def halve_body(bit, me_ref, keep_ref, near_ref, keep_out, send_out, total_ref):
    total_ref[...] = total_of((keep_ref, near_ref))
    put_halves(total_ref, me_ref[bit], (keep_out, send_out))


def halve(bit, me, keep, near, after, through=()):
    rows, columns = keep.shape
    return launch(
        partial(halve_body, bit), "halve", [keep, near], [struct((rows // 2, columns), bf16)] * 2,
        [pltpu.VMEM(keep.shape, f32)], scalars=[me], after=after, through=through,
    )


def pair_add_body(keep_ref, near_ref, out_ref):
    out_ref[...] = total_of((keep_ref, near_ref)).astype(bf16)


def pair_add(keep, near, after=(), through=()):
    got = launch(pair_add_body, "pair_add", [keep, near], [struct(keep.shape, bf16)], after=after, through=through)
    return got if through else got[0]


back_flips = ((4, 2, 1), (1, 4, 2))


def spread_back(total, flips):
    parts = [total]
    for flip in flips:
        parts += [across_rows(part, flip) for part in parts]
    return parts


def top_store(me, parts, after):
    size, columns = parts[0].shape

    def body(me_ref, *refs):
        outs = refs[-2:]

        def put(kept):
            for f, part in enumerate(refs[:8]):
                at = (me_ref[3] ^ (f >> 1 & 1)) * 2 + (me_ref[4] ^ (f & 1))
                outs[kept ^ (f >> 2)][0, pl.ds(pl.multiple_of(at * size, size), size), :] = part[...].astype(f32)

        @pl.when(me_ref[2] == 0)
        def _():
            put(0)

        @pl.when(me_ref[2] == 1)
        def _():
            put(1)

    return pl.pallas_call(
        body,
        grid=(1,),
        in_specs=[smem_spec()] + [pl.BlockSpec(part.shape, lambda i: (0, 0)) for part in parts] + [any_spec()] * len(after),
        out_specs=[pl.BlockSpec((1, 4 * size, columns), lambda i: (1, 0, 0))] * 2,
        out_shape=[struct((2, 4 * size, columns), f32)] * 2,
        name="top_store",
        **params(),
    )(me, *parts, *after)


def finish(flips, me, held, parts, after=()):
    size, columns = parts[0].shape
    block = pl.BlockSpec((1,) + held.shape[1:], lambda i: (0, 0, 0))

    def body(me_ref, *refs):
        out = refs[-1]
        for f, part in enumerate(refs[:8]):
            flipped = sum(flip for bit, flip in enumerate(flips) if f >> bit & 1)
            at = (me_ref[2] ^ (flipped & 1)) * 4 + (me_ref[3] ^ (flipped >> 1 & 1)) * 2 + (me_ref[4] ^ (flipped >> 2))
            out[0, pl.ds(pl.multiple_of(at * size, size), size), :] = part[...].astype(f32)

    return pl.pallas_call(
        body,
        grid=(1,),
        in_specs=[smem_spec()] + [pl.BlockSpec(part.shape, lambda i: (0, 0)) for part in parts]
        + [any_spec()] * (1 + len(after)),
        out_specs=block,
        out_shape=struct(held.shape, f32),
        input_output_aliases={1 + len(parts): 0},
        name="finish",
        **params(),
    )(me, *parts, held, *after)


def exchange(pieces):
    return lax.all_to_all(pieces, "rows", split_axis=0, concat_axis=0, tiled=True)


def rows_to_cols(packed, moving, count, picture):
    if packed:
        return [exchange(moving[0])]
    canvases, rows, channels, width = picture
    pieces = []
    for part in moving:
        cut = part.reshape(canvases, rows, channels, count, width // count)
        pieces.append(cut.transpose(3, 2, 0, 1, 4).reshape(count, channels, -1))
    moved = exchange(jnp.stack(pieces, axis=1))
    moved = moved.reshape(count, len(moving), channels, canvases, rows, width // count)
    return [moved[:, k].transpose(1, 2, 0, 3, 4).reshape(channels, -1) for k in range(len(moving))]


def cols_to_rows(packed, moving, count, picture):
    if packed:
        return [exchange(moving[0])]
    canvases, rows, channels, width = picture
    pieces = []
    for part in moving:
        cut = part.reshape(channels, canvases, count, rows, width // count)
        pieces.append(cut.transpose(2, 0, 1, 3, 4).reshape(count, channels, -1))
    moved = exchange(jnp.stack(pieces, axis=1))
    moved = moved.reshape(count, len(moving), channels, canvases, rows, width // count)
    return [moved[:, k].transpose(2, 3, 1, 0, 4).reshape(picture) for k in range(len(moving))]


def crop_reach(starts):
    count = starts.shape[1]
    places = jnp.arange(count, dtype=jnp.int32)
    here, there = places[None, :, None], places[None, None, :]
    begins = starts[:, None, :] > 0
    first = jnp.max(jnp.where(begins & (there <= here), there, 0), axis=2)
    following = jnp.min(jnp.where(begins & (there > here), there, count), axis=2)
    return places[None, :] - first, following - 1 - places[None, :]


def band_turns(age):
    return jnp.max(age.reshape(age.shape[0], -1, band), axis=2) // ahead + 1


def on_device(
    count,
    pixels,
    row_starts,
    col_starts,
    log_step,
    log_decay,
    frequency,
    coef_real,
    coef_imag,
    skip_gain,
    norm_gain,
    norm_shift,
    weight_in,
    bias_in,
    weight_out,
    bias_out,
    layer_scale,
    cotangent,
):
    canvases, rows, width, channels = pixels.shape
    height = row_starts.shape[1]
    channels_all = weight_in.shape[1]
    lengths = (height, width)
    picture = (canvases, rows, channels, width)
    cols = (channels, canvases * height * (width // count))
    eight = count == 8
    packed = eight and picture == (2, 2, 2 * half_rows, lane)
    place = lax.axis_index("rows")
    bits = [place % 2, place // 2 % 2, place // 4] if eight else [0 * place] * 3
    me = jnp.stack([lax.axis_index("ch"), place, *bits]).astype(jnp.int32)

    stream = jnp.swapaxes(pixels, 2, 3)
    upstream = jnp.swapaxes(cotangent, 2, 3)
    states = [jnp.swapaxes(value, 2, 3) for value in (log_decay, frequency, coef_real, coef_imag)]

    age, fore = crop_reach(col_starts)
    age_reach, fore_reach = band_turns(age), band_turns(fore)
    age = jnp.broadcast_to(age[:, :, None], (canvases, width, lane))
    fore = jnp.broadcast_to(fore[:, :, None], (canvases, width, lane))
    row_age, row_fore = crop_reach(row_starts)
    row_age = jnp.repeat(row_age, width // count, axis=1)[:, None, :]
    row_fore = jnp.repeat(row_fore, width // count, axis=1)[:, None, :]

    packs = [
        jnp.stack([skip_gain[k], norm_gain[k], norm_shift[k], bias_out[k], layer_scale[k]], axis=1) for k in range(2)
    ]
    shaping = gather_channels(jnp.stack([norm_gain[0], norm_shift[0], norm_gain[1], norm_shift[1]], axis=1))
    bias_columns = [bias_in[k][:, None] for k in range(2)]

    wide_low = s4_wide(0, width, rows, log_step, *states)
    across = wide_forward(packed, stream, wide_low, age, age_reach)
    tall_low, tall_top, wide_top, top_scaled, top_bias_sums = s4_rest(
        lengths, rows, log_step, states, upstream, packs[1], [across]
    )
    moved = rows_to_cols(packed, [across] if packed else [across, stream], count, picture)
    mixed_low, across_cols, stream_cols = tall_mixed(packed, height, moved, cols, tall_low, row_age, packs[0])
    low_parts = gather_channels(mixed_low)
    first = mlp_first(0, me, low_parts, shaping, weight_in, bias_columns[0], weight_out)
    normed_low, hidden_low, slope_low, stats_low = first[4:]
    branches, _ = scatter_channels(*first[:4])
    top_parts = gather_channels(top_scaled)

    next_cols, branch_cols, moving = tall_next(packed, height, branches, stream_cols, packs[0], tall_top, row_age)
    moved = cols_to_rows(packed, moving, count, picture)
    mixed_top, tall_rows, next_rows = wide_mixed(packed, moved, picture, wide_top, age, age_reach, packs[1])
    top_mixed_parts = gather_channels(mixed_top)
    top = mlp_top(1, me, top_mixed_parts, top_parts, shaping, weight_in, bias_columns[1], weight_out)
    stats_top, normed_top, hidden_top, before_grad_top = top[4:]
    top_grads, onward = scatter_channels(*top[:4])
    top_keep, top_send, top_units = weight_grads(me, hidden_top, top_parts, normed_top, before_grad_top, [onward])
    top_weights = [top_keep, top_send]

    moving, grad_rows, top_sums = wide_norm_back(
        packed, channels_all, top_grads, mixed_top, stats_top, packs[1], next_rows, upstream, wide_top, fore, fore_reach,
        [top_send],
    )
    top_partials = mlp_out(1, me, hidden_top, weight_out, moving[:1])
    top_wide = wide_top_grad(grad_rows, tall_rows, age, age_reach, top_partials[:1])
    moved = rows_to_cols(packed, moving, count, picture)
    grad_cols, grad_low, conv_cols, top_send = tall_back(
        packed, height, moved, cols, tall_top, row_fore, packs[0], branch_cols, [top_wide], [top_send]
    )

    grad_parts = gather_channels(grad_low)
    *back, before_grad_low = mlp_back(
        0, me, low_parts, grad_parts, shaping, weight_in, weight_out, slope_low, stats_low, []
    )
    low_grads, onward = scatter_channels(*back)
    out_keep, out_send = out_grad(me, hidden_low, grad_parts, [onward])
    if eight:
        top_keep, top_send = halve(3, me, top_keep, across_rows(top_send, 1), [out_send])
        top_near = across_rows(top_send, 2)
    in_keep, in_send, low_units = in_grad(me, normed_low, before_grad_low, [top_send])
    if eight:
        out_near, in_near = across_rows(out_send, 1), across_rows(in_send, 1)
    moving, low_grad_cols, low_sums = tall_norm_back(
        packed, height, channels_all, low_grads, mixed_low, stats_low, packs[0], stream_cols, grad_cols, tall_low, row_fore,
        [in_send],
    )
    if eight:
        out_keep, out_send = halve(3, me, out_keep, out_near, [moving[0]])
        out_near = across_rows(out_send, 2)
        top_keep, top_send = halve(4, me, top_keep, top_near, [out_send])
        top_near = across_rows(top_send, 4)
    top_branches, _ = scatter_channels(*top_partials)
    activations, top_scale_sums = top_output(top_branches, next_rows, upstream, packs[1], [top_send])
    held = tall_low_grad(
        height, low_grad_cols, across_cols, row_age, low_sums, grad_cols, branch_cols, packs[0], top_scale_sums, low_units,
        [out_keep],
    )
    if eight:
        out_keep, out_send = halve(4, me, out_keep, out_near, [held])
        out_near = across_rows(out_send, 4)
        in_keep, in_send = halve(3, me, in_keep, in_near, [out_send])
        in_near = across_rows(in_send, 2)
        top_total = pair_add(top_keep, top_near, [in_send])
        top_weights = spread_back(top_total, back_flips[0])
    top_small = tall_top_grad(
        height, conv_cols, next_cols, row_age, top_wide, top_sums, top_bias_sums, top_units, [top_total] if eight else [held]
    )
    if eight:
        out_total = pair_add(out_keep, out_near, [top_small])
        out_parts = spread_back(out_total, back_flips[0])
    moved = cols_to_rows(packed, moving, count, picture)
    pixels_grad, small = wide_last(
        packed, moved, picture, stream, wide_low, age, fore, held, top_small, age_reach, fore_reach, [out_total] if eight else []
    )
    if eight:
        in_keep, in_send = halve(4, me, in_keep, in_near, [small])
        in_total = pair_add(in_keep, across_rows(in_send, 4), [in_send])
        in_parts = spread_back(in_total, back_flips[1])
        out_grads, in_grads = top_store(me, top_weights, [in_total])
        out_grads = finish(back_flips[0], me, out_grads, out_parts)
        small = rows_sum(small)
    else:
        small = lax.psum(small.astype(f32), "rows").astype(bf16)
    gradients = s4_pullback(lengths, weight_in.shape[2], small, log_step, *states, [out_grads] if eight else [])
    step_grad, decay_grad, freq_grad, real_grad, imag_grad, skip_grad, gain_grad, shift_grad, units_grad, bias_grad, scale_grad = gradients
    if eight:
        in_grads = finish(back_flips[1], me, in_grads, in_parts, [step_grad])
    else:
        low_weights = lax.psum((out_keep, out_send, in_keep, in_send), "rows")
        top_weights = lax.psum(tuple(top_weights), "rows")
        out_grads = jnp.stack([jnp.concatenate(low_weights[:2]), top_weights[0]]).astype(f32)
        in_grads = jnp.stack([jnp.concatenate(low_weights[2:]), top_weights[1]]).astype(f32)
    return (
        jnp.swapaxes(activations, 2, 3),
        jnp.swapaxes(pixels_grad, 2, 3),
        step_grad,
        jnp.swapaxes(decay_grad, 2, 3),
        jnp.swapaxes(freq_grad, 2, 3),
        jnp.swapaxes(real_grad, 2, 3),
        jnp.swapaxes(imag_grad, 2, 3),
        skip_grad,
        gain_grad,
        shift_grad,
        in_grads,
        units_grad,
        out_grads,
        bias_grad,
        scale_grad,
    )


def solution(mesh):
    picture = P(None, "rows", None, "ch")
    state = P(None, None, "ch", None)
    step = P(None, None, "ch")
    vector = P(None, "ch")
    into = P(None, None, "ch")
    out = P(None, "ch", None)
    in_specs = (
        picture, P(), P(), step, state, state, state, state, vector, vector, vector, into, vector, out, vector, vector, picture,
    )
    out_specs = (
        picture, picture, step, state, state, state, state, vector, vector, vector, into, vector, out, vector, vector,
    )
    return jax.shard_map(
        partial(on_device, mesh.shape["rows"]), mesh=mesh, in_specs=in_specs, out_specs=out_specs, check_vma=False
    )
```

```python
from functools import partial

import jax
import jax.numpy as jnp
from jax import lax
from jax.experimental import pallas as pl
from jax.experimental.pallas import tpu as pltpu
from jax.sharding import PartitionSpec as P


epsilon = 1e-06
bf16 = jnp.bfloat16
f32 = jnp.float32
vmem_bytes = 52 * 1024 * 1024
ahead = 8
band = 16
lane = 128


def dot(a, b, ca, cb):
    return lax.dot_general(a, b, (((ca,), (cb,)), ((), ())), preferred_element_type=f32)


def vmem_spec():
    return pl.BlockSpec(memory_space=pltpu.VMEM)


def smem_spec():
    return pl.BlockSpec(memory_space=pltpu.SMEM)


def any_spec():
    return pl.BlockSpec(memory_space=pl.ANY)


def struct(shape, dtype):
    return jax.ShapeDtypeStruct(shape, dtype)


def params():
    return dict(
        compiler_params=pltpu.CompilerParams(vmem_limit_bytes=vmem_bytes),
        cost_estimate=pl.CostEstimate(flops=1, bytes_accessed=1, transcendentals=0),
    )


def launch(body, name, ins, outs, scratch=(), scalars=(), after=(), through=()):
    given, kept = len(scalars) + len(ins), len(after) + len(through)

    def run(*refs):
        body(*refs[:given], *refs[given + kept:given + kept + len(outs)], *refs[given + kept + len(outs) + len(through):])

    return pl.pallas_call(
        run,
        in_specs=[smem_spec()] * len(scalars) + [vmem_spec()] * len(ins) + [any_spec()] * kept,
        out_specs=[vmem_spec()] * len(outs) + [any_spec()] * len(through),
        out_shape=list(outs) + [struct(value.shape, value.dtype) for value in through],
        scratch_shapes=list(scratch),
        input_output_aliases={given + len(after) + k: len(outs) + k for k in range(len(through))},
        name=name,
        **params(),
    )(*scalars, *ins, *after, *through)


def swap(parts, number, chunk):
    width = 16 << chunk
    lanes = lax.broadcasted_iota(jnp.int32, parts[0].shape, 1)
    low = (lanes // width) % 2 == 0
    parts = list(parts)
    for i in range(8):
        j = i | (1 << number)
        if i != j:
            a, b = parts[i], parts[j]
            parts[i] = jnp.where(low, a, pltpu.roll(b, width, 1))
            parts[j] = jnp.where(low, pltpu.roll(a, lane - width, 1), b)
    return parts


half_rows = 96
strip = 32


def pieces_from_rows(get, out_ref, kind):
    for at in range(0, half_rows, strip):
        parts = [get((i >> 1) & 1, i & 1, slice((i >> 2) * half_rows + at, (i >> 2) * half_rows + at + strip)) for i in range(8)]
        for bit in range(3):
            parts = swap(parts, bit, bit)
        for target in range(8):
            out_ref[target, kind, at:at + strip, :] = parts[target].astype(bf16)


def rows_from_pieces(in_ref, kind, put):
    for at in range(0, half_rows, strip):
        parts = [in_ref[source, kind, at:at + strip, :].astype(f32) for source in range(8)]
        for bit in range(3):
            parts = swap(parts, bit, bit)
        for i in range(8):
            put((i >> 1) & 1, i & 1, slice((i >> 2) * half_rows + at, (i >> 2) * half_rows + at + strip), parts[i])


def pieces_from_cols(get, out_ref, kind):
    for at in range(0, half_rows, strip):
        parts = []
        for i in range(8):
            upper, half, canvas = i >> 2, (i >> 1) & 1, i & 1
            first = (canvas * 2 + upper) * lane
            parts.append(get(slice(half * half_rows + at, half * half_rows + at + strip), slice(first, first + lane)))
        parts = swap(swap(parts, 1, 2), 0, 1)
        for target in range(8):
            out_ref[target, kind, at:at + strip, :] = parts[target].astype(bf16)


def cols_from_pieces(in_ref, kind, out_ref):
    for at in range(0, half_rows, strip):
        parts = [in_ref[source, kind, at:at + strip, :].astype(f32) for source in range(8)]
        parts = swap(swap(parts, 1, 2), 0, 1)
        for i in range(8):
            upper, half, canvas = i >> 2, (i >> 1) & 1, i & 1
            first = (canvas * 2 + upper) * lane
            out_ref[half * half_rows + at:half * half_rows + at + strip, first:first + lane] = parts[i].astype(out_ref.dtype)


def piece_shape(kinds):
    return struct((8, kinds, half_rows, lane), bf16)


def state_powers(step, decay, frequency):
    size = jnp.exp(-step * decay)
    turn = step * frequency
    z = (size * jnp.cos(turn), size * jnp.sin(turn))

    def times(p, q):
        return (p[0] * q[0] - p[1] * q[1], p[0] * q[1] + p[1] * q[0])

    z2 = times(z, z)
    z3 = times(z2, z)
    z4 = times(z2, z2)
    return [None, z, z2, z3, z4, times(z4, z), times(z4, z2), times(z4, z3)], times(z4, z4), times


def pack_lanes(value):
    half = value.shape[0] // 2
    return jnp.concatenate([value[:half], value[half:]], axis=1)


def unpack_lanes(value):
    half = value.shape[1] // 2
    return jnp.concatenate([value[:, :half], value[:, half:]], axis=0)


def s4_section(direction, length, section, step_ref, decay_ref, freq_ref, real_ref, imag_ref, q_ref, flat_ref):
    channels = step_ref.shape[2]
    step = jnp.exp(step_ref[section, direction:direction + 1, :])
    step = jnp.concatenate([step, step], axis=1)
    decay = jnp.exp(pack_lanes(decay_ref[section, direction]))
    powers, z8, times = state_powers(step, decay, pack_lanes(freq_ref[section, direction]))
    for a in range(1, ahead):
        q_ref[2 * a] = powers[a][0]
        q_ref[2 * a + 1] = powers[a][1]
    q_ref[0] = z8[0]
    q_ref[1] = z8[1]

    def block(b, carry):
        pr, pi = carry
        rows = [jnp.sum(pr, axis=0, keepdims=True)]
        for a in range(1, ahead):
            rows.append(jnp.sum(pr * q_ref[2 * a] - pi * q_ref[2 * a + 1], axis=0, keepdims=True))
        flat_ref[pl.ds(pl.multiple_of(b * ahead, ahead), ahead), :] = step * jnp.concatenate(rows, axis=0)
        zr, zi = q_ref[0], q_ref[1]
        return (pr * zr - pi * zi, pr * zi + pi * zr)

    start = (pack_lanes(real_ref[section, direction]), pack_lanes(imag_ref[section, direction]))
    lax.fori_loop(0, length // ahead, block, start)
    flat = jnp.transpose(flat_ref[...])
    return (flat[:channels] + flat[channels:]).astype(bf16).astype(f32)


def s4_scratch(states, channels):
    return [pltpu.VMEM((2 * ahead, states // 2, 2 * channels), f32), pltpu.VMEM((lane, 2 * channels), f32)]


def s4_wide_body(length, section, copies, step_ref, decay_ref, freq_ref, real_ref, imag_ref, out_ref, q_ref, flat_ref):
    kernel = s4_section(1, length, section, step_ref, decay_ref, freq_ref, real_ref, imag_ref, q_ref, flat_ref)
    out_ref[...] = jnp.transpose(jnp.concatenate([kernel] * copies, axis=0))


def s4_wide(section, length, copies, log_step, *states):
    channels = states[0].shape[3]
    return launch(
        partial(s4_wide_body, length, section, copies), "s4_wide", [log_step, *states],
        [struct((lane, copies * channels), f32)], s4_scratch(states[0].shape[2], channels),
    )[0]


def s4_rest_body(lengths, copies, step_ref, decay_ref, freq_ref, real_ref, imag_ref, upstream_ref, pack_ref,
                 tall_low, tall_top, wide_top, scaled_ref, sums_ref, q_ref, flat_ref):
    refs = (step_ref, decay_ref, freq_ref, real_ref, imag_ref, q_ref, flat_ref)
    tall_low[...] = s4_section(0, lengths[0], 0, *refs)
    tall_top[...] = s4_section(0, lengths[0], 1, *refs)
    wide_top[...] = jnp.transpose(jnp.concatenate([s4_section(1, lengths[1], 1, *refs)] * copies, axis=0))
    scale = pack_ref[:, 4:5]
    total = jnp.zeros(scale.shape, f32)
    rows = upstream_ref.shape[1]
    for canvas in range(upstream_ref.shape[0]):
        for row in range(rows):
            scaled = upstream_ref[canvas, row].astype(f32) * scale
            at = (canvas * rows + row) * lane
            scaled_ref[:, at:at + lane] = scaled.astype(bf16)
            total += jnp.sum(scaled, axis=1, keepdims=True)
    put_columns(sums_ref, [total])


def s4_rest(lengths, copies, log_step, states, upstream, pack, after):
    channels = states[0].shape[3]
    pixels = upstream.shape[0] * upstream.shape[1] * lane
    column = struct((channels, lane), f32)
    return launch(
        partial(s4_rest_body, lengths, copies), "s4_rest", [log_step, *states, upstream, pack],
        [column, column, struct((lane, copies * channels), f32), struct((channels, pixels), bf16), column],
        s4_scratch(states[0].shape[2], channels), after=after,
    )


def pull_section(direction, length, grads_ref, step_ref, decay_ref, freq_ref, real_ref, imag_ref,
                 dstep_ref, ddecay_ref, dfreq_ref, dreal_ref, dimag_ref, turn_ref, spread_ref, q_ref, s_ref):
    channels = step_ref.shape[2]
    states = decay_ref.shape[2]
    tiles = 2 * channels // lane
    step = jnp.exp(step_ref[0, direction:direction + 1, :])
    decay = jnp.exp(decay_ref[0, direction])
    freq = freq_ref[0, direction]
    wide_step = jnp.concatenate([step, step], axis=1)
    powers, z8, times = state_powers(wide_step, pack_lanes(decay), pack_lanes(freq))
    for a in range(ahead):
        for part in range(2):
            value = (z8 if a == 0 else powers[a])[part]
            for t in range(tiles):
                q_ref[2 * a + part, t] = value[:, t * lane:(t + 1) * lane]
    first = (1 - direction) * lane
    grads = grads_ref[0, :, first:first + lane].astype(f32)
    turn_ref[0:channels, :] = grads
    turn_ref[channels:2 * channels, :] = grads
    flat = jnp.transpose(turn_ref[...])
    for place in range(length):
        for t in range(tiles):
            spread_ref[t, place] = jnp.broadcast_to(flat[place:place + 1, t * lane:(t + 1) * lane], (8, lane))
    turns = length // ahead
    groups = states // 16

    def group(index, carry):
        t = index // groups
        part = pl.ds(pl.multiple_of(lax.rem(index, groups) * 8, 8), 8)
        q = [(q_ref[2 * a, t, part, :], q_ref[2 * a + 1, t, part, :]) for a in range(ahead)]
        zr, zi = q[0]

        def block(turn, sums):
            s0r, s0i, s1r, s1i = sums
            b = turns - 1 - turn
            t0r = t0i = t1r = t1i = None
            for a in range(ahead - 1, 0, -1):
                g = spread_ref[t, b * ahead + a]
                x, y = g * q[a][0], g * q[a][1]
                t0r, t0i = (x, y) if t0r is None else (t0r + x, t0i + y)
                t1r, t1i = (t0r, t0i) if t1r is None else (t1r + t0r, t1i + t0i)
            t0r = t0r + spread_ref[t, b * ahead]
            base = (b * ahead).astype(f32)
            v1r, v1i = t1r + base * t0r, t1i + base * t0i
            return (
                s0r * zr - s0i * zi + t0r,
                s0r * zi + s0i * zr + t0i,
                s1r * zr - s1i * zi + v1r,
                s1r * zi + s1i * zr + v1i,
            )

        zero = jnp.zeros((8, lane), f32)
        sums = lax.fori_loop(0, turns, block, (zero, zero, zero, zero))
        for k in range(4):
            s_ref[k, t, part, :] = sums[k]
        return carry

    lax.fori_loop(0, tiles * groups, group, 0)
    s0r, s0i, s1r, s1i = [
        unpack_lanes(jnp.concatenate([s_ref[k, t] for t in range(tiles)], axis=1)) for k in range(4)
    ]
    real, imag = real_ref[0, direction], imag_ref[0, direction]
    dreal = step * s0r
    dimag = -step * s0i
    ddecay = -step * step * decay * (real * s1r - imag * s1i)
    dfreq = -step * step * (real * s1i + imag * s1r)
    dreal_ref[0, direction] = dreal
    dimag_ref[0, direction] = dimag
    ddecay_ref[0, direction] = ddecay
    dfreq_ref[0, direction] = dfreq
    dstep_ref[0, direction:direction + 1, :] = jnp.sum(
        real * dreal + imag * dimag + ddecay + freq * dfreq, axis=0, keepdims=True
    )
    return flat


def pull_body(lengths, grads_ref, step_ref, decay_ref, freq_ref, real_ref, imag_ref, dstep_ref, ddecay_ref, dfreq_ref, dreal_ref,
              dimag_ref, skip_ref, gain_ref, shift_ref, units_ref, bias_ref, scale_ref, *scratch):
    channels = step_ref.shape[2]
    refs = (grads_ref, step_ref, decay_ref, freq_ref, real_ref, imag_ref, dstep_ref, ddecay_ref, dfreq_ref, dreal_ref, dimag_ref)
    pull_section(1, lengths[1], *refs, *scratch)
    rows = pull_section(0, lengths[0], *refs, *scratch)
    first = lengths[0]
    if first + 16 > lane:
        turn_ref = scratch[0]
        turn_ref[0:channels, :] = grads_ref[0, :, 2 * lane:].astype(f32)
        rows, first = jnp.transpose(turn_ref[...]), first - lane
    per = units_ref.shape[1] // channels
    section = pl.program_id(0)

    def row(index):
        return rows[first + index:first + index + 1, 0:channels]

    def put(at):
        for index, ref in enumerate((skip_ref, gain_ref, shift_ref, bias_ref)):
            ref[at:at + 1, :] = row(index)
        units_ref[at:at + 1, :] = jnp.concatenate([row(4 + index) for index in range(per)], axis=1)

    @pl.when(section == 0)
    def _():
        put(0)
        scale_ref[0:1, :] = row(4 + per)
        scale_ref[1:2, :] = row(5 + per)

    @pl.when(section == 1)
    def _():
        put(1)


def s4_pullback(lengths, units, grads, log_step, log_decay, frequency, coef_real, coef_imag, after):
    states, channels = log_decay.shape[2], log_decay.shape[3]
    whole = pl.BlockSpec((1, 2, states, channels), lambda i: (i, 0, 0, 0))
    row = pl.BlockSpec((1, 2, channels), lambda i: (i, 0, 0))
    tiles = 2 * channels // lane
    vectors = [(2, channels)] * 3 + [(2, units)] + [(2, channels)] * 2

    def body(*refs):
        pull_body(lengths, *refs[:6], *refs[6 + len(after):])

    return pl.pallas_call(
        body,
        grid=(2,),
        in_specs=[pl.BlockSpec((1,) + grads.shape[1:], lambda i: (i, 0, 0)), row, whole, whole, whole, whole]
        + [any_spec()] * len(after),
        out_specs=[row, whole, whole, whole, whole] + [pl.BlockSpec(shape, lambda i: (0, 0)) for shape in vectors],
        out_shape=[struct(log_step.shape, f32)] + [struct(log_decay.shape, f32)] * 4 + [struct(shape, f32) for shape in vectors],
        scratch_shapes=[
            pltpu.VMEM((2 * channels, lane), f32),
            pltpu.VMEM((tiles, lane, 8, lane), f32),
            pltpu.VMEM((2 * ahead, tiles, states // 2, lane), f32),
            pltpu.VMEM((4, tiles, states // 2, lane), f32),
        ],
        name="s4_pullback",
        **params(),
    )(grads, log_step, log_decay, frequency, coef_real, coef_imag, *after)


pad = 8


def lane_tiles(value):
    return [value[:, at:at + lane] for at in range(0, value.shape[1], lane)]


def load_tiles(value, ref, first):
    for index, part in enumerate(lane_tiles(value)):
        ref[index, first:first + part.shape[0], :] = part


def width_conv(canvas, sign, signal_ref, kernel_ref, age_ref, reach_ref, out_ref):
    tiles, width = out_ref.shape[0], out_ref.shape[1]
    per = band // 8
    for index in range(width // band):
        ages = [age_ref[canvas, pl.ds((index * per + k) * 8, 8), :] for k in range(per)]

        def body(q, sums):
            sums = list(sums)
            places = [
                pl.multiple_of(jnp.clip(index * per + k - sign * q, 0, width // 8 - 1) * 8, 8) for k in range(per)
            ]
            for s in range(ahead):
                lag = q * ahead + s
                seen = [ages[k] >= lag for k in range(per)]
                for t in range(tiles):
                    value = jnp.broadcast_to(kernel_ref[t, pl.ds(lag, 1), :], (8, lane))
                    for k in range(per):
                        x = signal_ref[t, pl.ds(places[k] + (pad - sign * s), 8), :]
                        sums[k * tiles + t] += value * jnp.where(seen[k], x, 0.0)
            return tuple(sums)

        zero = jnp.zeros((8, lane), f32)
        sums = lax.fori_loop(0, reach_ref[canvas, index], body, (zero,) * (per * tiles))
        for k in range(per):
            for t in range(tiles):
                out_ref[t, pl.ds((index * per + k) * 8, 8), :] = sums[k * tiles + t]


def width_products(canvas, signal_ref, grad_ref, age_ref, reach_ref, total_ref):
    tiles, width = grad_ref.shape[0], grad_ref.shape[1]
    per = band // 8
    for index in range(width // band):
        ages = [age_ref[canvas, pl.ds((index * per + k) * 8, 8), :] for k in range(per)]
        grads = [[grad_ref[t, pl.ds((index * per + k) * 8, 8), :] for t in range(tiles)] for k in range(per)]

        def body(q, carry):
            places = [
                pl.multiple_of(jnp.clip(index * per + k - q, 0, width // 8 - 1) * 8, 8) for k in range(per)
            ]
            for s in range(ahead):
                lag = q * ahead + s
                seen = [ages[k] >= lag for k in range(per)]
                for t in range(tiles):
                    total = total_ref[t, lag]
                    for k in range(per):
                        x = signal_ref[t, pl.ds(places[k] + (pad - s), 8), :]
                        total += grads[k][t] * jnp.where(seen[k], x, 0.0)
                    total_ref[t, lag] = total
            return carry

        lax.fori_loop(0, reach_ref[canvas, index], body, 0)


def stacked_rows(ref, canvas):
    picture = ref[canvas].astype(f32)
    return jnp.transpose(picture.reshape(-1, picture.shape[2]))


def unstacked(ref, rows):
    flat = jnp.concatenate([jnp.transpose(ref[t]) for t in range(ref.shape[0])], axis=0)
    return flat.reshape(rows, flat.shape[0] // rows, flat.shape[1])


def width_scratch(rows, channels):
    tiles = rows * channels // lane
    return [
        pltpu.VMEM((tiles, lane + 2 * pad, lane), f32),
        pltpu.VMEM((tiles, lane, lane), f32),
        pltpu.VMEM((tiles, lane, lane), f32),
    ]


def convolve_canvas(canvas, sign, picture_ref, age_ref, reach_ref, signal_ref, kernel_ref, sum_ref):
    load_tiles(stacked_rows(picture_ref, canvas), signal_ref, pad)
    width_conv(canvas, sign, signal_ref, kernel_ref, age_ref, reach_ref, sum_ref)
    return unstacked(sum_ref, picture_ref.shape[1])


def wide_forward_body(packed, reach_ref, picture_ref, wide_ref, age_ref, out_ref, signal_ref, kernel_ref, sum_ref, *held):
    load_tiles(wide_ref[...], kernel_ref, 0)
    across_ref = held[0] if packed else out_ref
    for canvas in range(picture_ref.shape[0]):
        across_ref[canvas] = convolve_canvas(
            canvas, 1, picture_ref, age_ref, reach_ref, signal_ref, kernel_ref, sum_ref
        ).astype(across_ref.dtype)
    if packed:
        pieces_from_rows(lambda b, r, c: across_ref[b, r, c, :], out_ref, 0)
        pieces_from_rows(lambda b, r, c: picture_ref[b, r, c, :].astype(f32), out_ref, 1)


def wide_forward(packed, picture, wide, age, reach):
    out = piece_shape(2) if packed else struct(picture.shape, bf16)
    scratch = width_scratch(picture.shape[1], picture.shape[2])
    return launch(
        partial(wide_forward_body, packed), "wide_forward", [picture, wide, age], [out],
        scratch + [pltpu.VMEM(picture.shape, f32)] * packed, scalars=[reach],
    )[0]


def split_refs(packed, refs, held):
    return (refs[0], refs[1:]) if packed else (refs[:held], refs[held:])


def wide_mixed_body(packed, reach_ref, *refs):
    if packed:
        pieces, wide_ref, age_ref, pack_ref, out_ref, tall_ref, stream_ref, signal_ref, kernel_ref, sum_ref = refs
        for kind, ref in enumerate((tall_ref, stream_ref)):
            def put(b, r, c, value, ref=ref):
                ref[b, r, c, :] = value.astype(bf16)
            rows_from_pieces(pieces, kind, put)
    else:
        tall_ref, stream_ref, wide_ref, age_ref, pack_ref, out_ref, signal_ref, kernel_ref, sum_ref = refs
    rows = tall_ref.shape[1]
    skip = pack_ref[:, 0:1]
    load_tiles(wide_ref[...], kernel_ref, 0)
    for canvas in range(tall_ref.shape[0]):
        mixer = convolve_canvas(canvas, 1, tall_ref, age_ref, reach_ref, signal_ref, kernel_ref, sum_ref)
        for row in range(rows):
            at = (canvas * rows + row) * lane
            out_ref[:, at:at + lane] = (
                mixer[row] + skip * stream_ref[canvas, row].astype(f32)
            ).astype(bf16)


def wide_mixed(packed, moved, picture, wide, age, reach, pack):
    canvases, rows, channels, width = picture
    outs = [struct((channels, canvases * rows * lane), bf16)] + [struct(picture, bf16)] * (2 * packed)
    got = launch(
        partial(wide_mixed_body, packed), "wide_mixed", [*moved, wide, age, pack], outs,
        width_scratch(rows, channels), scalars=[reach],
    )
    return tuple(got) if packed else (got[0], *moved)


def norm_backward(grads, mixed_ref, stats_ref, pack_ref, channels_all):
    channels = mixed_ref.shape[0]
    keep, near, far = grads
    total = keep[...].astype(f32) + near[...].astype(f32) + far[...].astype(f32)
    normed_grad = total[0:channels]
    scaled_mean = total[channels:channels + 1] / channels_all
    paired_mean = total[channels + 1:channels + 2] / channels_all
    average, inverse = stats_ref[0:1, :], stats_ref[1:2, :]
    centred = (mixed_ref[...].astype(f32) - average) * inverse
    gain = pack_ref[:, 1:2]
    mixed_grad = inverse * (normed_grad * gain - scaled_mean - centred * paired_mean)
    return (
        mixed_grad,
        jnp.sum(normed_grad * centred, axis=1, keepdims=True),
        jnp.sum(normed_grad, axis=1, keepdims=True),
    )


def put_columns(ref, columns):
    places = lax.broadcasted_iota(jnp.int32, ref.shape, 1)
    value = jnp.zeros(ref.shape, f32)
    for index, column in enumerate(columns):
        value = jnp.where(places == index, column, value)
    ref[...] = value


def wide_norm_back_body(packed, channels_all, reach_ref, keep_ref, near_ref, far_ref, mixed_ref, stats_ref, pack_ref,
                        stream_ref, cotangent_ref, wide_ref, fore_ref, *refs):
    if packed:
        out_ref, grad_ref, sums_ref, signal_ref, kernel_ref, sum_ref, conv_ref, rest_ref = refs
    else:
        conv_ref, rest_ref, grad_ref, sums_ref, signal_ref, kernel_ref, sum_ref = refs
    canvases, rows = conv_ref.shape[0], conv_ref.shape[1]
    mixed_grad, gain_grad, shift_grad = norm_backward(
        (keep_ref, near_ref, far_ref), mixed_ref, stats_ref, pack_ref, channels_all
    )
    skip = pack_ref[:, 0:1]
    skip_grad = jnp.zeros_like(gain_grad)
    load_tiles(wide_ref[...], kernel_ref, 0)
    for canvas in range(canvases):
        for row in range(rows):
            at = (canvas * rows + row) * lane
            part = mixed_grad[:, at:at + lane]
            grad_ref[canvas, row] = part.astype(bf16)
            skip_grad += jnp.sum(part * stream_ref[canvas, row].astype(f32), axis=1, keepdims=True)
            rest_ref[canvas, row] = (cotangent_ref[canvas, row].astype(f32) + skip * part).astype(rest_ref.dtype)
        conv_ref[canvas] = convolve_canvas(
            canvas, -1, grad_ref, fore_ref, reach_ref, signal_ref, kernel_ref, sum_ref
        ).astype(conv_ref.dtype)
    put_columns(sums_ref, [skip_grad, gain_grad, shift_grad])
    if packed:
        pieces_from_rows(lambda b, r, c: conv_ref[b, r, c, :], out_ref, 0)
        pieces_from_rows(lambda b, r, c: rest_ref[b, r, c, :], out_ref, 1)


def wide_norm_back(packed, channels_all, grads, mixed, stats, pack, stream, cotangent, wide, fore, reach, after):
    plain = struct(stream.shape, bf16)
    sums = struct((stream.shape[2], lane), f32)
    got = launch(
        partial(wide_norm_back_body, packed, channels_all), "wide_norm_back",
        [*grads, mixed, stats, pack, stream, cotangent, wide, fore],
        [piece_shape(2), plain, sums] if packed else [plain, plain, plain, sums],
        width_scratch(stream.shape[1], stream.shape[2]) + [pltpu.VMEM(stream.shape, f32)] * (2 * packed),
        scalars=[reach], after=after,
    )
    return got[:-2], got[-2], got[-1]


def kernel_products(grad_ref, input_ref, age_ref, reach_ref, signal_ref, flat_ref, sum_ref, total_ref):
    channels = grad_ref.shape[2]
    rows = grad_ref.shape[1]
    total_ref[...] = jnp.zeros(total_ref.shape, f32)
    for canvas in range(grad_ref.shape[0]):
        load_tiles(stacked_rows(input_ref, canvas), signal_ref, pad)
        load_tiles(stacked_rows(grad_ref, canvas), flat_ref, 0)
        width_products(canvas, signal_ref, flat_ref, age_ref, reach_ref, total_ref)

    def reduce(index, carry):
        at = pl.multiple_of(index * 8, 8)
        for t in range(sum_ref.shape[0]):
            sum_ref[t, pl.ds(at, 8), :] = jnp.sum(total_ref[t, pl.ds(at, 8)], axis=1)
        return carry

    lax.fori_loop(0, lane // 8, reduce, 0)
    picture = unstacked(sum_ref, rows)
    return sum(picture[row] for row in range(rows))


def products_scratch(rows, channels):
    return width_scratch(rows, channels) + [pltpu.VMEM((rows * channels // lane, lane, 8, lane), f32)]


def wide_top_grad_body(reach_ref, grad_ref, input_ref, age_ref, out_ref, *scratch):
    out_ref[...] = kernel_products(grad_ref, input_ref, age_ref, reach_ref, *scratch)


def wide_top_grad(grad, inputs, age, reach, after=()):
    channels = grad.shape[2]
    return launch(
        wide_top_grad_body, "wide_top_grad", [grad, inputs, age], [struct((channels, lane), f32)],
        products_scratch(grad.shape[1], channels), scalars=[reach], after=after,
    )[0]


def wide_last_body(packed, forth_reach, back_reach, *refs):
    if packed:
        pieces, input_ref, wide_ref, age_ref, fore_ref, held_ref, top_ref, out_ref, total_out, *refs = refs
        signal_ref, kernel_ref, sum_ref, total_ref, grad_ref, rest_ref = refs

        def put_grad(b, r, c, value):
            grad_ref[b, r, c, :] = value.astype(bf16)

        def put_rest(b, r, c, value):
            rest_ref[b, r, c, :] = value

        rows_from_pieces(pieces, 0, put_grad)
        rows_from_pieces(pieces, 1, put_rest)
    else:
        grad_ref, rest_ref, input_ref, wide_ref, age_ref, fore_ref, held_ref, top_ref, out_ref, total_out, *refs = refs
        signal_ref, kernel_ref, sum_ref, total_ref = refs
    total_out[0, :, 0:lane] = kernel_products(
        grad_ref, input_ref, age_ref, forth_reach, signal_ref, kernel_ref, sum_ref, total_ref
    ).astype(bf16)
    total_out[0, :, lane:] = held_ref[...].astype(bf16)
    total_out[1] = top_ref[...]
    load_tiles(wide_ref[...], kernel_ref, 0)
    for canvas in range(grad_ref.shape[0]):
        value = convolve_canvas(canvas, -1, grad_ref, fore_ref, back_reach, signal_ref, kernel_ref, sum_ref)
        out_ref[canvas] = (value + rest_ref[canvas].astype(f32)).astype(bf16)


def wide_last(packed, moved, picture, inputs, wide, age, fore, held, top, forth_reach, back_reach, after):
    plain = struct(picture, bf16)
    scratch = products_scratch(picture[1], picture[2])
    if packed:
        scratch += [pltpu.VMEM(picture, bf16), pltpu.VMEM(picture, f32)]
    return launch(
        partial(wide_last_body, packed), "wide_last", [*moved, inputs, wide, age, fore, held, top],
        [plain, struct((2,) + top.shape, bf16)], scratch, scalars=[forth_reach, back_reach], after=after,
    )


def height_loop(count, body, carry):
    if count <= 16:
        for lag in range(count):
            carry = body(lag, carry)
        return carry
    return lax.fori_loop(0, count, body, carry)


def tap(kernel, lag):
    if isinstance(lag, int):
        return kernel[:, lag:lag + 1]
    places = lax.broadcasted_iota(jnp.int32, kernel.shape, 1)
    return jnp.sum(jnp.where(places == lag, kernel, 0.0), axis=1, keepdims=True)


def moved_by(value, shift):
    size = value.shape[1]
    if not isinstance(shift, int):
        return pltpu.roll(value, lax.rem(shift + size, size), 1)
    shift %= size
    return pltpu.roll(value, shift, 1) if shift else value


def height_conv(get, put, channels, kernel_ref, age_ref, sign, height):
    for at in range(0, channels, strip):
        rows = slice(at, at + strip)
        kernel = kernel_ref[rows, :]
        for canvas in range(age_ref.shape[0]):
            value, age = get(rows, canvas), age_ref[canvas]
            columns = value.shape[1] // height

            def body(lag, total):
                return total + tap(kernel, lag) * jnp.where(age >= lag, moved_by(value, sign * lag * columns), 0.0)

            put(rows, canvas, height_loop(height, body, jnp.zeros_like(value)))


def height_products(grads, values, ages, height):
    columns = values[0].shape[1] // height
    channels = values[0].shape[0]
    places = lax.broadcasted_iota(jnp.int32, (channels, lane), 1)

    def body(lag, total):
        part = None
        for grad, value, age in zip(grads, values, ages, strict=True):
            product = grad * jnp.where(age >= lag, moved_by(value, lag * columns), 0.0)
            for piece in lane_tiles(product):
                part = piece if part is None else part + piece
        return total + jnp.where(places == lag, jnp.sum(part, axis=1, keepdims=True), 0.0)

    return height_loop(height, body, jnp.zeros((channels, lane), f32))


def canvas_cut(ref, canvas, canvases):
    each = ref.shape[1] // canvases
    return slice(canvas * each, (canvas + 1) * each)


def tall_mixed_body(packed, height, *refs):
    if packed:
        pieces, kernel_ref, age_ref, pack_ref, out_ref, across_ref, stream_ref = refs
        cols_from_pieces(pieces, 0, across_ref)
        cols_from_pieces(pieces, 1, stream_ref)
    else:
        across_ref, stream_ref, kernel_ref, age_ref, pack_ref, out_ref = refs
    canvases = age_ref.shape[0]

    def get(rows, canvas):
        return across_ref[rows, canvas_cut(across_ref, canvas, canvases)].astype(f32)

    def put(rows, canvas, mixer):
        cut = canvas_cut(across_ref, canvas, canvases)
        out_ref[rows, cut] = (mixer + pack_ref[rows, 0:1] * stream_ref[rows, cut].astype(f32)).astype(bf16)

    height_conv(get, put, out_ref.shape[0], kernel_ref, age_ref, 1, height)


def tall_mixed(packed, height, moved, cols, kernel, age, pack, after):
    got = launch(
        partial(tall_mixed_body, packed, height), "tall_mixed", [*moved, kernel, age, pack],
        [struct(cols, bf16)] * (1 + 2 * packed), after=after,
    )
    return tuple(got) if packed else (got[0], *moved)


def tall_next_body(packed, height, keep_ref, near_ref, far_ref, stream_ref, pack_ref, kernel_ref, age_ref,
                   next_ref, branch_ref, out_ref, *held):
    canvases = age_ref.shape[0]
    conv_ref = held[0] if packed else out_ref

    def get(rows, canvas):
        cut = canvas_cut(stream_ref, canvas, canvases)
        branch = (
            keep_ref[rows, cut].astype(f32) + near_ref[rows, cut].astype(f32) + far_ref[rows, cut].astype(f32)
            + pack_ref[rows, 3:4]
        )
        branch_ref[rows, cut] = branch
        low = (stream_ref[rows, cut].astype(f32) + pack_ref[rows, 4:5] * branch).astype(bf16)
        next_ref[rows, cut] = low
        return low.astype(f32)

    def put(rows, canvas, value):
        conv_ref[rows, canvas_cut(stream_ref, canvas, canvases)] = value.astype(conv_ref.dtype)

    height_conv(get, put, stream_ref.shape[0], kernel_ref, age_ref, 1, height)
    if packed:
        pieces_from_cols(lambda rows, cut: conv_ref[rows, cut], out_ref, 0)
        pieces_from_cols(lambda rows, cut: next_ref[rows, cut].astype(f32), out_ref, 1)


def tall_next(packed, height, branches, stream, pack, kernel, age):
    got = launch(
        partial(tall_next_body, packed, height), "tall_next", [*branches, stream, pack, kernel, age],
        [struct(stream.shape, bf16), struct(stream.shape, f32), piece_shape(2) if packed else struct(stream.shape, bf16)],
        [pltpu.VMEM(stream.shape, f32)] * packed,
    )
    return got[0], got[1], [got[2]] if packed else [got[2], got[0]]


def tall_back_body(packed, height, *refs):
    if packed:
        pieces, kernel_ref, fore_ref, pack_ref, branch_ref, grad_ref, low_ref, sums_ref, conv_ref, rest_ref = refs
        cols_from_pieces(pieces, 0, conv_ref)
        cols_from_pieces(pieces, 1, rest_ref)
    else:
        conv_ref, rest_ref, kernel_ref, fore_ref, pack_ref, branch_ref, grad_ref, low_ref, sums_ref = refs
    canvases = fore_ref.shape[0]

    def get(rows, canvas):
        return conv_ref[rows, canvas_cut(conv_ref, canvas, canvases)].astype(f32)

    def put(rows, canvas, value):
        cut = canvas_cut(conv_ref, canvas, canvases)
        grad = rest_ref[rows, cut].astype(f32) + value
        grad_ref[rows, cut] = grad
        low_ref[rows, cut] = (grad * pack_ref[rows, 4:5]).astype(bf16)

    height_conv(get, put, conv_ref.shape[0], kernel_ref, fore_ref, -1, height)
    sums_ref[...] = jnp.zeros(sums_ref.shape, f32)


def tall_back(packed, height, moved, cols, kernel, fore, pack, branch, after, through):
    got = launch(
        partial(tall_back_body, packed, height), "tall_back", [*moved, kernel, fore, pack, branch],
        [struct(cols, f32), struct(cols, bf16), struct((cols[0], lane), f32)] + [struct(cols, bf16)] * packed,
        [pltpu.VMEM(cols, f32)] * packed, after=after, through=through,
    )
    return got[0], got[1], got[3] if packed else moved[0], *got[3 + packed:]


def tall_norm_back_body(packed, height, channels_all, keep_ref, near_ref, far_ref, mixed_ref, stats_ref, pack_ref, stream_ref,
                        grad_ref, kernel_ref, fore_ref, *refs):
    if packed:
        out_ref, low_ref, sums_ref, conv_ref, rest_ref = refs
    else:
        conv_ref, rest_ref, low_ref, sums_ref = refs
    canvases = fore_ref.shape[0]
    mixed_grad, gain_grad, shift_grad = norm_backward(
        (keep_ref, near_ref, far_ref), mixed_ref, stats_ref, pack_ref, channels_all
    )
    low_ref[...] = mixed_grad.astype(bf16)
    rest_ref[...] = (grad_ref[...] + pack_ref[:, 0:1] * mixed_grad).astype(rest_ref.dtype)
    skip_grad = jnp.sum(mixed_grad * stream_ref[...].astype(f32), axis=1, keepdims=True)

    def get(rows, canvas):
        return low_ref[rows, canvas_cut(low_ref, canvas, canvases)].astype(f32)

    def put(rows, canvas, value):
        conv_ref[rows, canvas_cut(low_ref, canvas, canvases)] = value.astype(conv_ref.dtype)

    height_conv(get, put, low_ref.shape[0], kernel_ref, fore_ref, -1, height)
    put_columns(sums_ref, [skip_grad, gain_grad, shift_grad])
    if packed:
        pieces_from_cols(lambda rows, cut: conv_ref[rows, cut], out_ref, 0)
        pieces_from_cols(lambda rows, cut: rest_ref[rows, cut], out_ref, 1)


def tall_norm_back(packed, height, channels_all, grads, mixed, stats, pack, stream, grad, kernel, fore, after):
    plain, sums = struct(mixed.shape, bf16), struct((mixed.shape[0], lane), f32)
    got = launch(
        partial(tall_norm_back_body, packed, height, channels_all), "tall_norm_back",
        [*grads, mixed, stats, pack, stream, grad, kernel, fore],
        [piece_shape(2), plain, sums] if packed else [plain, plain, plain, sums],
        [pltpu.VMEM(mixed.shape, f32)] * (2 * packed), after=after,
    )
    return got[:-2], got[-2], got[-1]


def tall_products(height, grad_ref, input_ref, age_ref, put):
    canvases = age_ref.shape[0]
    for at in range(0, grad_ref.shape[0], strip):
        rows = slice(at, at + strip)
        cuts = [canvas_cut(grad_ref, canvas, canvases) for canvas in range(canvases)]
        put(rows, height_products(
            [grad_ref[rows, cut].astype(f32) for cut in cuts], [input_ref[rows, cut].astype(f32) for cut in cuts],
            [age_ref[canvas] for canvas in range(canvases)], height,
        ))


def held_lanes(height):
    return -(-(height + 16) // lane) * lane


def beside(held, height, columns):
    if held_lanes(height) > lane:
        held = jnp.concatenate([held, jnp.zeros_like(held)], axis=1)
    places = lax.broadcasted_iota(jnp.int32, held.shape, 1)
    held = jnp.where(places < height, held, 0.0)
    for index, column in enumerate(columns):
        held = jnp.where(places == height + index, column, held)
    return held


def unit_columns(units_ref, rows, channels):
    return [units_ref[at + rows.start:at + rows.stop, 0:1] for at in range(0, units_ref.shape[0], channels)]


def tall_top_grad_body(height, grad_ref, input_ref, age_ref, wide_ref, norm_ref, bias_ref, units_ref, out_ref):
    channels = grad_ref.shape[0]

    def put(rows, held):
        columns = [norm_ref[rows, k:k + 1] for k in range(3)] + [bias_ref[rows, 0:1]]
        out_ref[rows, lane:] = beside(held, height, columns + unit_columns(units_ref, rows, channels)).astype(bf16)

    tall_products(height, grad_ref, input_ref, age_ref, put)
    out_ref[:, 0:lane] = wide_ref[...].astype(bf16)


def tall_top_grad(height, grad, inputs, age, wide, norm, bias, units, after):
    return launch(
        partial(tall_top_grad_body, height), "tall_top_grad", [grad, inputs, age, wide, norm, bias, units],
        [struct((grad.shape[0], lane + held_lanes(height)), bf16)], after=after,
    )[0]


def tall_low_grad_body(height, grad_ref, input_ref, age_ref, norm_ref, grad_out_ref, branch_ref, pack_ref, scale_ref, units_ref,
                       out_ref):
    channels = grad_ref.shape[0]

    def put(rows, held):
        grad = grad_out_ref[rows, :]
        columns = [norm_ref[rows, k:k + 1] for k in range(3)]
        columns.append(jnp.sum(grad, axis=1, keepdims=True) * pack_ref[rows, 4:5])
        columns += unit_columns(units_ref, rows, channels)
        columns.append(jnp.sum(grad * branch_ref[rows, :], axis=1, keepdims=True))
        columns.append(scale_ref[rows, 0:1])
        out_ref[rows, :] = beside(held, height, columns)

    tall_products(height, grad_ref, input_ref, age_ref, put)


def tall_low_grad(height, grad, inputs, age, norm, grad_out, branch, pack, scale, units, after):
    return launch(
        partial(tall_low_grad_body, height), "tall_low_grad",
        [grad, inputs, age, norm, grad_out, branch, pack, scale, units],
        [struct((grad.shape[0], held_lanes(height)), f32)], after=after,
    )[0]


root = 0.7978845608028654
cubic = 0.044715


def gather_into(me_ref, parts, whole_ref):
    me = me_ref[0]
    for flip, part in enumerate(parts):
        whole_ref[me ^ flip] = part[...]


def scatter_out(me_ref, whole_ref, outs):
    me = me_ref[0]
    for flip, out in zip((3, 1, 2, 0), outs, strict=True):
        out[...] = whole_ref[me ^ flip]


def gather_shape(me_ref, parts, section, shape_ref):
    gather_into(me_ref, parts, shape_ref)
    every = shape_ref[...].reshape(-1, shape_ref.shape[2])
    return every[:, 2 * section:2 * section + 1], every[:, 2 * section + 1:2 * section + 2]


def mlp_forward(me_ref, parts, full_ref, shape, weight_in_ref, bias_ref, normed_ref, hidden_ref, slope_ref, stats_ref):
    gather_into(me_ref, parts, full_ref)
    mixed = full_ref[...].astype(f32).reshape(-1, full_ref.shape[2])
    average = jnp.mean(mixed, axis=0, keepdims=True)
    moved = mixed - average
    inverse = lax.rsqrt(jnp.mean(moved * moved, axis=0, keepdims=True) + epsilon)
    centred = moved * inverse
    stats_ref[0:1, :] = average
    stats_ref[1:2, :] = inverse
    normed = (centred * shape[0] + shape[1]).astype(bf16)
    normed_ref[...] = normed
    before = dot(weight_in_ref[0], normed, 0, 0) + bias_ref[...]
    square = before * before
    bend = jnp.tanh(root * before * (1.0 + cubic * square))
    half = 0.5 * (1.0 + bend)
    hidden_ref[...] = (before * half).astype(bf16)
    slope_ref[...] = (half + 0.5 * before * (1.0 - bend * bend) * root * (1.0 + 3.0 * cubic * square)).astype(slope_ref.dtype)
    return centred


def mlp_first_body(section, me_ref, own, near, far, cross, shape_own, shape_near, shape_far, shape_cross, weight_in_ref,
                   bias_ref, weight_out_ref,
                   send_far, send_own, keep_far, keep_own, normed_ref, hidden_ref, slope_ref, stats_ref, full_ref, sum_ref,
                   shape_ref):
    shape = gather_shape(me_ref, (shape_own, shape_near, shape_far, shape_cross), section, shape_ref)
    mlp_forward(me_ref, (own, near, far, cross), full_ref, shape, weight_in_ref, bias_ref,
                normed_ref, hidden_ref, slope_ref, stats_ref)
    partial_out = dot(weight_out_ref[0], hidden_ref[...], 0, 0)
    sum_ref[...] = partial_out.astype(bf16).reshape(sum_ref.shape)
    scatter_out(me_ref, sum_ref, (send_far, send_own, keep_far, keep_own))


def mlp_backward(me_ref, parts, full_ref, weight_out_ref, weight_in_ref, slope, gain, centred, sum_ref, outs, before_grad_ref):
    gather_into(me_ref, parts, full_ref)
    grad = full_ref[...].reshape(-1, full_ref.shape[2])
    before_grad = (dot(weight_out_ref[0], grad, 1, 0) * slope).astype(bf16)
    before_grad_ref[...] = before_grad
    normed_part = dot(weight_in_ref[0], before_grad, 1, 0)
    channels = sum_ref.shape[1] - 16
    scaled = normed_part * gain
    scaled_sum = jnp.sum(scaled, axis=0, keepdims=True)
    paired_sum = jnp.sum(scaled * centred, axis=0, keepdims=True)
    places = lax.broadcasted_iota(jnp.int32, (16, grad.shape[1]), 0)
    tail = jnp.where(places == 0, scaled_sum, jnp.where(places == 1, paired_sum, 0.0)).astype(bf16)
    for index in range(sum_ref.shape[0]):
        sum_ref[index, 0:channels, :] = normed_part[index * channels:(index + 1) * channels].astype(bf16)
        sum_ref[index, channels:, :] = tail
    scatter_out(me_ref, sum_ref, outs)


def mlp_top_body(section, me_ref, own, near, far, cross, grad_own, grad_near, grad_far, grad_cross,
                 shape_own, shape_near, shape_far, shape_cross, weight_in_ref, bias_ref, weight_out_ref,
                 back_sf, back_so, back_kf, back_ko, stats_ref, normed_ref, hidden_ref, before_grad_ref,
                 full_ref, back_ref, slope_ref, shape_ref):
    shape = gather_shape(me_ref, (shape_own, shape_near, shape_far, shape_cross), section, shape_ref)
    centred = mlp_forward(me_ref, (own, near, far, cross), full_ref, shape, weight_in_ref, bias_ref,
                          normed_ref, hidden_ref, slope_ref, stats_ref)
    mlp_backward(me_ref, (grad_own, grad_near, grad_far, grad_cross), full_ref, weight_out_ref, weight_in_ref,
                 slope_ref[...], shape[0], centred, back_ref, (back_sf, back_so, back_kf, back_ko), before_grad_ref)


def mlp_back_body(section, me_ref, own, near, far, cross, grad_own, grad_near, grad_far, grad_cross,
                  shape_own, shape_near, shape_far, shape_cross, weight_in_ref, weight_out_ref, slope_ref, stats_ref,
                  back_sf, back_so, back_kf, back_ko, before_grad_ref, full_ref, back_ref, shape_ref):
    shape = gather_shape(me_ref, (shape_own, shape_near, shape_far, shape_cross), section, shape_ref)
    gather_into(me_ref, (own, near, far, cross), full_ref)
    centred = (full_ref[...].astype(f32).reshape(-1, full_ref.shape[2]) - stats_ref[0:1, :]) * stats_ref[1:2, :]
    mlp_backward(me_ref, (grad_own, grad_near, grad_far, grad_cross), full_ref, weight_out_ref, weight_in_ref,
                 slope_ref[...].astype(f32), shape[0], centred, back_ref, (back_sf, back_so, back_kf, back_ko), before_grad_ref)


tile = 256


def pixel_block(rows):
    return pl.BlockSpec((rows, tile), lambda i: (0, i))


def fixed_block(shape):
    return pl.BlockSpec(shape, lambda i: (0,) * len(shape))


def section_block(section, shape):
    return pl.BlockSpec((1,) + shape, lambda i: (section, 0, 0))


def mlp_first(section, me, parts, shaping, weight_in, bias, weight_out):
    own = parts[0]
    channels, pixels = own.shape
    wide, units = weight_in.shape[1], weight_in.shape[2]
    piece = pixel_block(channels)
    return pl.pallas_call(
        partial(mlp_first_body, section),
        grid=(pixels // tile,),
        in_specs=[smem_spec()] + [piece] * 4 + [
            *[fixed_block(shaping[0].shape)] * 4, section_block(section, (wide, units)), fixed_block(bias.shape),
            section_block(section, (units, wide)),
        ],
        out_specs=[piece] * 4 + [pixel_block(wide), pixel_block(units), pixel_block(units), pixel_block(8)],
        out_shape=[struct(own.shape, bf16)] * 4 + [
            struct((wide, pixels), bf16), struct((units, pixels), bf16), struct((units, pixels), bf16), struct((8, pixels), f32),
        ],
        scratch_shapes=[
            pltpu.VMEM((4, channels, tile), bf16), pltpu.VMEM((4, channels, tile), bf16), pltpu.VMEM((4,) + shaping[0].shape, f32),
        ],
        name="mlp_first",
        **params(),
    )(me, *parts, *shaping, weight_in, bias, weight_out)


def mlp_top(section, me, parts, grads, shaping, weight_in, bias, weight_out):
    own = parts[0]
    channels, pixels = own.shape
    wide, units = weight_in.shape[1], weight_in.shape[2]
    piece, back = pixel_block(channels), pixel_block(channels + 16)
    return pl.pallas_call(
        partial(mlp_top_body, section),
        grid=(pixels // tile,),
        in_specs=[smem_spec()] + [piece] * 8 + [
            *[fixed_block(shaping[0].shape)] * 4, section_block(section, (wide, units)), fixed_block(bias.shape),
            section_block(section, (units, wide)),
        ],
        out_specs=[back] * 4 + [pixel_block(8), pixel_block(wide), pixel_block(units), pixel_block(units)],
        out_shape=[struct((channels + 16, pixels), bf16)] * 4 + [
            struct((8, pixels), f32), struct((wide, pixels), bf16), struct((units, pixels), bf16), struct((units, pixels), bf16),
        ],
        scratch_shapes=[
            pltpu.VMEM((4, channels, tile), bf16), pltpu.VMEM((4, channels + 16, tile), bf16),
            pltpu.VMEM((units, tile), f32), pltpu.VMEM((4,) + shaping[0].shape, f32),
        ],
        name="mlp_top",
        **params(),
    )(me, *parts, *grads, *shaping, weight_in, bias, weight_out)


def mlp_back(section, me, parts, grads, shaping, weight_in, weight_out, slope, stats, after):
    own = parts[0]
    channels, pixels = own.shape
    wide, units = weight_in.shape[1], weight_in.shape[2]
    piece, back = pixel_block(channels), pixel_block(channels + 16)
    given = 1 + 8 + 4 + 4

    def body(*refs):
        mlp_back_body(section, *refs[:given], *refs[given + len(after):])

    return pl.pallas_call(
        body,
        grid=(pixels // tile,),
        in_specs=[smem_spec()] + [piece] * 8 + [
            *[fixed_block(shaping[0].shape)] * 4, section_block(section, (wide, units)), section_block(section, (units, wide)),
            pixel_block(units), pixel_block(8), *[any_spec()] * len(after),
        ],
        out_specs=[back] * 4 + [pixel_block(units)],
        out_shape=[struct((channels + 16, pixels), bf16)] * 4 + [struct((units, pixels), bf16)],
        scratch_shapes=[
            pltpu.VMEM((4, channels, tile), bf16), pltpu.VMEM((4, channels + 16, tile), bf16),
            pltpu.VMEM((4,) + shaping[0].shape, f32),
        ],
        name="mlp_back",
        **params(),
    )(me, *parts, *grads, *shaping, weight_in, weight_out, slope, stats, *after)


def mlp_out_body(section, me_ref, hidden_ref, weight_out_ref, send_far, send_own, keep_far, keep_own, sum_ref):
    for at in range(0, hidden_ref.shape[1], tile):
        cut = slice(at, at + tile)
        value = dot(weight_out_ref[section], hidden_ref[:, cut], 0, 0).astype(bf16)
        sum_ref[:, :, cut] = value.reshape(sum_ref.shape[0], sum_ref.shape[1], tile)
    scatter_out(me_ref, sum_ref, (send_far, send_own, keep_far, keep_own))


def mlp_out(section, me, hidden, weight_out, after):
    wide, pixels = weight_out.shape[2], hidden.shape[1]
    piece = struct((wide // 4, pixels), bf16)
    return launch(
        partial(mlp_out_body, section), "mlp_out", [hidden, weight_out], [piece] * 4,
        [pltpu.VMEM((4, wide // 4, pixels), bf16)], scalars=[me], after=after,
    )


def put_halves(ref, at, outs):
    size = outs[0].shape[0]
    for side, out in zip((at, 1 - at), outs, strict=True):
        out[...] = ref[pl.ds(pl.multiple_of(side * size, size), size), :].astype(bf16)


def weights_body(me_ref, hidden_ref, grad_own, grad_near, grad_far, grad_cross, normed_ref, before_grad_ref,
                 keep, send, units_ref, full_ref, total_ref):
    units = hidden_ref.shape[0]
    gather_into(me_ref, (grad_own, grad_near, grad_far, grad_cross), full_ref)
    total_ref[0:units] = dot(hidden_ref[...], full_ref[...].reshape(-1, full_ref.shape[2]), 1, 1)
    before_grad = before_grad_ref[...]
    total_ref[units:] = dot(normed_ref[...], before_grad, 1, 1)
    units_ref[...] = jnp.broadcast_to(jnp.sum(before_grad.astype(f32), axis=1, keepdims=True), units_ref.shape)
    put_halves(total_ref, me_ref[2], (keep, send))


def weight_grads(me, hidden, grads, normed, before_grad, after=()):
    units, wide = hidden.shape[0], normed.shape[0]
    return launch(
        weights_body, "weight_grads", [hidden, *grads, normed, before_grad],
        [struct((units, wide), bf16)] * 2 + [struct((units, lane), f32)],
        [pltpu.VMEM((4,) + grads[0].shape, bf16), pltpu.VMEM((units + wide, wide), f32)], scalars=[me], after=after,
    )


def out_grad_body(me_ref, hidden_ref, grad_own, grad_near, grad_far, grad_cross, keep, send, full_ref, total_ref):
    gather_into(me_ref, (grad_own, grad_near, grad_far, grad_cross), full_ref)
    total_ref[...] = dot(hidden_ref[...], full_ref[...].reshape(-1, full_ref.shape[2]), 1, 1)
    put_halves(total_ref, me_ref[2], (keep, send))


def out_grad(me, hidden, grads, after=()):
    units, wide = hidden.shape[0], 4 * grads[0].shape[0]
    return launch(
        out_grad_body, "out_grad", [hidden, *grads], [struct((units // 2, wide), bf16)] * 2,
        [pltpu.VMEM((4,) + grads[0].shape, bf16), pltpu.VMEM((units, wide), f32)], scalars=[me], after=after,
    )


def in_grad_body(me_ref, normed_ref, before_grad_ref, keep, send, units_ref, total_ref):
    before_grad = before_grad_ref[...]
    total_ref[...] = dot(normed_ref[...], before_grad, 1, 1)
    put_halves(total_ref, me_ref[2], (keep, send))
    units_ref[...] = jnp.broadcast_to(jnp.sum(before_grad.astype(f32), axis=1, keepdims=True), units_ref.shape)


def in_grad(me, normed, before_grad, after=()):
    wide, units = normed.shape[0], before_grad.shape[0]
    return launch(
        in_grad_body, "in_grad", [normed, before_grad],
        [struct((wide // 2, units), bf16)] * 2 + [struct((units, lane), f32)],
        [pltpu.VMEM((wide, units), f32)], scalars=[me], after=after,
    )


def top_output_body(keep_ref, near_ref, far_ref, stream_ref, cotangent_ref, pack_ref, out_ref, sums_ref):
    bias, scale = pack_ref[:, 3:4], pack_ref[:, 4:5]
    total = jnp.zeros(scale.shape, f32)
    rows = stream_ref.shape[1]
    for canvas in range(stream_ref.shape[0]):
        for row in range(rows):
            at = (canvas * rows + row) * lane
            cut = slice(at, at + lane)
            branch = keep_ref[:, cut].astype(f32) + near_ref[:, cut].astype(f32) + far_ref[:, cut].astype(f32) + bias
            out_ref[canvas, row] = (stream_ref[canvas, row].astype(f32) + scale * branch).astype(bf16)
            total += jnp.sum(cotangent_ref[canvas, row].astype(f32) * branch, axis=1, keepdims=True)
    put_columns(sums_ref, [total])


def top_output(branches, stream, cotangent, pack, after):
    return launch(
        top_output_body, "top_output", [*branches, stream, cotangent, pack],
        [struct(stream.shape, bf16), struct((stream.shape[2], lane), f32)], after=after,
    )


core_pairs = [(i, i ^ 1) for i in range(4)]
chip_pairs = [(i, i ^ 2) for i in range(4)]


def gather_channels(own):
    far = lax.ppermute(own, "ch", chip_pairs)
    near = lax.ppermute(own, "ch", core_pairs)
    cross = lax.ppermute(far, "ch", core_pairs)
    return (own, near, far, cross)


def scatter_channels(send_far, send_own, keep_far, keep_own):
    near_far = lax.ppermute(send_far, "ch", core_pairs)
    near_own = lax.ppermute(send_own, "ch", core_pairs)
    onward = (keep_far.astype(f32) + near_far.astype(f32)).astype(bf16)
    far = lax.ppermute(onward, "ch", chip_pairs)
    return (keep_own, near_own, far), onward


def across_rows(value, flip):
    return lax.ppermute(value, "rows", [(i, i ^ flip) for i in range(8)])


def rows_sum(value):
    for flip in (1, 2, 4):
        value = (value.astype(f32) + across_rows(value, flip).astype(f32)).astype(bf16)
    return value


def total_of(refs):
    return sum(ref[...].astype(f32) for ref in refs)


def halve_body(bit, me_ref, keep_ref, near_ref, keep_out, send_out, total_ref):
    total_ref[...] = total_of((keep_ref, near_ref))
    put_halves(total_ref, me_ref[bit], (keep_out, send_out))


def halve(bit, me, keep, near, after, through=()):
    rows, columns = keep.shape
    return launch(
        partial(halve_body, bit), "halve", [keep, near], [struct((rows // 2, columns), bf16)] * 2,
        [pltpu.VMEM(keep.shape, f32)], scalars=[me], after=after, through=through,
    )


def pair_add_body(keep_ref, near_ref, out_ref):
    out_ref[...] = total_of((keep_ref, near_ref)).astype(bf16)


def pair_add(keep, near, after=(), through=()):
    got = launch(pair_add_body, "pair_add", [keep, near], [struct(keep.shape, bf16)], after=after, through=through)
    return got if through else got[0]


back_flips = ((4, 2, 1), (1, 4, 2))


def spread_back(total, flips):
    parts = [total]
    for flip in flips:
        parts += [across_rows(part, flip) for part in parts]
    return parts


def top_store(me, parts, after):
    size, columns = parts[0].shape

    def body(me_ref, *refs):
        outs = refs[-2:]

        def put(kept):
            for f, part in enumerate(refs[:8]):
                at = (me_ref[3] ^ (f >> 1 & 1)) * 2 + (me_ref[4] ^ (f & 1))
                outs[kept ^ (f >> 2)][0, pl.ds(pl.multiple_of(at * size, size), size), :] = part[...].astype(f32)

        @pl.when(me_ref[2] == 0)
        def _():
            put(0)

        @pl.when(me_ref[2] == 1)
        def _():
            put(1)

    return pl.pallas_call(
        body,
        grid=(1,),
        in_specs=[smem_spec()] + [pl.BlockSpec(part.shape, lambda i: (0, 0)) for part in parts] + [any_spec()] * len(after),
        out_specs=[pl.BlockSpec((1, 4 * size, columns), lambda i: (1, 0, 0))] * 2,
        out_shape=[struct((2, 4 * size, columns), f32)] * 2,
        name="top_store",
        **params(),
    )(me, *parts, *after)


def finish(flips, me, held, parts, after=()):
    size, columns = parts[0].shape
    block = pl.BlockSpec((1,) + held.shape[1:], lambda i: (0, 0, 0))

    def body(me_ref, *refs):
        out = refs[-1]
        for f, part in enumerate(refs[:8]):
            flipped = sum(flip for bit, flip in enumerate(flips) if f >> bit & 1)
            at = (me_ref[2] ^ (flipped & 1)) * 4 + (me_ref[3] ^ (flipped >> 1 & 1)) * 2 + (me_ref[4] ^ (flipped >> 2))
            out[0, pl.ds(pl.multiple_of(at * size, size), size), :] = part[...].astype(f32)

    return pl.pallas_call(
        body,
        grid=(1,),
        in_specs=[smem_spec()] + [pl.BlockSpec(part.shape, lambda i: (0, 0)) for part in parts]
        + [any_spec()] * (1 + len(after)),
        out_specs=block,
        out_shape=struct(held.shape, f32),
        input_output_aliases={1 + len(parts): 0},
        name="finish",
        **params(),
    )(me, *parts, held, *after)


def exchange(pieces):
    return lax.all_to_all(pieces, "rows", split_axis=0, concat_axis=0, tiled=True)


def rows_to_cols(packed, moving, count, picture):
    if packed:
        return [exchange(moving[0])]
    canvases, rows, channels, width = picture
    pieces = []
    for part in moving:
        cut = part.reshape(canvases, rows, channels, count, width // count)
        pieces.append(cut.transpose(3, 2, 0, 1, 4).reshape(count, channels, -1))
    moved = exchange(jnp.stack(pieces, axis=1))
    moved = moved.reshape(count, len(moving), channels, canvases, rows, width // count)
    return [moved[:, k].transpose(1, 2, 0, 3, 4).reshape(channels, -1) for k in range(len(moving))]


def cols_to_rows(packed, moving, count, picture):
    if packed:
        return [exchange(moving[0])]
    canvases, rows, channels, width = picture
    pieces = []
    for part in moving:
        cut = part.reshape(channels, canvases, count, rows, width // count)
        pieces.append(cut.transpose(2, 0, 1, 3, 4).reshape(count, channels, -1))
    moved = exchange(jnp.stack(pieces, axis=1))
    moved = moved.reshape(count, len(moving), channels, canvases, rows, width // count)
    return [moved[:, k].transpose(2, 3, 1, 0, 4).reshape(picture) for k in range(len(moving))]


def crop_reach(starts):
    count = starts.shape[1]
    places = jnp.arange(count, dtype=jnp.int32)
    here, there = places[None, :, None], places[None, None, :]
    begins = starts[:, None, :] > 0
    first = jnp.max(jnp.where(begins & (there <= here), there, 0), axis=2)
    following = jnp.min(jnp.where(begins & (there > here), there, count), axis=2)
    return places[None, :] - first, following - 1 - places[None, :]


def band_turns(age):
    return jnp.max(age.reshape(age.shape[0], -1, band), axis=2) // ahead + 1


def on_device(
    count,
    pixels,
    row_starts,
    col_starts,
    log_step,
    log_decay,
    frequency,
    coef_real,
    coef_imag,
    skip_gain,
    norm_gain,
    norm_shift,
    weight_in,
    bias_in,
    weight_out,
    bias_out,
    layer_scale,
    cotangent,
):
    canvases, rows, width, channels = pixels.shape
    height = row_starts.shape[1]
    channels_all = weight_in.shape[1]
    lengths = (height, width)
    picture = (canvases, rows, channels, width)
    cols = (channels, canvases * height * (width // count))
    eight = count == 8
    packed = eight and picture == (2, 2, 2 * half_rows, lane)
    place = lax.axis_index("rows")
    bits = [place % 2, place // 2 % 2, place // 4] if eight else [0 * place] * 3
    me = jnp.stack([lax.axis_index("ch"), place, *bits]).astype(jnp.int32)

    stream = jnp.swapaxes(pixels, 2, 3)
    upstream = jnp.swapaxes(cotangent, 2, 3)
    states = [jnp.swapaxes(value, 2, 3) for value in (log_decay, frequency, coef_real, coef_imag)]

    age, fore = crop_reach(col_starts)
    age_reach, fore_reach = band_turns(age), band_turns(fore)
    age = jnp.broadcast_to(age[:, :, None], (canvases, width, lane))
    fore = jnp.broadcast_to(fore[:, :, None], (canvases, width, lane))
    row_age, row_fore = crop_reach(row_starts)
    row_age = jnp.repeat(row_age, width // count, axis=1)[:, None, :]
    row_fore = jnp.repeat(row_fore, width // count, axis=1)[:, None, :]

    packs = [
        jnp.stack([skip_gain[k], norm_gain[k], norm_shift[k], bias_out[k], layer_scale[k]], axis=1) for k in range(2)
    ]
    shaping = gather_channels(jnp.stack([norm_gain[0], norm_shift[0], norm_gain[1], norm_shift[1]], axis=1))
    bias_columns = [bias_in[k][:, None] for k in range(2)]

    wide_low = s4_wide(0, width, rows, log_step, *states)
    across = wide_forward(packed, stream, wide_low, age, age_reach)
    tall_low, tall_top, wide_top, top_scaled, top_bias_sums = s4_rest(
        lengths, rows, log_step, states, upstream, packs[1], [across]
    )
    moved = rows_to_cols(packed, [across] if packed else [across, stream], count, picture)
    mixed_low, across_cols, stream_cols = tall_mixed(
        packed, height, moved, cols, tall_low, row_age, packs[0], [*shaping[1:], *bias_columns, me]
    )
    low_parts = gather_channels(mixed_low)
    first = mlp_first(0, me, low_parts, shaping, weight_in, bias_columns[0], weight_out)
    normed_low, hidden_low, slope_low, stats_low = first[4:]
    branches, _ = scatter_channels(*first[:4])
    top_parts = gather_channels(top_scaled)

    next_cols, branch_cols, moving = tall_next(packed, height, branches, stream_cols, packs[0], tall_top, row_age)
    moved = cols_to_rows(packed, moving, count, picture)
    mixed_top, tall_rows, next_rows = wide_mixed(packed, moved, picture, wide_top, age, age_reach, packs[1])
    top_mixed_parts = gather_channels(mixed_top)
    top = mlp_top(1, me, top_mixed_parts, top_parts, shaping, weight_in, bias_columns[1], weight_out)
    stats_top, normed_top, hidden_top, before_grad_top = top[4:]
    top_grads, onward = scatter_channels(*top[:4])
    top_keep, top_send, top_units = weight_grads(me, hidden_top, top_parts, normed_top, before_grad_top, [onward])
    top_weights = [top_keep, top_send]

    moving, grad_rows, top_sums = wide_norm_back(
        packed, channels_all, top_grads, mixed_top, stats_top, packs[1], next_rows, upstream, wide_top, fore, fore_reach,
        [top_send],
    )
    top_partials = mlp_out(1, me, hidden_top, weight_out, moving[:1])
    top_wide = wide_top_grad(grad_rows, tall_rows, age, age_reach, top_partials[:1])
    moved = rows_to_cols(packed, moving, count, picture)
    grad_cols, grad_low, conv_cols, top_send = tall_back(
        packed, height, moved, cols, tall_top, row_fore, packs[0], branch_cols, [top_wide], [top_send]
    )

    grad_parts = gather_channels(grad_low)
    *back, before_grad_low = mlp_back(
        0, me, low_parts, grad_parts, shaping, weight_in, weight_out, slope_low, stats_low, []
    )
    low_grads, onward = scatter_channels(*back)
    out_keep, out_send = out_grad(me, hidden_low, grad_parts, [onward])
    if eight:
        top_keep, top_send = halve(3, me, top_keep, across_rows(top_send, 1), [out_send])
        top_near = across_rows(top_send, 2)
    in_keep, in_send, low_units = in_grad(me, normed_low, before_grad_low, [top_send])
    if eight:
        out_near, in_near = across_rows(out_send, 1), across_rows(in_send, 1)
    moving, low_grad_cols, low_sums = tall_norm_back(
        packed, height, channels_all, low_grads, mixed_low, stats_low, packs[0], stream_cols, grad_cols, tall_low, row_fore,
        [in_send],
    )
    if eight:
        out_keep, out_send = halve(3, me, out_keep, out_near, [moving[0]])
        out_near = across_rows(out_send, 2)
        top_keep, top_send = halve(4, me, top_keep, top_near, [out_send])
        top_near = across_rows(top_send, 4)
    top_branches, _ = scatter_channels(*top_partials)
    activations, top_scale_sums = top_output(top_branches, next_rows, upstream, packs[1], [top_send])
    held = tall_low_grad(
        height, low_grad_cols, across_cols, row_age, low_sums, grad_cols, branch_cols, packs[0], top_scale_sums, low_units,
        [out_keep],
    )
    if eight:
        out_keep, out_send = halve(4, me, out_keep, out_near, [held])
        out_near = across_rows(out_send, 4)
        in_keep, in_send = halve(3, me, in_keep, in_near, [out_send])
        in_near = across_rows(in_send, 2)
        top_total = pair_add(top_keep, top_near, [in_send])
        top_weights = spread_back(top_total, back_flips[0])
    top_small = tall_top_grad(
        height, conv_cols, next_cols, row_age, top_wide, top_sums, top_bias_sums, top_units, [top_total] if eight else [held]
    )
    if eight:
        out_total = pair_add(out_keep, out_near, [top_small])
        out_parts = spread_back(out_total, back_flips[0])
    moved = cols_to_rows(packed, moving, count, picture)
    pixels_grad, small = wide_last(
        packed, moved, picture, stream, wide_low, age, fore, held, top_small, age_reach, fore_reach, [out_total] if eight else []
    )
    if eight:
        in_keep, in_send = halve(4, me, in_keep, in_near, [small])
        in_total = pair_add(in_keep, across_rows(in_send, 4), [in_send])
        in_parts = spread_back(in_total, back_flips[1])
        out_grads, in_grads = top_store(me, top_weights, [in_total])
        out_grads = finish(back_flips[0], me, out_grads, out_parts)
        small = rows_sum(small)
    else:
        small = lax.psum(small.astype(f32), "rows").astype(bf16)
    gradients = s4_pullback(lengths, weight_in.shape[2], small, log_step, *states, [out_grads] if eight else [])
    step_grad, decay_grad, freq_grad, real_grad, imag_grad, skip_grad, gain_grad, shift_grad, units_grad, bias_grad, scale_grad = gradients
    if eight:
        in_grads = finish(back_flips[1], me, in_grads, in_parts, [step_grad])
    else:
        low_weights = lax.psum((out_keep, out_send, in_keep, in_send), "rows")
        top_weights = lax.psum(tuple(top_weights), "rows")
        out_grads = jnp.stack([jnp.concatenate(low_weights[:2]), top_weights[0]]).astype(f32)
        in_grads = jnp.stack([jnp.concatenate(low_weights[2:]), top_weights[1]]).astype(f32)
    return (
        jnp.swapaxes(activations, 2, 3),
        jnp.swapaxes(pixels_grad, 2, 3),
        step_grad,
        jnp.swapaxes(decay_grad, 2, 3),
        jnp.swapaxes(freq_grad, 2, 3),
        jnp.swapaxes(real_grad, 2, 3),
        jnp.swapaxes(imag_grad, 2, 3),
        skip_grad,
        gain_grad,
        shift_grad,
        in_grads,
        units_grad,
        out_grads,
        bias_grad,
        scale_grad,
    )


def solution(mesh):
    picture = P(None, "rows", None, "ch")
    state = P(None, None, "ch", None)
    step = P(None, None, "ch")
    vector = P(None, "ch")
    into = P(None, None, "ch")
    out = P(None, "ch", None)
    in_specs = (
        picture, P(), P(), step, state, state, state, state, vector, vector, vector, into, vector, out, vector, vector, picture,
    )
    out_specs = (
        picture, picture, step, state, state, state, state, vector, vector, vector, into, vector, out, vector, vector,
    )
    return jax.shard_map(
        partial(on_device, mesh.shape["rows"]), mesh=mesh, in_specs=in_specs, out_specs=out_specs, check_vma=False
    )
```

```python
from functools import partial

import jax
import jax.numpy as jnp
from jax import lax
from jax.experimental import pallas as pl
from jax.experimental.pallas import tpu as pltpu
from jax.sharding import PartitionSpec as P


epsilon = 1e-06
bf16 = jnp.bfloat16
f32 = jnp.float32
vmem_bytes = 52 * 1024 * 1024
ahead = 8
band = 16
lane = 128


def dot(a, b, ca, cb):
    return lax.dot_general(a, b, (((ca,), (cb,)), ((), ())), preferred_element_type=f32)


def vmem_spec():
    return pl.BlockSpec(memory_space=pltpu.VMEM)


def smem_spec():
    return pl.BlockSpec(memory_space=pltpu.SMEM)


def any_spec():
    return pl.BlockSpec(memory_space=pl.ANY)


def struct(shape, dtype):
    return jax.ShapeDtypeStruct(shape, dtype)


def params():
    return dict(
        compiler_params=pltpu.CompilerParams(vmem_limit_bytes=vmem_bytes),
        cost_estimate=pl.CostEstimate(flops=1, bytes_accessed=1, transcendentals=0),
    )


def launch(body, name, ins, outs, scratch=(), scalars=(), after=(), through=()):
    given, kept = len(scalars) + len(ins), len(after) + len(through)

    def run(*refs):
        body(*refs[:given], *refs[given + kept:given + kept + len(outs)], *refs[given + kept + len(outs) + len(through):])

    return pl.pallas_call(
        run,
        in_specs=[smem_spec()] * len(scalars) + [vmem_spec()] * len(ins) + [any_spec()] * kept,
        out_specs=[vmem_spec()] * len(outs) + [any_spec()] * len(through),
        out_shape=list(outs) + [struct(value.shape, value.dtype) for value in through],
        scratch_shapes=list(scratch),
        input_output_aliases={given + len(after) + k: len(outs) + k for k in range(len(through))},
        name=name,
        **params(),
    )(*scalars, *ins, *after, *through)


def swap(parts, number, chunk):
    width = 16 << chunk
    lanes = lax.broadcasted_iota(jnp.int32, parts[0].shape, 1)
    low = (lanes // width) % 2 == 0
    parts = list(parts)
    for i in range(8):
        j = i | (1 << number)
        if i != j:
            a, b = parts[i], parts[j]
            parts[i] = jnp.where(low, a, pltpu.roll(b, width, 1))
            parts[j] = jnp.where(low, pltpu.roll(a, lane - width, 1), b)
    return parts


half_rows = 96
strip = 32


def pieces_from_rows(get, out_ref, kind):
    for at in range(0, half_rows, strip):
        parts = [get((i >> 1) & 1, i & 1, slice((i >> 2) * half_rows + at, (i >> 2) * half_rows + at + strip)) for i in range(8)]
        for bit in range(3):
            parts = swap(parts, bit, bit)
        for target in range(8):
            out_ref[target, kind, at:at + strip, :] = parts[target].astype(bf16)


def rows_from_pieces(in_ref, kind, put):
    for at in range(0, half_rows, strip):
        parts = [in_ref[source, kind, at:at + strip, :].astype(f32) for source in range(8)]
        for bit in range(3):
            parts = swap(parts, bit, bit)
        for i in range(8):
            put((i >> 1) & 1, i & 1, slice((i >> 2) * half_rows + at, (i >> 2) * half_rows + at + strip), parts[i])


def pieces_from_cols(get, out_ref, kind):
    for at in range(0, half_rows, strip):
        parts = []
        for i in range(8):
            upper, half, canvas = i >> 2, (i >> 1) & 1, i & 1
            first = (canvas * 2 + upper) * lane
            parts.append(get(slice(half * half_rows + at, half * half_rows + at + strip), slice(first, first + lane)))
        parts = swap(swap(parts, 1, 2), 0, 1)
        for target in range(8):
            out_ref[target, kind, at:at + strip, :] = parts[target].astype(bf16)


def cols_from_pieces(in_ref, kind, out_ref):
    for at in range(0, half_rows, strip):
        parts = [in_ref[source, kind, at:at + strip, :].astype(f32) for source in range(8)]
        parts = swap(swap(parts, 1, 2), 0, 1)
        for i in range(8):
            upper, half, canvas = i >> 2, (i >> 1) & 1, i & 1
            first = (canvas * 2 + upper) * lane
            out_ref[half * half_rows + at:half * half_rows + at + strip, first:first + lane] = parts[i].astype(out_ref.dtype)


def piece_shape(kinds):
    return struct((8, kinds, half_rows, lane), bf16)


def state_powers(step, decay, frequency):
    size = jnp.exp(-step * decay)
    turn = step * frequency
    z = (size * jnp.cos(turn), size * jnp.sin(turn))

    def times(p, q):
        return (p[0] * q[0] - p[1] * q[1], p[0] * q[1] + p[1] * q[0])

    z2 = times(z, z)
    z3 = times(z2, z)
    z4 = times(z2, z2)
    return [None, z, z2, z3, z4, times(z4, z), times(z4, z2), times(z4, z3)], times(z4, z4), times


def pack_lanes(value):
    half = value.shape[0] // 2
    return jnp.concatenate([value[:half], value[half:]], axis=1)


def unpack_lanes(value):
    half = value.shape[1] // 2
    return jnp.concatenate([value[:, :half], value[:, half:]], axis=0)


def s4_section(direction, length, section, step_ref, decay_ref, freq_ref, real_ref, imag_ref, q_ref, flat_ref):
    channels = step_ref.shape[2]
    step = jnp.exp(step_ref[section, direction:direction + 1, :])
    step = jnp.concatenate([step, step], axis=1)
    decay = jnp.exp(pack_lanes(decay_ref[section, direction]))
    powers, z8, times = state_powers(step, decay, pack_lanes(freq_ref[section, direction]))
    for a in range(1, ahead):
        q_ref[2 * a] = powers[a][0]
        q_ref[2 * a + 1] = powers[a][1]
    q_ref[0] = z8[0]
    q_ref[1] = z8[1]

    def block(b, carry):
        pr, pi = carry
        rows = [jnp.sum(pr, axis=0, keepdims=True)]
        for a in range(1, ahead):
            rows.append(jnp.sum(pr * q_ref[2 * a] - pi * q_ref[2 * a + 1], axis=0, keepdims=True))
        flat_ref[pl.ds(pl.multiple_of(b * ahead, ahead), ahead), :] = step * jnp.concatenate(rows, axis=0)
        zr, zi = q_ref[0], q_ref[1]
        return (pr * zr - pi * zi, pr * zi + pi * zr)

    start = (pack_lanes(real_ref[section, direction]), pack_lanes(imag_ref[section, direction]))
    lax.fori_loop(0, length // ahead, block, start)
    flat = jnp.transpose(flat_ref[...])
    return (flat[:channels] + flat[channels:]).astype(bf16).astype(f32)


def s4_scratch(states, channels):
    return [pltpu.VMEM((2 * ahead, states // 2, 2 * channels), f32), pltpu.VMEM((lane, 2 * channels), f32)]


def s4_wide_body(length, section, copies, step_ref, decay_ref, freq_ref, real_ref, imag_ref, out_ref, q_ref, flat_ref):
    kernel = s4_section(1, length, section, step_ref, decay_ref, freq_ref, real_ref, imag_ref, q_ref, flat_ref)
    out_ref[...] = jnp.transpose(jnp.concatenate([kernel] * copies, axis=0))


def s4_wide(section, length, copies, log_step, *states):
    channels = states[0].shape[3]
    return launch(
        partial(s4_wide_body, length, section, copies), "s4_wide", [log_step, *states],
        [struct((lane, copies * channels), f32)], s4_scratch(states[0].shape[2], channels),
    )[0]


def s4_rest_body(lengths, copies, step_ref, decay_ref, freq_ref, real_ref, imag_ref, upstream_ref, pack_ref,
                 tall_low, tall_top, wide_top, scaled_ref, sums_ref, q_ref, flat_ref):
    refs = (step_ref, decay_ref, freq_ref, real_ref, imag_ref, q_ref, flat_ref)
    tall_low[...] = s4_section(0, lengths[0], 0, *refs)
    tall_top[...] = s4_section(0, lengths[0], 1, *refs)
    wide_top[...] = jnp.transpose(jnp.concatenate([s4_section(1, lengths[1], 1, *refs)] * copies, axis=0))
    scale = pack_ref[:, 4:5]
    total = jnp.zeros(scale.shape, f32)
    rows = upstream_ref.shape[1]
    for canvas in range(upstream_ref.shape[0]):
        for row in range(rows):
            scaled = upstream_ref[canvas, row].astype(f32) * scale
            at = (canvas * rows + row) * lane
            scaled_ref[:, at:at + lane] = scaled.astype(bf16)
            total += jnp.sum(scaled, axis=1, keepdims=True)
    put_columns(sums_ref, [total])


def s4_rest(lengths, copies, log_step, states, upstream, pack, after):
    channels = states[0].shape[3]
    pixels = upstream.shape[0] * upstream.shape[1] * lane
    column = struct((channels, lane), f32)
    return launch(
        partial(s4_rest_body, lengths, copies), "s4_rest", [log_step, *states, upstream, pack],
        [column, column, struct((lane, copies * channels), f32), struct((channels, pixels), bf16), column],
        s4_scratch(states[0].shape[2], channels), after=after,
    )


def twice(rows):
    return jnp.concatenate([rows, rows], axis=0)


def pull_section(direction, length, grads_ref, step_ref, decay_ref, freq_ref, real_ref, imag_ref,
                 dstep_ref, ddecay_ref, dfreq_ref, dreal_ref, dimag_ref, turn_ref, spread_ref, q_ref, s_ref):
    channels = step_ref.shape[2]
    states = decay_ref.shape[2]
    tiles = 2 * channels // lane
    step = jnp.exp(step_ref[0, direction:direction + 1, :])
    decay = jnp.exp(decay_ref[0, direction])
    freq = freq_ref[0, direction]
    wide_step = jnp.concatenate([step, step], axis=1)
    powers, z8, times = state_powers(wide_step, pack_lanes(decay), pack_lanes(freq))
    for a in range(ahead):
        for part in range(2):
            value = (z8 if a == 0 else powers[a])[part]
            for t in range(tiles):
                q_ref[2 * a + part, t] = value[:, t * lane:(t + 1) * lane]
    first = (1 - direction) * lane
    grads = grads_ref[0, :, first:first + lane].astype(f32)
    turn_ref[0:channels, :] = grads
    turn_ref[channels:2 * channels, :] = grads
    flat = jnp.transpose(turn_ref[...])
    for place in range(length):
        for t in range(tiles):
            spread_ref[t, place] = jnp.broadcast_to(flat[place:place + 1, t * lane:(t + 1) * lane], (8, lane))
    turns = length // ahead
    groups = states // 32

    def group(index, carry):
        t = index // groups
        part = pl.ds(pl.multiple_of(lax.rem(index, groups) * 16, 16), 16)
        q = [(q_ref[2 * a, t, part, :], q_ref[2 * a + 1, t, part, :]) for a in range(ahead)]
        zr, zi = q[0]

        def block(turn, sums):
            s0r, s0i, s1r, s1i = sums
            b = turns - 1 - turn
            t0r = t0i = t1r = t1i = None
            for a in range(ahead - 1, 0, -1):
                g = twice(spread_ref[t, b * ahead + a])
                x, y = g * q[a][0], g * q[a][1]
                t0r, t0i = (x, y) if t0r is None else (t0r + x, t0i + y)
                t1r, t1i = (t0r, t0i) if t1r is None else (t1r + t0r, t1i + t0i)
            t0r = t0r + twice(spread_ref[t, b * ahead])
            base = (b * ahead).astype(f32)
            v1r, v1i = t1r + base * t0r, t1i + base * t0i
            return (
                s0r * zr - s0i * zi + t0r,
                s0r * zi + s0i * zr + t0i,
                s1r * zr - s1i * zi + v1r,
                s1r * zi + s1i * zr + v1i,
            )

        zero = jnp.zeros((16, lane), f32)
        sums = lax.fori_loop(0, turns, block, (zero, zero, zero, zero))
        for k in range(4):
            s_ref[k, t, part, :] = sums[k]
        return carry

    lax.fori_loop(0, tiles * groups, group, 0)
    s0r, s0i, s1r, s1i = [
        unpack_lanes(jnp.concatenate([s_ref[k, t] for t in range(tiles)], axis=1)) for k in range(4)
    ]
    real, imag = real_ref[0, direction], imag_ref[0, direction]
    dreal = step * s0r
    dimag = -step * s0i
    ddecay = -step * step * decay * (real * s1r - imag * s1i)
    dfreq = -step * step * (real * s1i + imag * s1r)
    dreal_ref[0, direction] = dreal
    dimag_ref[0, direction] = dimag
    ddecay_ref[0, direction] = ddecay
    dfreq_ref[0, direction] = dfreq
    dstep_ref[0, direction:direction + 1, :] = jnp.sum(
        real * dreal + imag * dimag + ddecay + freq * dfreq, axis=0, keepdims=True
    )
    return flat


def pull_body(lengths, grads_ref, step_ref, decay_ref, freq_ref, real_ref, imag_ref, dstep_ref, ddecay_ref, dfreq_ref, dreal_ref,
              dimag_ref, skip_ref, gain_ref, shift_ref, units_ref, bias_ref, scale_ref, *scratch):
    channels = step_ref.shape[2]
    refs = (grads_ref, step_ref, decay_ref, freq_ref, real_ref, imag_ref, dstep_ref, ddecay_ref, dfreq_ref, dreal_ref, dimag_ref)
    pull_section(1, lengths[1], *refs, *scratch)
    rows = pull_section(0, lengths[0], *refs, *scratch)
    first = lengths[0]
    if first + 16 > lane:
        turn_ref = scratch[0]
        turn_ref[0:channels, :] = grads_ref[0, :, 2 * lane:].astype(f32)
        rows, first = jnp.transpose(turn_ref[...]), first - lane
    per = units_ref.shape[1] // channels
    section = pl.program_id(0)

    def row(index):
        return rows[first + index:first + index + 1, 0:channels]

    def put(at):
        for index, ref in enumerate((skip_ref, gain_ref, shift_ref, bias_ref)):
            ref[at:at + 1, :] = row(index)
        units_ref[at:at + 1, :] = jnp.concatenate([row(4 + index) for index in range(per)], axis=1)

    @pl.when(section == 0)
    def _():
        put(0)
        scale_ref[0:1, :] = row(4 + per)
        scale_ref[1:2, :] = row(5 + per)

    @pl.when(section == 1)
    def _():
        put(1)


def s4_pullback(lengths, units, grads, log_step, log_decay, frequency, coef_real, coef_imag, after):
    states, channels = log_decay.shape[2], log_decay.shape[3]
    whole = pl.BlockSpec((1, 2, states, channels), lambda i: (i, 0, 0, 0))
    row = pl.BlockSpec((1, 2, channels), lambda i: (i, 0, 0))
    tiles = 2 * channels // lane
    vectors = [(2, channels)] * 3 + [(2, units)] + [(2, channels)] * 2

    def body(*refs):
        pull_body(lengths, *refs[:6], *refs[6 + len(after):])

    return pl.pallas_call(
        body,
        grid=(2,),
        in_specs=[pl.BlockSpec((1,) + grads.shape[1:], lambda i: (i, 0, 0)), row, whole, whole, whole, whole]
        + [any_spec()] * len(after),
        out_specs=[row, whole, whole, whole, whole] + [pl.BlockSpec(shape, lambda i: (0, 0)) for shape in vectors],
        out_shape=[struct(log_step.shape, f32)] + [struct(log_decay.shape, f32)] * 4 + [struct(shape, f32) for shape in vectors],
        scratch_shapes=[
            pltpu.VMEM((2 * channels, lane), f32),
            pltpu.VMEM((tiles, lane, 8, lane), f32),
            pltpu.VMEM((2 * ahead, tiles, states // 2, lane), f32),
            pltpu.VMEM((4, tiles, states // 2, lane), f32),
        ],
        name="s4_pullback",
        **params(),
    )(grads, log_step, log_decay, frequency, coef_real, coef_imag, *after)


pad = 8


def lane_tiles(value):
    return [value[:, at:at + lane] for at in range(0, value.shape[1], lane)]


def load_tiles(value, ref, first):
    for index, part in enumerate(lane_tiles(value)):
        ref[index, first:first + part.shape[0], :] = part


def width_conv(canvas, sign, signal_ref, kernel_ref, age_ref, reach_ref, out_ref):
    tiles, width = out_ref.shape[0], out_ref.shape[1]
    per = band // 8
    for index in range(width // band):
        ages = [age_ref[canvas, pl.ds((index * per + k) * 8, 8), :] for k in range(per)]

        def body(q, sums):
            sums = list(sums)
            places = [
                pl.multiple_of(jnp.clip(index * per + k - sign * q, 0, width // 8 - 1) * 8, 8) for k in range(per)
            ]
            for s in range(ahead):
                lag = q * ahead + s
                seen = [ages[k] >= lag for k in range(per)]
                for t in range(tiles):
                    value = jnp.broadcast_to(kernel_ref[t, pl.ds(lag, 1), :], (8, lane))
                    for k in range(per):
                        x = signal_ref[t, pl.ds(places[k] + (pad - sign * s), 8), :]
                        sums[k * tiles + t] += value * jnp.where(seen[k], x, 0.0)
            return tuple(sums)

        zero = jnp.zeros((8, lane), f32)
        sums = lax.fori_loop(0, reach_ref[canvas, index], body, (zero,) * (per * tiles))
        for k in range(per):
            for t in range(tiles):
                out_ref[t, pl.ds((index * per + k) * 8, 8), :] = sums[k * tiles + t]


def width_products(canvas, signal_ref, grad_ref, age_ref, reach_ref, total_ref):
    tiles, width = grad_ref.shape[0], grad_ref.shape[1]
    per = band // 8
    for index in range(width // band):
        ages = [age_ref[canvas, pl.ds((index * per + k) * 8, 8), :] for k in range(per)]
        grads = [[grad_ref[t, pl.ds((index * per + k) * 8, 8), :] for t in range(tiles)] for k in range(per)]

        def body(q, carry):
            places = [
                pl.multiple_of(jnp.clip(index * per + k - q, 0, width // 8 - 1) * 8, 8) for k in range(per)
            ]
            for s in range(ahead):
                lag = q * ahead + s
                seen = [ages[k] >= lag for k in range(per)]
                for t in range(tiles):
                    total = total_ref[t, lag]
                    for k in range(per):
                        x = signal_ref[t, pl.ds(places[k] + (pad - s), 8), :]
                        total += grads[k][t] * jnp.where(seen[k], x, 0.0)
                    total_ref[t, lag] = total
            return carry

        lax.fori_loop(0, reach_ref[canvas, index], body, 0)


def stacked_rows(ref, canvas):
    picture = ref[canvas].astype(f32)
    return jnp.transpose(picture.reshape(-1, picture.shape[2]))


def unstacked(ref, rows):
    flat = jnp.concatenate([jnp.transpose(ref[t]) for t in range(ref.shape[0])], axis=0)
    return flat.reshape(rows, flat.shape[0] // rows, flat.shape[1])


def width_scratch(rows, channels):
    tiles = rows * channels // lane
    return [
        pltpu.VMEM((tiles, lane + 2 * pad, lane), f32),
        pltpu.VMEM((tiles, lane, lane), f32),
        pltpu.VMEM((tiles, lane, lane), f32),
    ]


def convolve_canvas(canvas, sign, picture_ref, age_ref, reach_ref, signal_ref, kernel_ref, sum_ref):
    load_tiles(stacked_rows(picture_ref, canvas), signal_ref, pad)
    width_conv(canvas, sign, signal_ref, kernel_ref, age_ref, reach_ref, sum_ref)
    return unstacked(sum_ref, picture_ref.shape[1])


def wide_forward_body(packed, reach_ref, picture_ref, wide_ref, age_ref, out_ref, signal_ref, kernel_ref, sum_ref, *held):
    load_tiles(wide_ref[...], kernel_ref, 0)
    across_ref = held[0] if packed else out_ref
    for canvas in range(picture_ref.shape[0]):
        across_ref[canvas] = convolve_canvas(
            canvas, 1, picture_ref, age_ref, reach_ref, signal_ref, kernel_ref, sum_ref
        ).astype(across_ref.dtype)
    if packed:
        pieces_from_rows(lambda b, r, c: across_ref[b, r, c, :], out_ref, 0)
        pieces_from_rows(lambda b, r, c: picture_ref[b, r, c, :].astype(f32), out_ref, 1)


def wide_forward(packed, picture, wide, age, reach):
    out = piece_shape(2) if packed else struct(picture.shape, bf16)
    scratch = width_scratch(picture.shape[1], picture.shape[2])
    return launch(
        partial(wide_forward_body, packed), "wide_forward", [picture, wide, age], [out],
        scratch + [pltpu.VMEM(picture.shape, f32)] * packed, scalars=[reach],
    )[0]


def split_refs(packed, refs, held):
    return (refs[0], refs[1:]) if packed else (refs[:held], refs[held:])


def wide_mixed_body(packed, reach_ref, *refs):
    if packed:
        pieces, wide_ref, age_ref, pack_ref, out_ref, tall_ref, stream_ref, signal_ref, kernel_ref, sum_ref = refs
        for kind, ref in enumerate((tall_ref, stream_ref)):
            def put(b, r, c, value, ref=ref):
                ref[b, r, c, :] = value.astype(bf16)
            rows_from_pieces(pieces, kind, put)
    else:
        tall_ref, stream_ref, wide_ref, age_ref, pack_ref, out_ref, signal_ref, kernel_ref, sum_ref = refs
    rows = tall_ref.shape[1]
    skip = pack_ref[:, 0:1]
    load_tiles(wide_ref[...], kernel_ref, 0)
    for canvas in range(tall_ref.shape[0]):
        mixer = convolve_canvas(canvas, 1, tall_ref, age_ref, reach_ref, signal_ref, kernel_ref, sum_ref)
        for row in range(rows):
            at = (canvas * rows + row) * lane
            out_ref[:, at:at + lane] = (
                mixer[row] + skip * stream_ref[canvas, row].astype(f32)
            ).astype(bf16)


def wide_mixed(packed, moved, picture, wide, age, reach, pack):
    canvases, rows, channels, width = picture
    outs = [struct((channels, canvases * rows * lane), bf16)] + [struct(picture, bf16)] * (2 * packed)
    got = launch(
        partial(wide_mixed_body, packed), "wide_mixed", [*moved, wide, age, pack], outs,
        width_scratch(rows, channels), scalars=[reach],
    )
    return tuple(got) if packed else (got[0], *moved)


def norm_backward(grads, mixed_ref, stats_ref, pack_ref, channels_all):
    channels = mixed_ref.shape[0]
    keep, near, far = grads
    total = keep[...].astype(f32) + near[...].astype(f32) + far[...].astype(f32)
    normed_grad = total[0:channels]
    scaled_mean = total[channels:channels + 1] / channels_all
    paired_mean = total[channels + 1:channels + 2] / channels_all
    average, inverse = stats_ref[0:1, :], stats_ref[1:2, :]
    centred = (mixed_ref[...].astype(f32) - average) * inverse
    gain = pack_ref[:, 1:2]
    mixed_grad = inverse * (normed_grad * gain - scaled_mean - centred * paired_mean)
    return (
        mixed_grad,
        jnp.sum(normed_grad * centred, axis=1, keepdims=True),
        jnp.sum(normed_grad, axis=1, keepdims=True),
    )


def put_columns(ref, columns):
    places = lax.broadcasted_iota(jnp.int32, ref.shape, 1)
    value = jnp.zeros(ref.shape, f32)
    for index, column in enumerate(columns):
        value = jnp.where(places == index, column, value)
    ref[...] = value


def wide_norm_back_body(packed, channels_all, reach_ref, keep_ref, near_ref, far_ref, mixed_ref, stats_ref, pack_ref,
                        stream_ref, cotangent_ref, wide_ref, fore_ref, *refs):
    if packed:
        out_ref, grad_ref, sums_ref, signal_ref, kernel_ref, sum_ref, conv_ref, rest_ref = refs
    else:
        conv_ref, rest_ref, grad_ref, sums_ref, signal_ref, kernel_ref, sum_ref = refs
    canvases, rows = conv_ref.shape[0], conv_ref.shape[1]
    mixed_grad, gain_grad, shift_grad = norm_backward(
        (keep_ref, near_ref, far_ref), mixed_ref, stats_ref, pack_ref, channels_all
    )
    skip = pack_ref[:, 0:1]
    skip_grad = jnp.zeros_like(gain_grad)
    load_tiles(wide_ref[...], kernel_ref, 0)
    for canvas in range(canvases):
        for row in range(rows):
            at = (canvas * rows + row) * lane
            part = mixed_grad[:, at:at + lane]
            grad_ref[canvas, row] = part.astype(bf16)
            skip_grad += jnp.sum(part * stream_ref[canvas, row].astype(f32), axis=1, keepdims=True)
            rest_ref[canvas, row] = (cotangent_ref[canvas, row].astype(f32) + skip * part).astype(rest_ref.dtype)
        conv_ref[canvas] = convolve_canvas(
            canvas, -1, grad_ref, fore_ref, reach_ref, signal_ref, kernel_ref, sum_ref
        ).astype(conv_ref.dtype)
    put_columns(sums_ref, [skip_grad, gain_grad, shift_grad])
    if packed:
        pieces_from_rows(lambda b, r, c: conv_ref[b, r, c, :], out_ref, 0)
        pieces_from_rows(lambda b, r, c: rest_ref[b, r, c, :], out_ref, 1)


def wide_norm_back(packed, channels_all, grads, mixed, stats, pack, stream, cotangent, wide, fore, reach, after):
    plain = struct(stream.shape, bf16)
    sums = struct((stream.shape[2], lane), f32)
    got = launch(
        partial(wide_norm_back_body, packed, channels_all), "wide_norm_back",
        [*grads, mixed, stats, pack, stream, cotangent, wide, fore],
        [piece_shape(2), plain, sums] if packed else [plain, plain, plain, sums],
        width_scratch(stream.shape[1], stream.shape[2]) + [pltpu.VMEM(stream.shape, f32)] * (2 * packed),
        scalars=[reach], after=after,
    )
    return got[:-2], got[-2], got[-1]


def kernel_products(grad_ref, input_ref, age_ref, reach_ref, signal_ref, flat_ref, sum_ref, total_ref):
    channels = grad_ref.shape[2]
    rows = grad_ref.shape[1]
    total_ref[...] = jnp.zeros(total_ref.shape, f32)
    for canvas in range(grad_ref.shape[0]):
        load_tiles(stacked_rows(input_ref, canvas), signal_ref, pad)
        load_tiles(stacked_rows(grad_ref, canvas), flat_ref, 0)
        width_products(canvas, signal_ref, flat_ref, age_ref, reach_ref, total_ref)

    def reduce(index, carry):
        at = pl.multiple_of(index * 8, 8)
        for t in range(sum_ref.shape[0]):
            sum_ref[t, pl.ds(at, 8), :] = jnp.sum(total_ref[t, pl.ds(at, 8)], axis=1)
        return carry

    lax.fori_loop(0, lane // 8, reduce, 0)
    picture = unstacked(sum_ref, rows)
    return sum(picture[row] for row in range(rows))


def products_scratch(rows, channels):
    return width_scratch(rows, channels) + [pltpu.VMEM((rows * channels // lane, lane, 8, lane), f32)]


def wide_top_grad_body(reach_ref, grad_ref, input_ref, age_ref, out_ref, *scratch):
    out_ref[...] = kernel_products(grad_ref, input_ref, age_ref, reach_ref, *scratch)


def wide_top_grad(grad, inputs, age, reach, after=()):
    channels = grad.shape[2]
    return launch(
        wide_top_grad_body, "wide_top_grad", [grad, inputs, age], [struct((channels, lane), f32)],
        products_scratch(grad.shape[1], channels), scalars=[reach], after=after,
    )[0]


def wide_last_body(packed, forth_reach, back_reach, *refs):
    if packed:
        pieces, input_ref, wide_ref, age_ref, fore_ref, held_ref, top_ref, out_ref, total_out, *refs = refs
        signal_ref, kernel_ref, sum_ref, total_ref, grad_ref, rest_ref = refs

        def put_grad(b, r, c, value):
            grad_ref[b, r, c, :] = value.astype(bf16)

        def put_rest(b, r, c, value):
            rest_ref[b, r, c, :] = value

        rows_from_pieces(pieces, 0, put_grad)
        rows_from_pieces(pieces, 1, put_rest)
    else:
        grad_ref, rest_ref, input_ref, wide_ref, age_ref, fore_ref, held_ref, top_ref, out_ref, total_out, *refs = refs
        signal_ref, kernel_ref, sum_ref, total_ref = refs
    total_out[0, :, 0:lane] = kernel_products(
        grad_ref, input_ref, age_ref, forth_reach, signal_ref, kernel_ref, sum_ref, total_ref
    ).astype(bf16)
    total_out[0, :, lane:] = held_ref[...].astype(bf16)
    total_out[1] = top_ref[...]
    load_tiles(wide_ref[...], kernel_ref, 0)
    for canvas in range(grad_ref.shape[0]):
        value = convolve_canvas(canvas, -1, grad_ref, fore_ref, back_reach, signal_ref, kernel_ref, sum_ref)
        out_ref[canvas] = (value + rest_ref[canvas].astype(f32)).astype(bf16)


def wide_last(packed, moved, picture, inputs, wide, age, fore, held, top, forth_reach, back_reach, after):
    plain = struct(picture, bf16)
    scratch = products_scratch(picture[1], picture[2])
    if packed:
        scratch += [pltpu.VMEM(picture, bf16), pltpu.VMEM(picture, f32)]
    return launch(
        partial(wide_last_body, packed), "wide_last", [*moved, inputs, wide, age, fore, held, top],
        [plain, struct((2,) + top.shape, bf16)], scratch, scalars=[forth_reach, back_reach], after=after,
    )


def height_loop(count, body, carry):
    if count <= 16:
        for lag in range(count):
            carry = body(lag, carry)
        return carry
    return lax.fori_loop(0, count, body, carry)


def tap(kernel, lag):
    if isinstance(lag, int):
        return kernel[:, lag:lag + 1]
    places = lax.broadcasted_iota(jnp.int32, kernel.shape, 1)
    return jnp.sum(jnp.where(places == lag, kernel, 0.0), axis=1, keepdims=True)


def moved_by(value, shift):
    size = value.shape[1]
    if not isinstance(shift, int):
        return pltpu.roll(value, lax.rem(shift + size, size), 1)
    shift %= size
    return pltpu.roll(value, shift, 1) if shift else value


def height_conv(get, put, channels, kernel_ref, age_ref, sign, height):
    for at in range(0, channels, strip):
        rows = slice(at, at + strip)
        kernel = kernel_ref[rows, :]
        for canvas in range(age_ref.shape[0]):
            value, age = get(rows, canvas), age_ref[canvas]
            columns = value.shape[1] // height

            def body(lag, total):
                return total + tap(kernel, lag) * jnp.where(age >= lag, moved_by(value, sign * lag * columns), 0.0)

            put(rows, canvas, height_loop(height, body, jnp.zeros_like(value)))


def height_products(grads, values, ages, height):
    columns = values[0].shape[1] // height
    channels = values[0].shape[0]
    places = lax.broadcasted_iota(jnp.int32, (channels, lane), 1)

    def body(lag, total):
        part = None
        for grad, value, age in zip(grads, values, ages, strict=True):
            product = grad * jnp.where(age >= lag, moved_by(value, lag * columns), 0.0)
            for piece in lane_tiles(product):
                part = piece if part is None else part + piece
        return total + jnp.where(places == lag, jnp.sum(part, axis=1, keepdims=True), 0.0)

    return height_loop(height, body, jnp.zeros((channels, lane), f32))


def canvas_cut(ref, canvas, canvases):
    each = ref.shape[1] // canvases
    return slice(canvas * each, (canvas + 1) * each)


def tall_mixed_body(packed, height, *refs):
    if packed:
        pieces, kernel_ref, age_ref, pack_ref, out_ref, across_ref, stream_ref = refs
        cols_from_pieces(pieces, 0, across_ref)
        cols_from_pieces(pieces, 1, stream_ref)
    else:
        across_ref, stream_ref, kernel_ref, age_ref, pack_ref, out_ref = refs
    canvases = age_ref.shape[0]

    def get(rows, canvas):
        return across_ref[rows, canvas_cut(across_ref, canvas, canvases)].astype(f32)

    def put(rows, canvas, mixer):
        cut = canvas_cut(across_ref, canvas, canvases)
        out_ref[rows, cut] = (mixer + pack_ref[rows, 0:1] * stream_ref[rows, cut].astype(f32)).astype(bf16)

    height_conv(get, put, out_ref.shape[0], kernel_ref, age_ref, 1, height)


def tall_mixed(packed, height, moved, cols, kernel, age, pack, after):
    got = launch(
        partial(tall_mixed_body, packed, height), "tall_mixed", [*moved, kernel, age, pack],
        [struct(cols, bf16)] * (1 + 2 * packed), after=after,
    )
    return tuple(got) if packed else (got[0], *moved)


def tall_next_body(packed, height, keep_ref, near_ref, far_ref, stream_ref, pack_ref, kernel_ref, age_ref,
                   next_ref, branch_ref, out_ref, *held):
    canvases = age_ref.shape[0]
    conv_ref = held[0] if packed else out_ref

    def get(rows, canvas):
        cut = canvas_cut(stream_ref, canvas, canvases)
        branch = (
            keep_ref[rows, cut].astype(f32) + near_ref[rows, cut].astype(f32) + far_ref[rows, cut].astype(f32)
            + pack_ref[rows, 3:4]
        )
        branch_ref[rows, cut] = branch
        low = (stream_ref[rows, cut].astype(f32) + pack_ref[rows, 4:5] * branch).astype(bf16)
        next_ref[rows, cut] = low
        return low.astype(f32)

    def put(rows, canvas, value):
        conv_ref[rows, canvas_cut(stream_ref, canvas, canvases)] = value.astype(conv_ref.dtype)

    height_conv(get, put, stream_ref.shape[0], kernel_ref, age_ref, 1, height)
    if packed:
        pieces_from_cols(lambda rows, cut: conv_ref[rows, cut], out_ref, 0)
        pieces_from_cols(lambda rows, cut: next_ref[rows, cut].astype(f32), out_ref, 1)


def tall_next(packed, height, branches, stream, pack, kernel, age):
    got = launch(
        partial(tall_next_body, packed, height), "tall_next", [*branches, stream, pack, kernel, age],
        [struct(stream.shape, bf16), struct(stream.shape, f32), piece_shape(2) if packed else struct(stream.shape, bf16)],
        [pltpu.VMEM(stream.shape, f32)] * packed,
    )
    return got[0], got[1], [got[2]] if packed else [got[2], got[0]]


def tall_back_body(packed, height, *refs):
    if packed:
        pieces, kernel_ref, fore_ref, pack_ref, branch_ref, grad_ref, low_ref, sums_ref, conv_ref, rest_ref = refs
        cols_from_pieces(pieces, 0, conv_ref)
        cols_from_pieces(pieces, 1, rest_ref)
    else:
        conv_ref, rest_ref, kernel_ref, fore_ref, pack_ref, branch_ref, grad_ref, low_ref, sums_ref = refs
    canvases = fore_ref.shape[0]

    def get(rows, canvas):
        return conv_ref[rows, canvas_cut(conv_ref, canvas, canvases)].astype(f32)

    def put(rows, canvas, value):
        cut = canvas_cut(conv_ref, canvas, canvases)
        grad = rest_ref[rows, cut].astype(f32) + value
        grad_ref[rows, cut] = grad
        low_ref[rows, cut] = (grad * pack_ref[rows, 4:5]).astype(bf16)

    height_conv(get, put, conv_ref.shape[0], kernel_ref, fore_ref, -1, height)
    sums_ref[...] = jnp.zeros(sums_ref.shape, f32)


def tall_back(packed, height, moved, cols, kernel, fore, pack, branch, after, through):
    got = launch(
        partial(tall_back_body, packed, height), "tall_back", [*moved, kernel, fore, pack, branch],
        [struct(cols, f32), struct(cols, bf16), struct((cols[0], lane), f32)] + [struct(cols, bf16)] * packed,
        [pltpu.VMEM(cols, f32)] * packed, after=after, through=through,
    )
    return got[0], got[1], got[3] if packed else moved[0], *got[3 + packed:]


def tall_norm_back_body(packed, height, channels_all, keep_ref, near_ref, far_ref, mixed_ref, stats_ref, pack_ref, stream_ref,
                        grad_ref, kernel_ref, fore_ref, *refs):
    if packed:
        out_ref, low_ref, sums_ref, conv_ref, rest_ref = refs
    else:
        conv_ref, rest_ref, low_ref, sums_ref = refs
    canvases = fore_ref.shape[0]
    mixed_grad, gain_grad, shift_grad = norm_backward(
        (keep_ref, near_ref, far_ref), mixed_ref, stats_ref, pack_ref, channels_all
    )
    low_ref[...] = mixed_grad.astype(bf16)
    rest_ref[...] = (grad_ref[...] + pack_ref[:, 0:1] * mixed_grad).astype(rest_ref.dtype)
    skip_grad = jnp.sum(mixed_grad * stream_ref[...].astype(f32), axis=1, keepdims=True)

    def get(rows, canvas):
        return low_ref[rows, canvas_cut(low_ref, canvas, canvases)].astype(f32)

    def put(rows, canvas, value):
        conv_ref[rows, canvas_cut(low_ref, canvas, canvases)] = value.astype(conv_ref.dtype)

    height_conv(get, put, low_ref.shape[0], kernel_ref, fore_ref, -1, height)
    put_columns(sums_ref, [skip_grad, gain_grad, shift_grad])
    if packed:
        pieces_from_cols(lambda rows, cut: conv_ref[rows, cut], out_ref, 0)
        pieces_from_cols(lambda rows, cut: rest_ref[rows, cut], out_ref, 1)


def tall_norm_back(packed, height, channels_all, grads, mixed, stats, pack, stream, grad, kernel, fore, after):
    plain, sums = struct(mixed.shape, bf16), struct((mixed.shape[0], lane), f32)
    got = launch(
        partial(tall_norm_back_body, packed, height, channels_all), "tall_norm_back",
        [*grads, mixed, stats, pack, stream, grad, kernel, fore],
        [piece_shape(2), plain, sums] if packed else [plain, plain, plain, sums],
        [pltpu.VMEM(mixed.shape, f32)] * (2 * packed), after=after,
    )
    return got[:-2], got[-2], got[-1]


def tall_products(height, grad_ref, input_ref, age_ref, put):
    canvases = age_ref.shape[0]
    for at in range(0, grad_ref.shape[0], strip):
        rows = slice(at, at + strip)
        cuts = [canvas_cut(grad_ref, canvas, canvases) for canvas in range(canvases)]
        put(rows, height_products(
            [grad_ref[rows, cut].astype(f32) for cut in cuts], [input_ref[rows, cut].astype(f32) for cut in cuts],
            [age_ref[canvas] for canvas in range(canvases)], height,
        ))


def held_lanes(height):
    return -(-(height + 16) // lane) * lane


def beside(held, height, columns):
    if held_lanes(height) > lane:
        held = jnp.concatenate([held, jnp.zeros_like(held)], axis=1)
    places = lax.broadcasted_iota(jnp.int32, held.shape, 1)
    held = jnp.where(places < height, held, 0.0)
    for index, column in enumerate(columns):
        held = jnp.where(places == height + index, column, held)
    return held


def unit_columns(units_ref, rows, channels):
    return [units_ref[at + rows.start:at + rows.stop, 0:1] for at in range(0, units_ref.shape[0], channels)]


def tall_top_grad_body(height, grad_ref, input_ref, age_ref, wide_ref, norm_ref, bias_ref, units_ref, out_ref):
    channels = grad_ref.shape[0]

    def put(rows, held):
        columns = [norm_ref[rows, k:k + 1] for k in range(3)] + [bias_ref[rows, 0:1]]
        out_ref[rows, lane:] = beside(held, height, columns + unit_columns(units_ref, rows, channels)).astype(bf16)

    tall_products(height, grad_ref, input_ref, age_ref, put)
    out_ref[:, 0:lane] = wide_ref[...].astype(bf16)


def tall_top_grad(height, grad, inputs, age, wide, norm, bias, units, after):
    return launch(
        partial(tall_top_grad_body, height), "tall_top_grad", [grad, inputs, age, wide, norm, bias, units],
        [struct((grad.shape[0], lane + held_lanes(height)), bf16)], after=after,
    )[0]


def tall_low_grad_body(height, grad_ref, input_ref, age_ref, norm_ref, grad_out_ref, branch_ref, pack_ref, scale_ref, units_ref,
                       out_ref):
    channels = grad_ref.shape[0]

    def put(rows, held):
        grad = grad_out_ref[rows, :]
        columns = [norm_ref[rows, k:k + 1] for k in range(3)]
        columns.append(jnp.sum(grad, axis=1, keepdims=True) * pack_ref[rows, 4:5])
        columns += unit_columns(units_ref, rows, channels)
        columns.append(jnp.sum(grad * branch_ref[rows, :], axis=1, keepdims=True))
        columns.append(scale_ref[rows, 0:1])
        out_ref[rows, :] = beside(held, height, columns)

    tall_products(height, grad_ref, input_ref, age_ref, put)


def tall_low_grad(height, grad, inputs, age, norm, grad_out, branch, pack, scale, units, after):
    return launch(
        partial(tall_low_grad_body, height), "tall_low_grad",
        [grad, inputs, age, norm, grad_out, branch, pack, scale, units],
        [struct((grad.shape[0], held_lanes(height)), f32)], after=after,
    )[0]


root = 0.7978845608028654
cubic = 0.044715


def gather_into(me_ref, parts, whole_ref):
    me = me_ref[0]
    for flip, part in enumerate(parts):
        whole_ref[me ^ flip] = part[...]


def scatter_out(me_ref, whole_ref, outs):
    me = me_ref[0]
    for flip, out in zip((3, 1, 2, 0), outs, strict=True):
        out[...] = whole_ref[me ^ flip]


def gather_shape(me_ref, parts, section, shape_ref):
    gather_into(me_ref, parts, shape_ref)
    every = shape_ref[...].reshape(-1, shape_ref.shape[2])
    return every[:, 2 * section:2 * section + 1], every[:, 2 * section + 1:2 * section + 2]


def mlp_forward(me_ref, parts, full_ref, shape, weight_in_ref, bias_ref, normed_ref, hidden_ref, slope_ref, stats_ref):
    gather_into(me_ref, parts, full_ref)
    mixed = full_ref[...].astype(f32).reshape(-1, full_ref.shape[2])
    average = jnp.mean(mixed, axis=0, keepdims=True)
    moved = mixed - average
    inverse = lax.rsqrt(jnp.mean(moved * moved, axis=0, keepdims=True) + epsilon)
    centred = moved * inverse
    stats_ref[0:1, :] = average
    stats_ref[1:2, :] = inverse
    normed = (centred * shape[0] + shape[1]).astype(bf16)
    normed_ref[...] = normed
    before = dot(weight_in_ref[0], normed, 0, 0) + bias_ref[...]
    square = before * before
    bend = jnp.tanh(root * before * (1.0 + cubic * square))
    half = 0.5 * (1.0 + bend)
    hidden_ref[...] = (before * half).astype(bf16)
    slope_ref[...] = (half + 0.5 * before * (1.0 - bend * bend) * root * (1.0 + 3.0 * cubic * square)).astype(slope_ref.dtype)
    return centred


def mlp_first_body(section, me_ref, own, near, far, cross, shape_own, shape_near, shape_far, shape_cross, weight_in_ref,
                   bias_ref, weight_out_ref,
                   send_far, send_own, keep_far, keep_own, normed_ref, hidden_ref, slope_ref, stats_ref, full_ref, sum_ref,
                   shape_ref):
    shape = gather_shape(me_ref, (shape_own, shape_near, shape_far, shape_cross), section, shape_ref)
    mlp_forward(me_ref, (own, near, far, cross), full_ref, shape, weight_in_ref, bias_ref,
                normed_ref, hidden_ref, slope_ref, stats_ref)
    partial_out = dot(weight_out_ref[0], hidden_ref[...], 0, 0)
    sum_ref[...] = partial_out.astype(bf16).reshape(sum_ref.shape)
    scatter_out(me_ref, sum_ref, (send_far, send_own, keep_far, keep_own))


def mlp_backward(me_ref, parts, full_ref, weight_out_ref, weight_in_ref, slope, gain, centred, sum_ref, outs, before_grad_ref):
    gather_into(me_ref, parts, full_ref)
    grad = full_ref[...].reshape(-1, full_ref.shape[2])
    before_grad = (dot(weight_out_ref[0], grad, 1, 0) * slope).astype(bf16)
    before_grad_ref[...] = before_grad
    normed_part = dot(weight_in_ref[0], before_grad, 1, 0)
    channels = sum_ref.shape[1] - 16
    scaled = normed_part * gain
    scaled_sum = jnp.sum(scaled, axis=0, keepdims=True)
    paired_sum = jnp.sum(scaled * centred, axis=0, keepdims=True)
    places = lax.broadcasted_iota(jnp.int32, (16, grad.shape[1]), 0)
    tail = jnp.where(places == 0, scaled_sum, jnp.where(places == 1, paired_sum, 0.0)).astype(bf16)
    for index in range(sum_ref.shape[0]):
        sum_ref[index, 0:channels, :] = normed_part[index * channels:(index + 1) * channels].astype(bf16)
        sum_ref[index, channels:, :] = tail
    scatter_out(me_ref, sum_ref, outs)


def mlp_top_body(section, me_ref, own, near, far, cross, grad_own, grad_near, grad_far, grad_cross,
                 shape_own, shape_near, shape_far, shape_cross, weight_in_ref, bias_ref, weight_out_ref,
                 back_sf, back_so, back_kf, back_ko, stats_ref, normed_ref, hidden_ref, before_grad_ref,
                 full_ref, back_ref, slope_ref, shape_ref):
    shape = gather_shape(me_ref, (shape_own, shape_near, shape_far, shape_cross), section, shape_ref)
    centred = mlp_forward(me_ref, (own, near, far, cross), full_ref, shape, weight_in_ref, bias_ref,
                          normed_ref, hidden_ref, slope_ref, stats_ref)
    mlp_backward(me_ref, (grad_own, grad_near, grad_far, grad_cross), full_ref, weight_out_ref, weight_in_ref,
                 slope_ref[...], shape[0], centred, back_ref, (back_sf, back_so, back_kf, back_ko), before_grad_ref)


def mlp_back_body(section, me_ref, own, near, far, cross, grad_own, grad_near, grad_far, grad_cross,
                  shape_own, shape_near, shape_far, shape_cross, weight_in_ref, weight_out_ref, slope_ref, stats_ref,
                  back_sf, back_so, back_kf, back_ko, before_grad_ref, full_ref, back_ref, shape_ref):
    shape = gather_shape(me_ref, (shape_own, shape_near, shape_far, shape_cross), section, shape_ref)
    gather_into(me_ref, (own, near, far, cross), full_ref)
    centred = (full_ref[...].astype(f32).reshape(-1, full_ref.shape[2]) - stats_ref[0:1, :]) * stats_ref[1:2, :]
    mlp_backward(me_ref, (grad_own, grad_near, grad_far, grad_cross), full_ref, weight_out_ref, weight_in_ref,
                 slope_ref[...].astype(f32), shape[0], centred, back_ref, (back_sf, back_so, back_kf, back_ko), before_grad_ref)


tile = 256


def pixel_block(rows):
    return pl.BlockSpec((rows, tile), lambda i: (0, i))


def fixed_block(shape):
    return pl.BlockSpec(shape, lambda i: (0,) * len(shape))


def section_block(section, shape):
    return pl.BlockSpec((1,) + shape, lambda i: (section, 0, 0))


def mlp_first(section, me, parts, shaping, weight_in, bias, weight_out):
    own = parts[0]
    channels, pixels = own.shape
    wide, units = weight_in.shape[1], weight_in.shape[2]
    piece = pixel_block(channels)
    return pl.pallas_call(
        partial(mlp_first_body, section),
        grid=(pixels // tile,),
        in_specs=[smem_spec()] + [piece] * 4 + [
            *[fixed_block(shaping[0].shape)] * 4, section_block(section, (wide, units)), fixed_block(bias.shape),
            section_block(section, (units, wide)),
        ],
        out_specs=[piece] * 4 + [pixel_block(wide), pixel_block(units), pixel_block(units), pixel_block(8)],
        out_shape=[struct(own.shape, bf16)] * 4 + [
            struct((wide, pixels), bf16), struct((units, pixels), bf16), struct((units, pixels), bf16), struct((8, pixels), f32),
        ],
        scratch_shapes=[
            pltpu.VMEM((4, channels, tile), bf16), pltpu.VMEM((4, channels, tile), bf16), pltpu.VMEM((4,) + shaping[0].shape, f32),
        ],
        name="mlp_first",
        **params(),
    )(me, *parts, *shaping, weight_in, bias, weight_out)


def mlp_top(section, me, parts, grads, shaping, weight_in, bias, weight_out):
    own = parts[0]
    channels, pixels = own.shape
    wide, units = weight_in.shape[1], weight_in.shape[2]
    piece, back = pixel_block(channels), pixel_block(channels + 16)
    return pl.pallas_call(
        partial(mlp_top_body, section),
        grid=(pixels // tile,),
        in_specs=[smem_spec()] + [piece] * 8 + [
            *[fixed_block(shaping[0].shape)] * 4, section_block(section, (wide, units)), fixed_block(bias.shape),
            section_block(section, (units, wide)),
        ],
        out_specs=[back] * 4 + [pixel_block(8), pixel_block(wide), pixel_block(units), pixel_block(units)],
        out_shape=[struct((channels + 16, pixels), bf16)] * 4 + [
            struct((8, pixels), f32), struct((wide, pixels), bf16), struct((units, pixels), bf16), struct((units, pixels), bf16),
        ],
        scratch_shapes=[
            pltpu.VMEM((4, channels, tile), bf16), pltpu.VMEM((4, channels + 16, tile), bf16),
            pltpu.VMEM((units, tile), f32), pltpu.VMEM((4,) + shaping[0].shape, f32),
        ],
        name="mlp_top",
        **params(),
    )(me, *parts, *grads, *shaping, weight_in, bias, weight_out)


def mlp_back(section, me, parts, grads, shaping, weight_in, weight_out, slope, stats, after):
    own = parts[0]
    channels, pixels = own.shape
    wide, units = weight_in.shape[1], weight_in.shape[2]
    piece, back = pixel_block(channels), pixel_block(channels + 16)
    given = 1 + 8 + 4 + 4

    def body(*refs):
        mlp_back_body(section, *refs[:given], *refs[given + len(after):])

    return pl.pallas_call(
        body,
        grid=(pixels // tile,),
        in_specs=[smem_spec()] + [piece] * 8 + [
            *[fixed_block(shaping[0].shape)] * 4, section_block(section, (wide, units)), section_block(section, (units, wide)),
            pixel_block(units), pixel_block(8), *[any_spec()] * len(after),
        ],
        out_specs=[back] * 4 + [pixel_block(units)],
        out_shape=[struct((channels + 16, pixels), bf16)] * 4 + [struct((units, pixels), bf16)],
        scratch_shapes=[
            pltpu.VMEM((4, channels, tile), bf16), pltpu.VMEM((4, channels + 16, tile), bf16),
            pltpu.VMEM((4,) + shaping[0].shape, f32),
        ],
        name="mlp_back",
        **params(),
    )(me, *parts, *grads, *shaping, weight_in, weight_out, slope, stats, *after)


def mlp_out_body(section, me_ref, hidden_ref, weight_out_ref, send_far, send_own, keep_far, keep_own, sum_ref):
    for at in range(0, hidden_ref.shape[1], tile):
        cut = slice(at, at + tile)
        value = dot(weight_out_ref[section], hidden_ref[:, cut], 0, 0).astype(bf16)
        sum_ref[:, :, cut] = value.reshape(sum_ref.shape[0], sum_ref.shape[1], tile)
    scatter_out(me_ref, sum_ref, (send_far, send_own, keep_far, keep_own))


def mlp_out(section, me, hidden, weight_out, after):
    wide, pixels = weight_out.shape[2], hidden.shape[1]
    piece = struct((wide // 4, pixels), bf16)
    return launch(
        partial(mlp_out_body, section), "mlp_out", [hidden, weight_out], [piece] * 4,
        [pltpu.VMEM((4, wide // 4, pixels), bf16)], scalars=[me], after=after,
    )


def put_halves(ref, at, outs):
    size = outs[0].shape[0]
    for side, out in zip((at, 1 - at), outs, strict=True):
        out[...] = ref[pl.ds(pl.multiple_of(side * size, size), size), :].astype(bf16)


def weights_body(me_ref, hidden_ref, grad_own, grad_near, grad_far, grad_cross, normed_ref, before_grad_ref,
                 keep, send, units_ref, full_ref, total_ref):
    units = hidden_ref.shape[0]
    gather_into(me_ref, (grad_own, grad_near, grad_far, grad_cross), full_ref)
    total_ref[0:units] = dot(hidden_ref[...], full_ref[...].reshape(-1, full_ref.shape[2]), 1, 1)
    before_grad = before_grad_ref[...]
    total_ref[units:] = dot(normed_ref[...], before_grad, 1, 1)
    units_ref[...] = jnp.broadcast_to(jnp.sum(before_grad.astype(f32), axis=1, keepdims=True), units_ref.shape)
    put_halves(total_ref, me_ref[2], (keep, send))


def weight_grads(me, hidden, grads, normed, before_grad, after=()):
    units, wide = hidden.shape[0], normed.shape[0]
    return launch(
        weights_body, "weight_grads", [hidden, *grads, normed, before_grad],
        [struct((units, wide), bf16)] * 2 + [struct((units, lane), f32)],
        [pltpu.VMEM((4,) + grads[0].shape, bf16), pltpu.VMEM((units + wide, wide), f32)], scalars=[me], after=after,
    )


def out_grad_body(me_ref, hidden_ref, grad_own, grad_near, grad_far, grad_cross, keep, send, full_ref, total_ref):
    gather_into(me_ref, (grad_own, grad_near, grad_far, grad_cross), full_ref)
    total_ref[...] = dot(hidden_ref[...], full_ref[...].reshape(-1, full_ref.shape[2]), 1, 1)
    put_halves(total_ref, me_ref[2], (keep, send))


def out_grad(me, hidden, grads, after=()):
    units, wide = hidden.shape[0], 4 * grads[0].shape[0]
    return launch(
        out_grad_body, "out_grad", [hidden, *grads], [struct((units // 2, wide), bf16)] * 2,
        [pltpu.VMEM((4,) + grads[0].shape, bf16), pltpu.VMEM((units, wide), f32)], scalars=[me], after=after,
    )


def in_grad_body(me_ref, normed_ref, before_grad_ref, keep, send, units_ref, total_ref):
    before_grad = before_grad_ref[...]
    total_ref[...] = dot(normed_ref[...], before_grad, 1, 1)
    put_halves(total_ref, me_ref[2], (keep, send))
    units_ref[...] = jnp.broadcast_to(jnp.sum(before_grad.astype(f32), axis=1, keepdims=True), units_ref.shape)


def in_grad(me, normed, before_grad, after=()):
    wide, units = normed.shape[0], before_grad.shape[0]
    return launch(
        in_grad_body, "in_grad", [normed, before_grad],
        [struct((wide // 2, units), bf16)] * 2 + [struct((units, lane), f32)],
        [pltpu.VMEM((wide, units), f32)], scalars=[me], after=after,
    )


def top_output_body(keep_ref, near_ref, far_ref, stream_ref, cotangent_ref, pack_ref, out_ref, sums_ref):
    bias, scale = pack_ref[:, 3:4], pack_ref[:, 4:5]
    total = jnp.zeros(scale.shape, f32)
    rows = stream_ref.shape[1]
    for canvas in range(stream_ref.shape[0]):
        for row in range(rows):
            at = (canvas * rows + row) * lane
            cut = slice(at, at + lane)
            branch = keep_ref[:, cut].astype(f32) + near_ref[:, cut].astype(f32) + far_ref[:, cut].astype(f32) + bias
            out_ref[canvas, row] = (stream_ref[canvas, row].astype(f32) + scale * branch).astype(bf16)
            total += jnp.sum(cotangent_ref[canvas, row].astype(f32) * branch, axis=1, keepdims=True)
    put_columns(sums_ref, [total])


def top_output(branches, stream, cotangent, pack, after):
    return launch(
        top_output_body, "top_output", [*branches, stream, cotangent, pack],
        [struct(stream.shape, bf16), struct((stream.shape[2], lane), f32)], after=after,
    )


core_pairs = [(i, i ^ 1) for i in range(4)]
chip_pairs = [(i, i ^ 2) for i in range(4)]


def gather_channels(own):
    far = lax.ppermute(own, "ch", chip_pairs)
    near = lax.ppermute(own, "ch", core_pairs)
    cross = lax.ppermute(far, "ch", core_pairs)
    return (own, near, far, cross)


def scatter_channels(send_far, send_own, keep_far, keep_own):
    near_far = lax.ppermute(send_far, "ch", core_pairs)
    near_own = lax.ppermute(send_own, "ch", core_pairs)
    onward = (keep_far.astype(f32) + near_far.astype(f32)).astype(bf16)
    far = lax.ppermute(onward, "ch", chip_pairs)
    return (keep_own, near_own, far), onward


def across_rows(value, flip):
    return lax.ppermute(value, "rows", [(i, i ^ flip) for i in range(8)])


def rows_sum(value):
    for flip in (1, 2, 4):
        value = (value.astype(f32) + across_rows(value, flip).astype(f32)).astype(bf16)
    return value


def total_of(refs):
    return sum(ref[...].astype(f32) for ref in refs)


def halve_body(bit, me_ref, keep_ref, near_ref, keep_out, send_out, total_ref):
    total_ref[...] = total_of((keep_ref, near_ref))
    put_halves(total_ref, me_ref[bit], (keep_out, send_out))


def halve(bit, me, keep, near, after, through=()):
    rows, columns = keep.shape
    return launch(
        partial(halve_body, bit), "halve", [keep, near], [struct((rows // 2, columns), bf16)] * 2,
        [pltpu.VMEM(keep.shape, f32)], scalars=[me], after=after, through=through,
    )


def pair_add_body(keep_ref, near_ref, out_ref):
    out_ref[...] = total_of((keep_ref, near_ref)).astype(bf16)


def pair_add(keep, near, after=(), through=()):
    got = launch(pair_add_body, "pair_add", [keep, near], [struct(keep.shape, bf16)], after=after, through=through)
    return got if through else got[0]


back_flips = ((4, 2, 1), (1, 4, 2))


def spread_back(total, flips):
    parts = [total]
    for flip in flips:
        parts += [across_rows(part, flip) for part in parts]
    return parts


def top_store(me, parts, after):
    size, columns = parts[0].shape

    def body(me_ref, *refs):
        outs = refs[-2:]

        def put(kept):
            for f, part in enumerate(refs[:8]):
                at = (me_ref[3] ^ (f >> 1 & 1)) * 2 + (me_ref[4] ^ (f & 1))
                outs[kept ^ (f >> 2)][0, pl.ds(pl.multiple_of(at * size, size), size), :] = part[...].astype(f32)

        @pl.when(me_ref[2] == 0)
        def _():
            put(0)

        @pl.when(me_ref[2] == 1)
        def _():
            put(1)

    return pl.pallas_call(
        body,
        grid=(1,),
        in_specs=[smem_spec()] + [pl.BlockSpec(part.shape, lambda i: (0, 0)) for part in parts] + [any_spec()] * len(after),
        out_specs=[pl.BlockSpec((1, 4 * size, columns), lambda i: (1, 0, 0))] * 2,
        out_shape=[struct((2, 4 * size, columns), f32)] * 2,
        name="top_store",
        **params(),
    )(me, *parts, *after)


def finish(flips, me, held, parts, after=()):
    size, columns = parts[0].shape
    block = pl.BlockSpec((1,) + held.shape[1:], lambda i: (0, 0, 0))

    def body(me_ref, *refs):
        out = refs[-1]
        for f, part in enumerate(refs[:8]):
            flipped = sum(flip for bit, flip in enumerate(flips) if f >> bit & 1)
            at = (me_ref[2] ^ (flipped & 1)) * 4 + (me_ref[3] ^ (flipped >> 1 & 1)) * 2 + (me_ref[4] ^ (flipped >> 2))
            out[0, pl.ds(pl.multiple_of(at * size, size), size), :] = part[...].astype(f32)

    return pl.pallas_call(
        body,
        grid=(1,),
        in_specs=[smem_spec()] + [pl.BlockSpec(part.shape, lambda i: (0, 0)) for part in parts]
        + [any_spec()] * (1 + len(after)),
        out_specs=block,
        out_shape=struct(held.shape, f32),
        input_output_aliases={1 + len(parts): 0},
        name="finish",
        **params(),
    )(me, *parts, held, *after)


def exchange(pieces):
    return lax.all_to_all(pieces, "rows", split_axis=0, concat_axis=0, tiled=True)


def rows_to_cols(packed, moving, count, picture):
    if packed:
        return [exchange(moving[0])]
    canvases, rows, channels, width = picture
    pieces = []
    for part in moving:
        cut = part.reshape(canvases, rows, channels, count, width // count)
        pieces.append(cut.transpose(3, 2, 0, 1, 4).reshape(count, channels, -1))
    moved = exchange(jnp.stack(pieces, axis=1))
    moved = moved.reshape(count, len(moving), channels, canvases, rows, width // count)
    return [moved[:, k].transpose(1, 2, 0, 3, 4).reshape(channels, -1) for k in range(len(moving))]


def cols_to_rows(packed, moving, count, picture):
    if packed:
        return [exchange(moving[0])]
    canvases, rows, channels, width = picture
    pieces = []
    for part in moving:
        cut = part.reshape(channels, canvases, count, rows, width // count)
        pieces.append(cut.transpose(2, 0, 1, 3, 4).reshape(count, channels, -1))
    moved = exchange(jnp.stack(pieces, axis=1))
    moved = moved.reshape(count, len(moving), channels, canvases, rows, width // count)
    return [moved[:, k].transpose(2, 3, 1, 0, 4).reshape(picture) for k in range(len(moving))]


def crop_reach(starts):
    count = starts.shape[1]
    places = jnp.arange(count, dtype=jnp.int32)
    here, there = places[None, :, None], places[None, None, :]
    begins = starts[:, None, :] > 0
    first = jnp.max(jnp.where(begins & (there <= here), there, 0), axis=2)
    following = jnp.min(jnp.where(begins & (there > here), there, count), axis=2)
    return places[None, :] - first, following - 1 - places[None, :]


def band_turns(age):
    return jnp.max(age.reshape(age.shape[0], -1, band), axis=2) // ahead + 1


def on_device(
    count,
    pixels,
    row_starts,
    col_starts,
    log_step,
    log_decay,
    frequency,
    coef_real,
    coef_imag,
    skip_gain,
    norm_gain,
    norm_shift,
    weight_in,
    bias_in,
    weight_out,
    bias_out,
    layer_scale,
    cotangent,
):
    canvases, rows, width, channels = pixels.shape
    height = row_starts.shape[1]
    channels_all = weight_in.shape[1]
    lengths = (height, width)
    picture = (canvases, rows, channels, width)
    cols = (channels, canvases * height * (width // count))
    eight = count == 8
    packed = eight and picture == (2, 2, 2 * half_rows, lane)
    place = lax.axis_index("rows")
    bits = [place % 2, place // 2 % 2, place // 4] if eight else [0 * place] * 3
    me = jnp.stack([lax.axis_index("ch"), place, *bits]).astype(jnp.int32)

    stream = jnp.swapaxes(pixels, 2, 3)
    upstream = jnp.swapaxes(cotangent, 2, 3)
    states = [jnp.swapaxes(value, 2, 3) for value in (log_decay, frequency, coef_real, coef_imag)]

    age, fore = crop_reach(col_starts)
    age_reach, fore_reach = band_turns(age), band_turns(fore)
    age = jnp.broadcast_to(age[:, :, None], (canvases, width, lane))
    fore = jnp.broadcast_to(fore[:, :, None], (canvases, width, lane))
    row_age, row_fore = crop_reach(row_starts)
    row_age = jnp.repeat(row_age, width // count, axis=1)[:, None, :]
    row_fore = jnp.repeat(row_fore, width // count, axis=1)[:, None, :]

    packs = [
        jnp.stack([skip_gain[k], norm_gain[k], norm_shift[k], bias_out[k], layer_scale[k]], axis=1) for k in range(2)
    ]
    shaping = gather_channels(jnp.stack([norm_gain[0], norm_shift[0], norm_gain[1], norm_shift[1]], axis=1))
    bias_columns = [bias_in[k][:, None] for k in range(2)]

    wide_low = s4_wide(0, width, rows, log_step, *states)
    across = wide_forward(packed, stream, wide_low, age, age_reach)
    tall_low, tall_top, wide_top, top_scaled, top_bias_sums = s4_rest(
        lengths, rows, log_step, states, upstream, packs[1], [across]
    )
    moved = rows_to_cols(packed, [across] if packed else [across, stream], count, picture)
    mixed_low, across_cols, stream_cols = tall_mixed(
        packed, height, moved, cols, tall_low, row_age, packs[0], [*shaping[1:], *bias_columns, me]
    )
    low_parts = gather_channels(mixed_low)
    first = mlp_first(0, me, low_parts, shaping, weight_in, bias_columns[0], weight_out)
    normed_low, hidden_low, slope_low, stats_low = first[4:]
    branches, _ = scatter_channels(*first[:4])
    top_parts = gather_channels(top_scaled)

    next_cols, branch_cols, moving = tall_next(packed, height, branches, stream_cols, packs[0], tall_top, row_age)
    moved = cols_to_rows(packed, moving, count, picture)
    mixed_top, tall_rows, next_rows = wide_mixed(packed, moved, picture, wide_top, age, age_reach, packs[1])
    top_mixed_parts = gather_channels(mixed_top)
    top = mlp_top(1, me, top_mixed_parts, top_parts, shaping, weight_in, bias_columns[1], weight_out)
    stats_top, normed_top, hidden_top, before_grad_top = top[4:]
    top_grads, onward = scatter_channels(*top[:4])
    top_keep, top_send, top_units = weight_grads(me, hidden_top, top_parts, normed_top, before_grad_top, [onward])
    top_weights = [top_keep, top_send]

    moving, grad_rows, top_sums = wide_norm_back(
        packed, channels_all, top_grads, mixed_top, stats_top, packs[1], next_rows, upstream, wide_top, fore, fore_reach,
        [top_send],
    )
    top_partials = mlp_out(1, me, hidden_top, weight_out, moving[:1])
    top_wide = wide_top_grad(grad_rows, tall_rows, age, age_reach, top_partials[:1])
    moved = rows_to_cols(packed, moving, count, picture)
    grad_cols, grad_low, conv_cols, top_send = tall_back(
        packed, height, moved, cols, tall_top, row_fore, packs[0], branch_cols, [top_wide], [top_send]
    )

    grad_parts = gather_channels(grad_low)
    *back, before_grad_low = mlp_back(
        0, me, low_parts, grad_parts, shaping, weight_in, weight_out, slope_low, stats_low, []
    )
    low_grads, onward = scatter_channels(*back)
    out_keep, out_send = out_grad(me, hidden_low, grad_parts, [onward])
    if eight:
        top_keep, top_send = halve(3, me, top_keep, across_rows(top_send, 1), [out_send])
        top_near = across_rows(top_send, 2)
    in_keep, in_send, low_units = in_grad(me, normed_low, before_grad_low, [top_send])
    if eight:
        out_near, in_near = across_rows(out_send, 1), across_rows(in_send, 1)
    moving, low_grad_cols, low_sums = tall_norm_back(
        packed, height, channels_all, low_grads, mixed_low, stats_low, packs[0], stream_cols, grad_cols, tall_low, row_fore,
        [in_send],
    )
    if eight:
        out_keep, out_send = halve(3, me, out_keep, out_near, [moving[0]])
        out_near = across_rows(out_send, 2)
        top_keep, top_send = halve(4, me, top_keep, top_near, [out_send])
        top_near = across_rows(top_send, 4)
    top_branches, _ = scatter_channels(*top_partials)
    activations, top_scale_sums = top_output(top_branches, next_rows, upstream, packs[1], [top_send])
    held = tall_low_grad(
        height, low_grad_cols, across_cols, row_age, low_sums, grad_cols, branch_cols, packs[0], top_scale_sums, low_units,
        [out_keep],
    )
    if eight:
        out_keep, out_send = halve(4, me, out_keep, out_near, [held])
        out_near = across_rows(out_send, 4)
        in_keep, in_send = halve(3, me, in_keep, in_near, [out_send])
        in_near = across_rows(in_send, 2)
        top_total = pair_add(top_keep, top_near, [in_send])
        top_weights = spread_back(top_total, back_flips[0])
    top_small = tall_top_grad(
        height, conv_cols, next_cols, row_age, top_wide, top_sums, top_bias_sums, top_units, [top_total] if eight else [held]
    )
    if eight:
        out_total = pair_add(out_keep, out_near, [top_small])
        out_parts = spread_back(out_total, back_flips[0])
    moved = cols_to_rows(packed, moving, count, picture)
    pixels_grad, small = wide_last(
        packed, moved, picture, stream, wide_low, age, fore, held, top_small, age_reach, fore_reach, [out_total] if eight else []
    )
    if eight:
        in_keep, in_send = halve(4, me, in_keep, in_near, [small])
        in_total = pair_add(in_keep, across_rows(in_send, 4), [in_send])
        in_parts = spread_back(in_total, back_flips[1])
        out_grads, in_grads = top_store(me, top_weights, [in_total])
        out_grads = finish(back_flips[0], me, out_grads, out_parts)
        small = rows_sum(small)
    else:
        small = lax.psum(small.astype(f32), "rows").astype(bf16)
    gradients = s4_pullback(lengths, weight_in.shape[2], small, log_step, *states, [out_grads] if eight else [])
    step_grad, decay_grad, freq_grad, real_grad, imag_grad, skip_grad, gain_grad, shift_grad, units_grad, bias_grad, scale_grad = gradients
    if eight:
        in_grads = finish(back_flips[1], me, in_grads, in_parts, [step_grad])
    else:
        low_weights = lax.psum((out_keep, out_send, in_keep, in_send), "rows")
        top_weights = lax.psum(tuple(top_weights), "rows")
        out_grads = jnp.stack([jnp.concatenate(low_weights[:2]), top_weights[0]]).astype(f32)
        in_grads = jnp.stack([jnp.concatenate(low_weights[2:]), top_weights[1]]).astype(f32)
    return (
        jnp.swapaxes(activations, 2, 3),
        jnp.swapaxes(pixels_grad, 2, 3),
        step_grad,
        jnp.swapaxes(decay_grad, 2, 3),
        jnp.swapaxes(freq_grad, 2, 3),
        jnp.swapaxes(real_grad, 2, 3),
        jnp.swapaxes(imag_grad, 2, 3),
        skip_grad,
        gain_grad,
        shift_grad,
        in_grads,
        units_grad,
        out_grads,
        bias_grad,
        scale_grad,
    )


def solution(mesh):
    picture = P(None, "rows", None, "ch")
    state = P(None, None, "ch", None)
    step = P(None, None, "ch")
    vector = P(None, "ch")
    into = P(None, None, "ch")
    out = P(None, "ch", None)
    in_specs = (
        picture, P(), P(), step, state, state, state, state, vector, vector, vector, into, vector, out, vector, vector, picture,
    )
    out_specs = (
        picture, picture, step, state, state, state, state, vector, vector, vector, into, vector, out, vector, vector,
    )
    return jax.shard_map(
        partial(on_device, mesh.shape["rows"]), mesh=mesh, in_specs=in_specs, out_specs=out_specs, check_vma=False
    )
```
